32 devices in a mesh: items: 16 (over z, y, x), mem: 2 (over core).
Axes of the slice: x: 2, y: 2, z: 4, core: 2. Of those that a mesh axis runs over, the one named last changes fastest.
Arguments:
- dec_in: bfloat16 [16, 128, 1024], P('items'), may hold values from -6 to 6
- memory: bfloat16 [16, 1024, 1024], P('items', 'mem'), may hold values from -6 to 6
- cotangent: bfloat16 [16, 128, 1024], P('items'), may hold values from -6 to 6
- mem_lengths: int32 [16], P('items'), may hold values from 52 to 1024, as said below
- dec_lengths: int32 [16], P('items'), may hold values from 17 to 128, as said below
- attn_in: bfloat16 [3072, 1024], P(('items', 'mem')), may hold values from -0.1875 to 0.1875
- cross_in: bfloat16 [3072, 1024], P(('items', 'mem')), may hold values from -0.1875 to 0.1875
- attn_out: bfloat16 [2048, 1024], P(('items', 'mem')), may hold values from -0.75 to 0.75
- fc_in: bfloat16 [4096, 1024], P(('items', 'mem')), may hold values from -0.1875 to 0.1875
- fc_out: bfloat16 [4096, 1024], P(('items', 'mem')), may hold values from -0.09375 to 0.09375
- biases: bfloat16 [7, 1024], P(None, ('items', 'mem')), may hold values from -1 to 1
- fc_bias: bfloat16 [4096], P(('items', 'mem')), may hold values from -1 to 1
- gains: bfloat16 [3, 1024], P(None, ('items', 'mem')), may hold values from 0.5 to 1.5
- shifts: bfloat16 [3, 1024], P(None, ('items', 'mem')), may hold values from -1 to 1
Outputs:
- output: bfloat16 [16, 128, 1024], P('items')
- grad_dec_in: bfloat16 [16, 128, 1024], P('items')
- grad_memory: bfloat16 [16, 1024, 1024], P('items', 'mem')
- grad_attn_in: float32 [3072, 1024], P(('items', 'mem'))
- grad_cross_in: float32 [3072, 1024], P(('items', 'mem'))
- grad_attn_out: float32 [2048, 1024], P(('items', 'mem'))
- grad_fc_in: float32 [4096, 1024], P(('items', 'mem'))
- grad_fc_out: float32 [4096, 1024], P(('items', 'mem'))
- grad_biases: float32 [7, 1024], P(None, ('items', 'mem'))
- grad_fc_bias: float32 [4096], P(('items', 'mem'))
- grad_gains: float32 [3, 1024], P(None, ('items', 'mem'))
- grad_shifts: float32 [3, 1024], P(None, ('items', 'mem'))
The draws below stay inside these ranges and needn't reach their ends.
Inputs may be any that keep to these rules, and one draw needn't show every extreme that they name: Item b's memory holds its first mem_lengths[b] positions; the rest is padding. In each aligned block of 8 items one item has all 1024 positions. Item b's target holds its first dec_lengths[b] positions. In each aligned block of 8 items one item has 128.
All inputs are finite; a program needn't handle non-finite values.
Results may differ from the reference program's by a relative error of at most 0.03.
Values may be sent and summed in bfloat16 or wider, within the bound.
No kernel may reach another device: no remote copies, remote signals or barrier semaphores. Data moves between devices by JAX's collectives and lax.ppermute only.
A program may use at most 256 MiB of HBM per device.

```python
import jax
import jax.numpy as jnp
from jax import lax

D = 1024
HEADS = 16
HEAD_DIM = 64
FF = 4096
DEC_LEN = 128
MEM_LEN = 1024
ITEMS = 16


def draw_lengths(key, longest, shortest):
    key_body, key_slot = jax.random.split(key)
    blocks = ITEMS // 8
    drawn_len = jax.random.randint(key_body, (ITEMS,), shortest, longest + 1)
    full_slot = jax.random.randint(key_slot, (blocks,), 0, 8)
    is_full = jnp.arange(ITEMS) % 8 == jnp.repeat(full_slot, 8)
    return jnp.where(is_full, longest, drawn_len).astype(jnp.int32)


def draw_mem_lengths(key, part):
    key = jax.random.fold_in(key, 11)
    return draw_lengths(key, MEM_LEN, MEM_LEN // 20 + 1)


def draw_dec_lengths(key, part):
    key = jax.random.fold_in(key, 23)
    return draw_lengths(key, DEC_LEN, DEC_LEN // 8 + 1)


def steps_of(key, shape, cuts, low, largest):
    loudness = 1.0
    for axis_at, blocks in cuts:
        steps = jax.random.uniform(jax.random.fold_in(jax.random.fold_in(key, 6), axis_at), (blocks,), jnp.float32, low / len(cuts), largest / len(cuts))
        loudness = loudness * jnp.repeat(jnp.exp(steps), shape[axis_at] // blocks).reshape((-1,) + (1,) * (len(shape) - 1 - axis_at))
    return loudness


def bell_draw(rng, shape, spread, reach, shards=(), held_as=jnp.bfloat16):
    array = spread * jax.random.normal(rng, shape, jnp.float32)
    if shards:
        array = array * steps_of(rng, shape, shards, -0.22, 0.18)
    return jnp.clip(array, -reach, reach).astype(held_as)


def setup_inputs(seed: int = 0) -> dict:
    key_of = jax.random.split(jax.random.key(seed), 15)
    return {
        "dec_in": bell_draw(key_of[0], (ITEMS, DEC_LEN, D), 1.0, 6.0, ((0, 16),)),
        "memory": bell_draw(key_of[1], (ITEMS, MEM_LEN, D), 1.0, 6.0, ((0, 16), (1, 2))),
        "cotangent": bell_draw(key_of[2], (ITEMS, DEC_LEN, D), 1.0, 6.0, ((0, 16),)),
        "mem_lengths": draw_mem_lengths(jax.random.fold_in(key_of[14], 71), 0),
        "dec_lengths": draw_dec_lengths(jax.random.fold_in(key_of[14], 71), 0),
        "attn_in": bell_draw(key_of[5], (3 * D, D), D ** -0.5, 0.1875, ((0, 32),)),
        "cross_in": bell_draw(key_of[6], (3 * D, D), D ** -0.5, 0.1875, ((0, 32),)),
        "attn_out": bell_draw(key_of[7], (2 * D, D), (D // 16) ** -0.5, 0.75, ((0, 32),)),
        "fc_in": bell_draw(key_of[8], (FF, D), D ** -0.5, 0.1875, ((0, 32),)),
        "fc_out": bell_draw(key_of[9], (FF, D), FF ** -0.5, 0.09375, ((0, 32),)),
        "biases": bell_draw(key_of[10], (7, D), 0.2, 1.0, ((1, 32),)),
        "fc_bias": bell_draw(key_of[11], (FF,), 0.2, 1.0, ((0, 32),)),
        "gains": jnp.clip(1.0 + 0.1 * jax.random.normal(key_of[12], (3, D), jnp.float32), 0.5, 1.5).astype(jnp.bfloat16),
        "shifts": bell_draw(key_of[13], (3, D), 0.2, 1.0, ((1, 32),)),
    }


@jax.custom_vjp
def low(v):
    return lax.optimization_barrier(v.astype(jnp.bfloat16)).astype(jnp.float32)

@jax.custom_vjp
def low_back(v):
    return v

def low_keep(v):
    return (low(v), None)

def low_pass(kept, grad):
    return (grad,)

def back_keep(v):
    return (v, None)

def back_low(kept, grad):
    return (low(grad),)
low.defvjp(low_keep, low_pass)
low_back.defvjp(back_keep, back_low)
masked_fill = -1e+30
norm_epsilon = 1e-05
score_scale = 0.125

def matmul(left, right):
    return jnp.dot(left, right, precision=lax.Precision.HIGHEST)

def normalize(hidden, gain_row, shift_row):
    center = hidden - lax.optimization_barrier(jnp.mean(hidden, axis=-1, keepdims=True))
    return center * lax.rsqrt(lax.optimization_barrier(jnp.mean(center * center, axis=-1, keepdims=True)) + norm_epsilon) * gain_row + shift_row

def attend(queries, keys, values, allowed):
    query_heads = queries.reshape(queries.shape[0], HEADS, HEAD_DIM)
    key_heads = keys.reshape(keys.shape[0], HEADS, HEAD_DIM)
    value_heads = values.reshape(values.shape[0], HEADS, HEAD_DIM)
    scores = low_back(jnp.einsum('qhd,khd->hqk', query_heads, key_heads, precision=lax.Precision.HIGHEST)) * score_scale
    scores = jnp.where(allowed[None], scores, masked_fill)
    weights = jnp.exp(scores - lax.optimization_barrier(jnp.max(scores, axis=-1, keepdims=True)))
    totals = lax.optimization_barrier(jnp.sum(weights, axis=-1))
    summed = low_back(jnp.einsum('hqk,khd->qhd', low(weights), value_heads, precision=lax.Precision.HIGHEST))
    output = summed / jnp.transpose(totals)[:, :, None]
    return low(low_back(output.reshape(queries.shape[0], HEADS * HEAD_DIM)))

def forward(dec_row, mem_row, params, mem_len, dec_len):
    attn_in, cross_in, attn_out, fc_in, fc_out, biases, fc_bias, gains, shifts = params
    steps_index = jnp.arange(DEC_LEN)
    causal = (steps_index[:, None] >= steps_index[None, :]) & (steps_index[None, :] < dec_len)
    projected = low_back(matmul(dec_row, attn_in.T))
    self_query = low(projected[:, :D] + biases[0])
    self_key = low(projected[:, D:2 * D])
    self_value = low(projected[:, 2 * D:] + biases[1])
    self_attn = attend(self_query, self_key, self_value, causal)
    normed_one = normalize(dec_row + low_back(matmul(self_attn, attn_out[:D])) + biases[2], gains[0], shifts[0])
    cross_query = low(low_back(matmul(low(normed_one), cross_in[:D].T)) + biases[3])
    mem_proj = low_back(matmul(mem_row, cross_in[D:].T))
    cross_key = low(mem_proj[:, :D])
    cross_value = low(mem_proj[:, D:] + biases[4])
    allowed = jnp.broadcast_to((jnp.arange(MEM_LEN) < mem_len)[None, :], (DEC_LEN, MEM_LEN))
    cross_attn = attend(cross_query, cross_key, cross_value, allowed)
    normed_two = normalize(normed_one + low_back(matmul(cross_attn, attn_out[D:])) + biases[5], gains[1], shifts[1])
    inner_pre = low_back(matmul(low(normed_two), fc_in.T)) + fc_bias
    activation = low(jax.nn.gelu(inner_pre, approximate=False))
    return normalize(normed_two + low_back(matmul(activation, fc_out)) + biases[6], gains[2], shifts[2])

def reference(dec_in, memory, cotangent, mem_lengths, dec_lengths, attn_in, cross_in, attn_out, fc_in, fc_out, biases, fc_bias, gains, shifts):
    params = tuple((tensor.astype(jnp.float32) for tensor in (attn_in, cross_in, attn_out, fc_in, fc_out, biases, fc_bias, gains, shifts)))

    def one_item(totals, item):
        dec_row, mem_row, cot_row, mem_len, dec_len = item

        def layer(dec_value, mem_value, param_value):
            return forward(dec_value, mem_value, param_value, mem_len, dec_len)
        result, pullback = jax.vjp(layer, dec_row.astype(jnp.float32), mem_row.astype(jnp.float32), params)
        grad_dec, grad_mem, grad_params = pullback(cot_row.astype(jnp.float32))
        totals = jax.tree.map(jnp.add, totals, grad_params)
        return (totals, (result.astype(jnp.bfloat16), grad_dec.astype(jnp.bfloat16), grad_mem.astype(jnp.bfloat16)))
    initial = jax.tree.map(jnp.zeros_like, params)
    totals, outputs = lax.scan(one_item, initial, (dec_in, memory, cotangent, mem_lengths, dec_lengths))
    return (outputs[0], outputs[1], outputs[2], totals[0], totals[1], totals[2], totals[3], totals[4], totals[5], totals[6], totals[7], totals[8])
```

```python
import jax
import jax.numpy as jnp
from jax import lax
from jax.experimental import pallas as pl
from jax.experimental.pallas import tpu as pltpu
from jax.sharding import PartitionSpec as P

HEAD_DIM = 64
GROUP = 4
FILL = -1e30
EPSILON = 1e-05
SCALE = 0.125
BF = jnp.bfloat16
F32 = jnp.float32


def contract(a, b, dim_a, dim_b):
    return lax.dot_general(a, b, (((dim_a,), (dim_b,)), ((), ())), preferred_element_type=F32)


def norm_parts(hidden):
    center = hidden - jnp.mean(hidden, axis=-1, keepdims=True)
    spread = lax.rsqrt(jnp.mean(center * center, axis=-1, keepdims=True) + EPSILON)
    return center * spread, spread


def norm_back(grad_out, normal, spread, gain_row):
    grad_normal = grad_out * gain_row
    grad_hidden = spread * (
        grad_normal
        - jnp.mean(grad_normal, axis=-1, keepdims=True)
        - normal * jnp.mean(grad_normal * normal, axis=-1, keepdims=True)
    )
    return grad_hidden, jnp.sum(grad_out * normal, axis=0), jnp.sum(grad_out, axis=0)


def self_fwd_kernel(len_ref, qkv_ref, out_ref, peak_ref, total_ref):
    width, steps = out_ref.shape
    key_at = lax.broadcasted_iota(jnp.int32, (steps, steps), 0)
    query_at = lax.broadcasted_iota(jnp.int32, (steps, steps), 1)
    allowed = (key_at <= query_at) & (key_at < len_ref[0])
    for head in range(width // HEAD_DIM):
        rows = slice(head * HEAD_DIM, (head + 1) * HEAD_DIM)
        query = qkv_ref[rows, :] * SCALE
        key = qkv_ref[width + head * HEAD_DIM : width + (head + 1) * HEAD_DIM, :]
        value = qkv_ref[2 * width + head * HEAD_DIM : 2 * width + (head + 1) * HEAD_DIM, :]
        scores = jnp.where(allowed, contract(key, query, 0, 0), FILL)
        peak = jnp.max(scores, axis=0, keepdims=True)
        weights = jnp.exp(scores - peak)
        total = jnp.sum(weights, axis=0, keepdims=True)
        out_ref[rows, :] = (contract(value, weights.astype(BF), 1, 0) / total).astype(BF)
        peak_ref[head : head + 1, :] = peak
        total_ref[head : head + 1, :] = total


def self_bwd_kernel(len_ref, qkv_ref, out_ref, grad_ref, peak_ref, total_ref, res_ref, sum_ref):
    width, steps = out_ref.shape
    key_at = lax.broadcasted_iota(jnp.int32, (steps, steps), 0)
    query_at = lax.broadcasted_iota(jnp.int32, (steps, steps), 1)
    allowed = (key_at <= query_at) & (key_at < len_ref[0])
    for head in range(width // HEAD_DIM):
        rows = slice(head * HEAD_DIM, (head + 1) * HEAD_DIM)
        key_rows = slice(width + head * HEAD_DIM, width + (head + 1) * HEAD_DIM)
        value_rows = slice(2 * width + head * HEAD_DIM, 2 * width + (head + 1) * HEAD_DIM)
        query, key, value = qkv_ref[rows, :], qkv_ref[key_rows, :], qkv_ref[value_rows, :]
        scores = jnp.where(allowed, contract(key, query * SCALE, 0, 0), FILL)
        weights = jnp.exp(scores - peak_ref[head : head + 1, :])
        inverse = 1.0 / total_ref[head : head + 1, :]
        grad = grad_ref[rows, :].astype(F32)
        scaled = (grad * inverse).astype(BF)
        delta = jnp.sum(grad * out_ref[rows, :].astype(F32), axis=0, keepdims=True) * inverse
        grad_weights = contract(value, scaled, 0, 0)
        grad_scores = (SCALE * (weights * (grad_weights - delta))).astype(BF)
        grad_query = contract(key, grad_scores, 1, 0)
        grad_value = contract(scaled, weights.astype(BF), 1, 1)
        res_ref[rows, :] = grad_query.astype(BF)
        res_ref[key_rows, :] = contract(query, grad_scores, 1, 1).astype(BF)
        res_ref[value_rows, :] = grad_value.astype(BF)
        sum_ref[rows, 0:1] = jnp.sum(grad_query, axis=1, keepdims=True)
        sum_ref[rows, 1:2] = jnp.sum(grad_value, axis=1, keepdims=True)


def cross_fwd_kernel(len_ref, query_ref, key_ref, value_ref, out_ref, peak_ref, total_ref):
    height, steps = query_ref.shape
    span = key_ref.shape[1]
    valid = lax.broadcasted_iota(jnp.int32, (span, steps), 0) < len_ref[0]
    for head in range(height // HEAD_DIM):
        rows = slice(head * HEAD_DIM, (head + 1) * HEAD_DIM)
        scores = contract(key_ref[rows, :], query_ref[rows, :] * SCALE, 0, 0)
        scores = jnp.where(valid, scores, FILL)
        peak = jnp.max(scores, axis=0, keepdims=True)
        weights = jnp.exp(scores - peak)
        out_ref[rows, :] = contract(value_ref[rows, :], weights.astype(BF), 1, 0).astype(BF)
        peak_ref[0, head : head + 1, :] = peak
        total_ref[0, head : head + 1, :] = jnp.sum(weights, axis=0, keepdims=True)


def cross_bwd_kernel(
    len_ref,
    query_ref,
    key_ref,
    value_ref,
    out_ref,
    grad_ref,
    peak_ref,
    total_ref,
    grad_query_ref,
    grad_key_ref,
    grad_value_ref,
    sum_ref,
):
    height, steps = query_ref.shape
    span = key_ref.shape[1]
    valid = lax.broadcasted_iota(jnp.int32, (span, steps), 0) < len_ref[0]
    for head in range(height // HEAD_DIM):
        rows = slice(head * HEAD_DIM, (head + 1) * HEAD_DIM)
        query, key, value = query_ref[rows, :], key_ref[rows, :], value_ref[rows, :]
        scores = jnp.where(valid, contract(key, query * SCALE, 0, 0), FILL)
        weights = jnp.exp(scores - peak_ref[0, head : head + 1, :])
        inverse = 1.0 / total_ref[0, head : head + 1, :]
        grad = grad_ref[rows, :].astype(F32)
        scaled = (grad * inverse).astype(BF)
        delta = jnp.sum(grad * out_ref[rows, :].astype(F32), axis=0, keepdims=True) * inverse
        grad_weights = contract(value, scaled, 0, 0)
        grad_scores = (SCALE * (weights * (grad_weights - delta))).astype(BF)
        grad_query_ref[rows, :] = contract(key, grad_scores, 1, 0).astype(BF)
        grad_key_ref[rows, :] = contract(query, grad_scores, 1, 1).astype(BF)
        grad_value = contract(scaled, weights.astype(BF), 1, 1)
        grad_value_ref[rows, :] = grad_value.astype(BF)
        sum_ref[rows, :] = jnp.sum(grad_value, axis=1, keepdims=True)


SCALARS = pl.BlockSpec(memory_space=pltpu.SMEM)
WHOLE = pl.BlockSpec(memory_space=pltpu.VMEM)
PARAMS = pltpu.CompilerParams(vmem_limit_bytes=48 * 1024 * 1024)
HEADS_A_STEP = 8


def shape(dims, dtype):
    return jax.ShapeDtypeStruct(dims, dtype)


def self_fwd(length, qkv):
    width, steps = qkv.shape[0] // 3, qkv.shape[1]
    heads = width // HEAD_DIM
    return pl.pallas_call(
        self_fwd_kernel,
        in_specs=[SCALARS, WHOLE],
        out_specs=[WHOLE] * 3,
        out_shape=[
            shape((width, steps), BF),
            shape((heads, steps), F32),
            shape((heads, steps), F32),
        ],
        compiler_params=PARAMS,
        name="self_fwd",
    )(length, qkv)


def self_bwd(length, qkv, out, grad, peak, total):
    return pl.pallas_call(
        self_bwd_kernel,
        in_specs=[SCALARS] + [WHOLE] * 5,
        out_specs=[WHOLE] * 2,
        out_shape=[shape(qkv.shape, BF), shape((out.shape[0], 2), F32)],
        compiler_params=PARAMS,
        name="self_bwd",
    )(length, qkv, out, grad, peak, total)


def cross_specs(width, steps, span):
    count = width // HEAD_DIM // HEADS_A_STEP
    height = HEADS_A_STEP * HEAD_DIM
    by_step = pl.BlockSpec((height, steps), lambda i: (i, 0))
    keys = pl.BlockSpec((height, span), lambda i: (i, 0))
    values = pl.BlockSpec((height, span), lambda i: (i + count, 0))
    stats = pl.BlockSpec((1, HEADS_A_STEP, steps), lambda i: (i, 0, 0))
    column = pl.BlockSpec((height, 1), lambda i: (i, 0))
    return count, by_step, keys, values, stats, column


def cross_fwd(length, query, key_value):
    width, steps = query.shape
    count, by_step, keys, values, stats, _ = cross_specs(width, steps, key_value.shape[1])
    stat_shape = shape((count, HEADS_A_STEP, steps), F32)
    return pl.pallas_call(
        cross_fwd_kernel,
        grid=(count,),
        in_specs=[SCALARS, by_step, keys, values],
        out_specs=[by_step, stats, stats],
        out_shape=[shape((width, steps), BF), stat_shape, stat_shape],
        compiler_params=PARAMS,
        name="cross_fwd",
    )(length, query, key_value, key_value)


def cross_bwd(length, query, key_value, out, grad, peak, total):
    width, steps = query.shape
    span = key_value.shape[1]
    count, by_step, keys, values, stats, column = cross_specs(width, steps, span)
    return pl.pallas_call(
        cross_bwd_kernel,
        grid=(count,),
        in_specs=[SCALARS, by_step, keys, values, by_step, by_step, stats, stats],
        out_specs=[by_step, keys, keys, column],
        out_shape=[
            shape((width, steps), BF),
            shape((width, span), BF),
            shape((width, span), BF),
            shape((width, 1), F32),
        ],
        compiler_params=PARAMS,
        name="cross_bwd",
    )(length, query, key_value, key_value, out, grad, peak, total)


def place_blocks(places, blocks, heights):
    count = len(blocks)
    width = blocks[0].shape[1]
    starts = [sum(heights[:n]) for n in range(len(heights))]

    def kernel(place_ref, *refs):
        ins, outs, sems = refs[:count], refs[count:-1], refs[-1]
        copies = []
        for block in range(count):
            place = place_ref[block]
            for n, (start, height) in enumerate(zip(starts, heights)):
                copies.append(
                    pltpu.make_async_copy(
                        ins[block].at[pl.ds(start, height)],
                        outs[n].at[place],
                        sems.at[block, n],
                    )
                )
        for copy in copies:
            copy.start()
        for copy in copies:
            copy.wait()

    anywhere = pl.BlockSpec(memory_space=pl.ANY)
    return pl.pallas_call(
        kernel,
        in_specs=[SCALARS] + [WHOLE] * count,
        out_specs=[anywhere] * len(heights),
        out_shape=[shape((count, height, width), blocks[0].dtype) for height in heights],
        scratch_shapes=[pltpu.SemaphoreType.DMA((count, len(heights)))],
        compiler_params=PARAMS,
        name="place_blocks",
    )(places, *blocks)


def local(mesh, dec_in, memory, cotangent, mem_lengths, dec_lengths, *weights):
    attn_in, cross_in, attn_out, fc_in, fc_out, biases, fc_bias, gains, shifts = weights
    chips, cores = mesh.shape["items"], mesh.shape["mem"]
    planes = chips // GROUP
    chip, core = lax.axis_index("items"), lax.axis_index("mem")
    plane, member = chip // GROUP, chip % GROUP

    def ring(a, step):
        pairs = [
            (i, (i // GROUP + step) % planes * GROUP + i % GROUP) for i in range(chips)
        ]
        return lax.ppermute(a, "items", pairs)

    def across(a, mask):
        return lax.ppermute(a, "items", [(i, i ^ mask) for i in range(chips)])

    def swap(a):
        return lax.ppermute(a, "mem", [(0, 1), (1, 0)])

    def by_core(mine, other):
        return jnp.where(core == 0, jnp.concatenate([mine, other]), jnp.concatenate([other, mine]))

    def ring_gather(a):
        held = [a]
        for _ in range(planes - 1):
            held.append(ring(held[-1], 1))
        return held

    def ring_sum(parts):
        if planes == 1:
            return parts(0)
        total = parts(1)
        for r in range(2, planes):
            total = ring(total.astype(BF), 1).astype(F32) + parts(r)
        return ring(total.astype(BF), 1).astype(F32) + parts(0)

    def gather_rows(pack, heights):
        if planes != 4:
            whole = lax.all_gather(pack, ("items", "mem"), axis=0)
            starts = [sum(heights[:n]) for n in range(len(heights))]
            return [whole[:, s : s + h] for s, h in zip(starts, heights)]
        held = ring_gather(pack)
        blocks, places = [], []
        for r, block in enumerate(held):
            first, second = (1, 2) if r < 2 else (2, 1)
            one = across(block, first)
            two = across(block, second)
            three = across(one, second)
            source = (plane - r) % planes
            for mask, piece in ((0, block), (first, one), (second, two), (3, three)):
                place = source * GROUP + (member ^ mask)
                blocks += [piece, swap(piece)]
                places += [place * cores + core, place * cores + 1 - core]
        return place_blocks(jnp.stack(places).astype(jnp.int32), blocks, heights)

    def scatter_rows(arrays):
        if planes != 4:
            return [
                lax.psum_scatter(a.astype(F32), "items", scatter_dimension=0, tiled=False)
                for a in arrays
            ]
        arrays = [a.reshape(planes, GROUP, *a.shape[1:]) for a in arrays]

        def term(r, mask):
            at = ((plane - r) % planes, member ^ mask)
            return jnp.concatenate(
                [
                    lax.dynamic_slice(a, (*at, 0, 0), (1, 1, *a.shape[2:]))[0, 0]
                    for a in arrays
                ]
            )

        def plane_sum(r):
            first, second = (1, 2) if r in (1, 2) else (2, 1)
            came = across(jnp.stack([term(r, first), term(r, 3)]).astype(BF), first)
            far = term(r, second).astype(F32) + came[1].astype(F32)
            near = term(r, 0).astype(F32) + came[0].astype(F32)
            return near + across(far.astype(BF), second).astype(F32)

        total = ring_sum(plane_sum)
        heights = [a.shape[2] for a in arrays]
        starts = [sum(heights[:n]) for n in range(len(heights))]
        return [total[s : s + h] for s, h in zip(starts, heights)]

    def group_gather(mine):
        near = jnp.stack([mine] + [across(mine, mask) for mask in range(1, GROUP)])
        both = jnp.stack([near, swap(near)])
        return both.reshape(cores * GROUP * mine.shape[0], mine.shape[1])

    def group_sum(part):
        part = part.reshape(cores, GROUP, -1, part.shape[1])
        near = part[0] + swap(part[1].astype(BF)).astype(F32)
        total = near[0]
        for mask in range(1, GROUP):
            total = total + across(near[mask].astype(BF), mask).astype(F32)
        return total

    width = dec_in.shape[2]
    steps = dec_in.shape[1]
    half = steps // cores
    span = memory.shape[1]
    row_attn, row_out, row_fc = attn_in.shape[0], attn_out.shape[0], fc_in.shape[0]
    small = jnp.concatenate([biases, gains, shifts])
    vectors, slice_width = small.shape

    def padded_row(flat):
        return jnp.zeros((16, width), flat.dtype).at[0, : flat.shape[0]].set(flat)

    pack = jnp.concatenate([attn_in, cross_in, attn_out, padded_row(small.reshape(-1))])
    w_attn, w_cross, w_out, w_small = gather_rows(pack, [row_attn, row_attn, row_out, 16])
    w_attn = w_attn.reshape(-1, width)
    w_cross = w_cross.reshape(-1, width)
    w_out = w_out.reshape(-1, width)
    w_small = w_small[:, 0, : small.size].reshape(-1, vectors, slice_width)
    rows_small = jnp.transpose(w_small, (1, 0, 2)).reshape(vectors, width).astype(F32)
    bias, gain, shift = rows_small[:7], rows_small[7:10], rows_small[10:13]
    fc_held = ring_gather(jnp.concatenate([fc_in, fc_out, padded_row(fc_bias)]))
    w_fc_in = jnp.concatenate([a[:row_fc] for a in fc_held])
    w_fc_out = jnp.concatenate([a[row_fc : 2 * row_fc] for a in fc_held])
    fc_bias_held = jnp.concatenate([a[2 * row_fc, :row_fc] for a in fc_held]).astype(F32)

    tokens = dec_in[0]
    mem_rows = memory[0]
    zeros = jnp.zeros((width,), F32)
    qkv_bias = jnp.concatenate([bias[0], zeros, bias[1]])[:, None]
    qkv = (contract(w_attn, tokens, 1, 1) + qkv_bias).astype(BF)
    self_out, self_peak, self_total = self_fwd(dec_lengths, qkv)
    hidden_one = tokens.astype(F32) + contract(self_out, w_out[:width], 0, 0) + bias[2]
    normal_one, spread_one = norm_parts(hidden_one)
    normed_one = normal_one * gain[0] + shift[0]
    normed_one_low = normed_one.astype(BF)
    cross_query = (contract(w_cross[:width], normed_one_low, 1, 1) + bias[3][:, None]).astype(BF)
    kv_bias = jnp.concatenate([zeros, bias[4]])[:, None]
    cross_kv = (contract(w_cross[width:], mem_rows, 1, 1) + kv_bias).astype(BF)
    mem_left = mem_lengths - core * span
    part_out, part_peak, part_total = cross_fwd(mem_left, cross_query, cross_kv)
    other_out = swap(part_out)
    other_stats = swap(jnp.stack([part_peak, part_total]))
    other_peak, other_total = other_stats[0], other_stats[1]
    cross_peak = jnp.maximum(part_peak, other_peak)
    mine_factor = jnp.exp(part_peak - cross_peak)
    other_factor = jnp.exp(other_peak - cross_peak)
    cross_total = mine_factor * part_total + other_factor * other_total
    heads = width // HEAD_DIM

    def per_head(stat):
        return stat.reshape(heads, 1, steps)

    cross_out = (
        per_head(mine_factor / cross_total) * part_out.reshape(heads, HEAD_DIM, steps).astype(F32)
        + per_head(other_factor / cross_total)
        * other_out.reshape(heads, HEAD_DIM, steps).astype(F32)
    )
    cross_out = cross_out.reshape(width, steps).astype(BF)

    def own(rows):
        return lax.dynamic_slice_in_dim(rows, core * half, half)

    hidden_two = own(normed_one + contract(cross_out, w_out[width:], 0, 0)) + bias[5]
    normal_two, spread_two = norm_parts(hidden_two)
    normed_two = normal_two * gain[1] + shift[1]
    group_two = group_gather(normed_two.astype(BF))
    inner = contract(group_two, w_fc_in, 1, 1) + fc_bias_held
    activation = jax.nn.gelu(inner, approximate=False).astype(BF)
    hidden_three = normed_two + group_sum(contract(activation, w_fc_out, 1, 0)) + bias[6]
    normal_three, spread_three = norm_parts(hidden_three)
    out_own = (normal_three * gain[2] + shift[2]).astype(BF)
    output = by_core(out_own, swap(out_own))[None]

    grad_three, grad_gain_three, grad_shift_three = norm_back(
        own(cotangent[0]).astype(F32), normal_three, spread_three, gain[2]
    )
    group_three = group_gather(grad_three.astype(BF))
    grad_activation = contract(group_three, w_fc_out, 1, 1)
    density = jnp.exp(-0.5 * inner * inner) * 0.3989422804014327
    grad_inner = grad_activation * (0.5 * (1.0 + lax.erf(inner * 0.7071067811865476)) + inner * density)
    grad_inner_low = grad_inner.astype(BF)
    grad_fc_out = contract(activation, group_three, 0, 0)
    grad_fc_in = contract(grad_inner_low, group_two, 0, 0)
    grad_fc_bias = jnp.sum(grad_inner, axis=0)
    grad_two, grad_gain_two, grad_shift_two = norm_back(
        grad_three + group_sum(contract(grad_inner_low, w_fc_in, 1, 0)),
        normal_two,
        spread_two,
        gain[1],
    )

    def fc_part(r):
        rows = slice(r * row_fc, (r + 1) * row_fc)
        return jnp.concatenate([grad_fc_in[rows], grad_fc_out[rows], padded_row(grad_fc_bias[rows])])

    fc_sum = ring_sum(fc_part)
    sum_fc_in, sum_fc_out = fc_sum[:row_fc], fc_sum[row_fc : 2 * row_fc]
    sum_fc_bias = fc_sum[2 * row_fc, :row_fc]

    grad_two_low = grad_two.astype(BF)
    grad_two_all = by_core(grad_two_low, swap(grad_two_low))
    grad_cross = contract(w_out[width:], grad_two_all, 1, 1).astype(BF)
    grad_query, grad_key, grad_value, grad_value_sum = cross_bwd(
        mem_left, cross_query, cross_kv, cross_out, grad_cross, cross_peak, cross_total
    )
    grad_query_all = grad_query.astype(F32) + swap(grad_query).astype(F32)
    grad_query_low = grad_query_all.astype(BF)
    grad_one, grad_gain_one, grad_shift_one = norm_back(
        grad_two + own(contract(grad_query_low, w_cross[:width], 0, 0)),
        own(normal_one),
        own(spread_one),
        gain[0],
    )
    grad_kv = jnp.concatenate([grad_key, grad_value])
    grad_memory = contract(grad_kv, w_cross[width:], 0, 0).astype(BF)[None]
    part_cross = jnp.concatenate(
        [contract(grad_query, normed_one_low, 1, 0), contract(grad_kv, mem_rows, 1, 0)]
    )
    part_cross = part_cross.reshape(chips, cores, row_attn, width)

    def of_core(a, which):
        return lax.dynamic_index_in_dim(a, which, 1, keepdims=False)

    sum_cores = of_core(part_cross, core) + swap(of_core(part_cross, 1 - core).astype(BF)).astype(F32)

    grad_one_low = grad_one.astype(BF)
    grad_one_all = by_core(grad_one_low, swap(grad_one_low))
    grad_self = contract(w_out[:width], grad_one_all, 1, 1).astype(BF)
    grad_qkv, grad_qv_sum = self_bwd(
        dec_lengths, qkv, self_out, grad_self, self_peak, self_total
    )
    grad_tokens = grad_one + own(contract(grad_qkv, w_attn, 0, 0))
    grad_tokens_low = grad_tokens.astype(BF)
    grad_dec_in = by_core(grad_tokens_low, swap(grad_tokens_low))[None]

    def own_rows(by_feature, rows, right):
        mine = of_core(by_feature.reshape(-1, cores, rows, steps), core)
        return contract(mine.reshape(-1, steps), right, 1, 0).reshape(-1, rows, width)

    part_attn = own_rows(grad_qkv, row_attn, tokens)
    part_out = jnp.concatenate(
        [own_rows(self_out, row_out, grad_one_all), own_rows(cross_out, row_out, grad_two_all)]
    )
    part_vectors = jnp.stack(
        [
            grad_qv_sum[:, 0] / cores,
            grad_qv_sum[:, 1] / cores,
            jnp.sum(grad_one, axis=0),
            jnp.sum(grad_query.astype(F32), axis=1),
            grad_value_sum[:, 0],
            jnp.sum(grad_two, axis=0),
            jnp.sum(grad_three, axis=0),
            grad_gain_one,
            grad_gain_two,
            grad_gain_three,
            grad_shift_one,
            grad_shift_two,
            grad_shift_three,
        ]
    )
    part_vectors = jnp.transpose(
        part_vectors.reshape(vectors, chips, cores, slice_width), (1, 2, 0, 3)
    ).reshape(chips, cores, vectors * slice_width)
    vector_sum = of_core(part_vectors, core) + swap(
        of_core(part_vectors, 1 - core).astype(BF)
    ).astype(F32)
    vector_rows = jnp.zeros((chips, 16, width), F32).at[:, 0, : vector_sum.shape[1]].set(vector_sum)
    sum_attn, sum_cross, sum_out, sum_vectors = scatter_rows(
        [part_attn, sum_cores, part_out, vector_rows]
    )
    sum_vectors = sum_vectors[0, : vectors * slice_width].reshape(vectors, slice_width)
    return (
        output,
        grad_dec_in,
        grad_memory,
        sum_attn,
        sum_cross,
        sum_out,
        sum_fc_in,
        sum_fc_out,
        sum_vectors[:7],
        sum_fc_bias,
        sum_vectors[7:10],
        sum_vectors[10:13],
    )


def solution(mesh):
    rows = P(("items", "mem"), None)
    columns = P(None, ("items", "mem"))
    item = P("items", None, None)
    in_specs = (
        item,
        P("items", "mem", None),
        item,
        P("items"),
        P("items"),
        rows,
        rows,
        rows,
        rows,
        rows,
        columns,
        P(("items", "mem")),
        columns,
        columns,
    )
    out_specs = (
        item,
        item,
        P("items", "mem", None),
        rows,
        rows,
        rows,
        rows,
        rows,
        columns,
        P(("items", "mem")),
        columns,
        columns,
    )

    def program(*args):
        return local(mesh, *args)

    return jax.shard_map(
        program, mesh=mesh, in_specs=in_specs, out_specs=out_specs, check_vma=False
    )
```

```python
import functools

import jax
import jax.numpy as jnp
from jax import lax
from jax.experimental import pallas as pl
from jax.experimental.pallas import tpu as pltpu
from jax.sharding import PartitionSpec as P

HEAD_DIM = 64
SMALL = 16
GROUP = 4
FILL = -1e30
EPSILON = 1e-05
SCALE = 0.125
BF = jnp.bfloat16
F32 = jnp.float32


def contract(a, b, dim_a, dim_b):
    return lax.dot_general(a, b, (((dim_a,), (dim_b,)), ((), ())), preferred_element_type=F32)


def norm_parts(hidden):
    center = hidden - jnp.mean(hidden, axis=-1, keepdims=True)
    spread = lax.rsqrt(jnp.mean(center * center, axis=-1, keepdims=True) + EPSILON)
    return center * spread, spread


def norm_back(grad_out, normal, spread, gain_row):
    grad_normal = grad_out * gain_row
    grad_hidden = spread * (
        grad_normal
        - jnp.mean(grad_normal, axis=-1, keepdims=True)
        - normal * jnp.mean(grad_normal * normal, axis=-1, keepdims=True)
    )
    return grad_hidden, jnp.sum(grad_out * normal, axis=0), jnp.sum(grad_out, axis=0)


def self_fwd_heads(length, qkv_ref, out_ref, peak_ref, total_ref):
    width, steps = out_ref.shape
    key_at = lax.broadcasted_iota(jnp.int32, (steps, steps), 0)
    query_at = lax.broadcasted_iota(jnp.int32, (steps, steps), 1)
    allowed = (key_at <= query_at) & (key_at < length)
    for head in range(width // HEAD_DIM):
        rows = slice(head * HEAD_DIM, (head + 1) * HEAD_DIM)
        query = qkv_ref[rows, :] * SCALE
        key = qkv_ref[width + head * HEAD_DIM : width + (head + 1) * HEAD_DIM, :]
        value = qkv_ref[2 * width + head * HEAD_DIM : 2 * width + (head + 1) * HEAD_DIM, :]
        scores = jnp.where(allowed, contract(key, query, 0, 0), FILL)
        peak = jnp.max(scores, axis=0, keepdims=True)
        weights = jnp.exp(scores - peak)
        total = jnp.sum(weights, axis=0, keepdims=True)
        out_ref[rows, :] = (contract(value, weights.astype(BF), 1, 0) / total).astype(BF)
        peak_ref[head : head + 1, :] = peak
        total_ref[head : head + 1, :] = total


def self_fwd_kernel(
    scalar_ref,
    mine_ref,
    other_ref,
    qkv_ref,
    out_ref,
    peak_ref,
    total_ref,
    small_ref,
    column_ref,
    *,
    planes,
):
    width, steps = out_ref.shape
    devices = 2 * GROUP * planes
    height = 3 * width // devices
    lanes = width // devices
    spread = (
        lax.broadcasted_iota(jnp.int32, (steps, width), 1) % lanes
        == lax.broadcasted_iota(jnp.int32, (steps, width), 0)
    ).astype(BF)
    lane_place = lax.broadcasted_iota(jnp.int32, (SMALL, width), 1) // lanes
    small = jnp.zeros((SMALL, width), F32)
    for n, source in enumerate((mine_ref, other_ref)):
        for k in range(GROUP):
            tiled = contract(source[k, planes * height :, :], spread, 1, 0)
            for r in range(planes):
                place = scalar_ref[1 + (n * GROUP + k) * planes + r]
                at = pl.multiple_of(place * height, height)
                qkv_ref[pl.ds(at, height), :] = source[k, r * height : (r + 1) * height, :]
                mine = tiled[r * SMALL : (r + 1) * SMALL]
                small = jnp.where(lane_place == place, mine, small)
    small_ref[...] = small
    small_low = small.astype(BF)

    def column(row):
        pick = (lax.broadcasted_iota(jnp.int32, (SMALL, steps), 0) == row).astype(BF)
        return contract(small_low, pick, 0, 0)

    for at, row in ((0, 0), (2 * width, 1)):
        rows = slice(at, at + width)
        qkv_ref[rows, :] = (qkv_ref[rows, :].astype(F32) + column(row)).astype(BF)
    column_ref[0] = column(3)
    column_ref[1] = column(4)
    self_fwd_heads(scalar_ref[0], qkv_ref, out_ref, peak_ref, total_ref)


def plain_self_fwd_kernel(scalar_ref, qkv_ref, out_ref, peak_ref, total_ref):
    self_fwd_heads(scalar_ref[0], qkv_ref, out_ref, peak_ref, total_ref)


def self_bwd_heads(length, qkv_ref, out_ref, grad_ref, peak_ref, total_ref, res_ref, sum_ref):
    width, steps = out_ref.shape
    key_at = lax.broadcasted_iota(jnp.int32, (steps, steps), 0)
    query_at = lax.broadcasted_iota(jnp.int32, (steps, steps), 1)
    allowed = (key_at <= query_at) & (key_at < length)
    for head in range(width // HEAD_DIM):
        rows = slice(head * HEAD_DIM, (head + 1) * HEAD_DIM)
        key_rows = slice(width + head * HEAD_DIM, width + (head + 1) * HEAD_DIM)
        value_rows = slice(2 * width + head * HEAD_DIM, 2 * width + (head + 1) * HEAD_DIM)
        query, key, value = qkv_ref[rows, :], qkv_ref[key_rows, :], qkv_ref[value_rows, :]
        scores = jnp.where(allowed, contract(key, query * SCALE, 0, 0), FILL)
        weights = jnp.exp(scores - peak_ref[head : head + 1, :])
        inverse = 1.0 / total_ref[head : head + 1, :]
        grad = grad_ref[rows, :].astype(F32)
        scaled = (grad * inverse).astype(BF)
        delta = jnp.sum(grad * out_ref[rows, :].astype(F32), axis=0, keepdims=True) * inverse
        grad_weights = contract(value, scaled, 0, 0)
        grad_scores = (SCALE * (weights * (grad_weights - delta))).astype(BF)
        grad_query = contract(key, grad_scores, 1, 0)
        grad_value = contract(scaled, weights.astype(BF), 1, 1)
        res_ref[rows, :] = grad_query.astype(BF)
        res_ref[key_rows, :] = contract(query, grad_scores, 1, 1).astype(BF)
        res_ref[value_rows, :] = grad_value.astype(BF)
        sum_ref[rows, 0:1] = jnp.sum(grad_query, axis=1, keepdims=True)
        sum_ref[rows, 1:2] = jnp.sum(grad_value, axis=1, keepdims=True)


def self_bwd_kernel(
    scalar_ref, qkv_ref, out_ref, grad_ref, peak_ref, total_ref, send_ref, sum_ref, res_ref, *, planes
):
    self_bwd_heads(
        scalar_ref[0], qkv_ref, out_ref, grad_ref, peak_ref, total_ref, res_ref, sum_ref
    )
    height = qkv_ref.shape[0] // (2 * GROUP * planes)
    for k in range(GROUP):
        for r in range(planes):
            at = pl.multiple_of(scalar_ref[1 + k * planes + r] * height, height)
            send_ref[k, r * height : (r + 1) * height, :] = res_ref[pl.ds(at, height), :]


def plain_self_bwd_kernel(
    scalar_ref, qkv_ref, out_ref, grad_ref, peak_ref, total_ref, res_ref, sum_ref
):
    self_bwd_heads(
        scalar_ref[0], qkv_ref, out_ref, grad_ref, peak_ref, total_ref, res_ref, sum_ref
    )


def cross_fwd_kernel(len_ref, query_ref, key_ref, value_ref, out_ref, peak_ref, total_ref):
    height, steps = query_ref.shape
    span = key_ref.shape[1]
    valid = lax.broadcasted_iota(jnp.int32, (span, steps), 0) < len_ref[0]
    for head in range(height // HEAD_DIM):
        rows = slice(head * HEAD_DIM, (head + 1) * HEAD_DIM)
        scores = contract(key_ref[rows, :], query_ref[rows, :] * SCALE, 0, 0)
        scores = jnp.where(valid, scores, FILL)
        peak = jnp.max(scores, axis=0, keepdims=True)
        weights = jnp.exp(scores - peak)
        out_ref[rows, :] = contract(value_ref[rows, :], weights.astype(BF), 1, 0).astype(BF)
        peak_ref[0, head : head + 1, :] = peak
        total_ref[0, head : head + 1, :] = jnp.sum(weights, axis=0, keepdims=True)


def cross_bwd_kernel(
    scalar_ref,
    query_ref,
    kv_ref,
    out_ref,
    grad_ref,
    peak_ref,
    total_ref,
    grad_query_ref,
    grad_kv_ref,
    sum_ref,
    *block_refs,
    height,
):
    width, steps = query_ref.shape
    span = kv_ref.shape[1]
    valid = lax.broadcasted_iota(jnp.int32, (span, steps), 0) < scalar_ref[0]

    for head in range(width // HEAD_DIM):
        first = head * HEAD_DIM
        rows = slice(first, first + HEAD_DIM)
        value_rows = slice(width + first, width + first + HEAD_DIM)
        query, key, value = query_ref[rows, :], kv_ref[rows, :], kv_ref[value_rows, :]
        scores = jnp.where(valid, contract(key, query * SCALE, 0, 0), FILL)
        weights = jnp.exp(scores - peak_ref[head : head + 1, :])
        inverse = 1.0 / total_ref[head : head + 1, :]
        grad = grad_ref[rows, :].astype(F32)
        scaled = (grad * inverse).astype(BF)
        delta = jnp.sum(grad * out_ref[rows, :].astype(F32), axis=0, keepdims=True) * inverse
        grad_weights = contract(value, scaled, 0, 0)
        grad_scores = (SCALE * (weights * (grad_weights - delta))).astype(BF)
        grad_query = contract(key, grad_scores, 1, 0).astype(BF)
        grad_key = contract(query, grad_scores, 1, 1).astype(BF)
        grad_value = contract(scaled, weights.astype(BF), 1, 1)
        sum_ref[rows, :] = jnp.sum(grad_value, axis=1, keepdims=True)
        grad_value = grad_value.astype(BF)
        grad_query_ref[rows, :] = grad_query
        grad_kv_ref[rows, :] = grad_key
        grad_kv_ref[value_rows, :] = grad_value
    if not block_refs:
        return
    for ref in block_refs:
        ref[...] = jnp.zeros_like(ref)
    for core in range(2):

        @pl.when(scalar_ref[1] == core)
        def _():
            for first in range(0, 3 * width, UNIT):
                block, offset = divmod(first, height)
                to = block_refs[(block + core) % 2]
                chip = scalar_ref[2 + block // 2]
                rows = slice(offset, offset + UNIT)
                if first < width:
                    to[chip, rows, :steps] = grad_query_ref[first : first + UNIT, :]
                else:
                    from_rows = slice(first - width, first - width + UNIT)
                    to[chip, rows, steps:] = grad_kv_ref[from_rows, :]


def store_messages(parts, own_ref, first_ref, second_ref, hold_first_ref, hold_second_ref):
    half = own_ref.shape[0] // 2
    own_ref[...] = parts[0]
    first_ref[:half] = parts[1][:half]
    first_ref[half:] = parts[3][:half]
    second_ref[:half] = parts[2][half:]
    second_ref[half:] = parts[3][half:]
    hold_first_ref[...] = parts[2][:half]
    hold_second_ref[...] = parts[1][half:]


def message_shapes(rows, width):
    return [shape((n, width), BF) for n in (rows, rows, rows, rows // 2, rows // 2)]


def store_messages(parts, own_ref, first_ref, second_ref, hold_first_ref, hold_second_ref):
    half = own_ref.shape[0] // 2
    own_ref[...] = parts[0]
    first_ref[:half] = parts[1][:half]
    first_ref[half:] = parts[3][:half]
    second_ref[:half] = parts[2][half:]
    second_ref[half:] = parts[3][half:]
    hold_first_ref[...] = parts[2][:half]
    hold_second_ref[...] = parts[1][half:]


def message_shapes(rows, width):
    return [shape((n, width), BF) for n in (rows, rows, rows, rows // 2, rows // 2)]


def cross_rows_kernel(mine_ref, came_ref, normed_ref, memory_ref, other_ref, *out_refs):
    steps = normed_ref.shape[0]
    chips, height, columns = mine_ref.shape
    rows = chips // GROUP
    parts = []
    for n in range(GROUP):
        at = slice(n * rows, (n + 1) * rows)
        mine = mine_ref[at].reshape(rows * height, columns)
        came = came_ref[at].reshape(rows * height, columns)
        query = (mine[:, :steps].astype(F32) + came[:, :steps].astype(F32)).astype(BF)
        total = contract(mine[:, steps:], memory_ref[...], 1, 0)
        total += contract(came[:, steps:], other_ref[...], 1, 0)
        total += contract(query, normed_ref[...], 1, 0)
        parts.append(total.astype(BF))
    store_messages(parts, *out_refs)


def out_rows_kernel(scalar_ref, self_ref, cross_ref, one_ref, two_ref, *rest, height):
    out_refs, left_ref = rest[:-1], rest[-1]
    width, steps = self_ref.shape
    each = width // GROUP
    rows = width // height
    for n in range(rows):
        at = pl.multiple_of(scalar_ref[n] * height, height)
        is_self = at < width
        own = jnp.where(
            is_self,
            self_ref[pl.ds(pl.multiple_of(jnp.where(is_self, at, 0), height), height), :],
            cross_ref[pl.ds(pl.multiple_of(jnp.where(is_self, 0, at - width), height), height), :],
        )
        none = jnp.zeros_like(own)
        to = slice(n * height, (n + 1) * height)
        left_ref[to, :steps] = jnp.where(is_self, own, none)
        left_ref[to, steps:] = jnp.where(is_self, none, own)
    parts = []
    for n in range(GROUP):
        left = left_ref[n * each : (n + 1) * each, :]
        total = contract(left[:, :steps], one_ref[...], 1, 0)
        total += contract(left[:, steps:], two_ref[...], 1, 0)
        parts.append(total.astype(BF))
    store_messages(parts, *out_refs)


def fc_blocks(packs):
    rows = (packs[0].shape[0] - SMALL) // 2
    for n in range(0, len(packs), 2):
        pair = packs[n : n + 2]
        first = jnp.concatenate([pack[:rows, :] for pack in pair])
        second = jnp.concatenate([pack[rows : 2 * rows, :] for pack in pair])
        bias = jnp.concatenate([pack[2 * rows : 2 * rows + 1, :rows] for pack in pair], axis=1)
        yield slice(n * rows, (n + 2) * rows), first, second, bias.astype(F32)


def store_by_member(total, refs):
    rows = refs[0].shape[0]
    for n, ref in enumerate(refs):
        ref[...] = total[n * rows : (n + 1) * rows].astype(ref.dtype)


def fc_fwd_kernel(*refs):
    token_refs, packs = refs[:GROUP], refs[GROUP : -2 - GROUP]
    out_refs, (act_ref, slope_ref) = refs[-2 - GROUP : -2], refs[-2:]
    tokens = jnp.concatenate([ref[...] for ref in token_refs])
    total = jnp.zeros(tokens.shape, F32)
    for at, first, second, bias in fc_blocks(packs):
        inner = contract(tokens, first, 1, 1) + bias
        below = 0.5 * (1.0 + lax.erf(inner * 0.7071067811865476))
        density = jnp.exp(-0.5 * inner * inner) * 0.3989422804014327
        activation = (inner * below).astype(BF)
        act_ref[:, at] = activation
        slope_ref[:, at] = below + inner * density
        total += contract(activation, second, 1, 0)
    store_by_member(total, out_refs)


def fc_bwd_kernel(*refs):
    grad_refs, slope_ref, packs = refs[:GROUP], refs[GROUP], refs[GROUP + 1 : -2 - GROUP]
    out_refs, (inner_ref, bias_ref) = refs[-2 - GROUP : -2], refs[-2:]
    grads = jnp.concatenate([ref[...] for ref in grad_refs])
    total = jnp.zeros(grads.shape, F32)
    for at, first, second, _ in fc_blocks(packs):
        grad_inner = contract(grads, second, 1, 1) * slope_ref[:, at]
        bias_ref[0:1, at] = jnp.sum(grad_inner, axis=0, keepdims=True)
        grad_inner = grad_inner.astype(BF)
        inner_ref[:, at] = grad_inner
        total += contract(grad_inner, first, 1, 0)
    store_by_member(total, out_refs)


def fc_rows_kernel(place_ref, *refs):
    token_refs, grad_refs = refs[:GROUP], refs[GROUP : 2 * GROUP]
    act_ref, inner_ref, bias_ref = refs[2 * GROUP : 2 * GROUP + 3]
    outs = refs[2 * GROUP + 3 :]
    tokens = jnp.concatenate([ref[...] for ref in token_refs])
    grads = jnp.concatenate([ref[...] for ref in grad_refs])
    width = tokens.shape[1]
    rows = (outs[0].shape[1] - SMALL) // 2
    at = 0
    for out in outs:
        for r in range(0, out.shape[0], 2):
            both = slice(at, at + 2 * rows)
            first = contract(inner_ref[:, both], tokens, 0, 0).astype(BF)
            second = contract(act_ref[:, both], grads, 0, 0).astype(BF)
            for n in range(2):
                place = place_ref[r + n]
                part = slice(n * rows, (n + 1) * rows)
                out[place, :rows, :] = first[part]
                out[place, rows : 2 * rows, :] = second[part]
                bias = bias_ref[0:1, at + n * rows : at + (n + 1) * rows].astype(BF)
                bias = jnp.concatenate([bias, jnp.zeros((1, width - rows), BF)], axis=1)
                bias = jnp.concatenate([bias, jnp.zeros((SMALL - 1, width), BF)])
                out[place, 2 * rows :, :] = bias
            at += 2 * rows


SCALARS = pl.BlockSpec(memory_space=pltpu.SMEM)
WHOLE = pl.BlockSpec(memory_space=pltpu.VMEM)
PARAMS = pltpu.CompilerParams(vmem_limit_bytes=48 * 1024 * 1024)
HEADS_A_STEP = 8
UNIT = 32


def shape(dims, dtype):
    return jax.ShapeDtypeStruct(dims, dtype)


def self_fwd(length, mine, other, places, planes):
    steps = mine.shape[2]
    width = (mine.shape[1] - planes * SMALL) * 2 * GROUP // 3
    stats = [shape((width // HEAD_DIM, steps), F32)] * 2
    return pl.pallas_call(
        functools.partial(self_fwd_kernel, planes=planes),
        in_specs=[SCALARS] + [WHOLE] * 2,
        out_specs=[WHOLE] * 6,
        out_shape=[shape((3 * width, steps), BF), shape((width, steps), BF)]
        + stats
        + [shape((SMALL, width), F32), shape((2, width, steps), F32)],
        compiler_params=PARAMS,
        name="self_fwd",
    )(jnp.concatenate([length, places]), mine, other)


def plain_self_fwd(length, mine, other, places, planes, small):
    width, steps = small.shape[1], mine.shape[2]
    stats = [shape((width // HEAD_DIM, steps), F32)] * 2
    height = 3 * width // (2 * GROUP * planes)
    blocks = jnp.stack([mine, other])[:, :, : planes * height].reshape(-1, height, steps)
    qkv = jnp.zeros_like(blocks).at[places].set(blocks).reshape(3 * width, steps)
    bias = jnp.concatenate([small[0], jnp.zeros((width,), F32), small[1]])
    qkv = (qkv.astype(F32) + bias[:, None]).astype(BF)
    column = jnp.broadcast_to(small[3:5, :, None], (2, width, steps))
    results = pl.pallas_call(
        plain_self_fwd_kernel,
        in_specs=[SCALARS, WHOLE],
        out_specs=[WHOLE] * 3,
        out_shape=[shape((width, steps), BF)] + stats,
        compiler_params=PARAMS,
        name="self_fwd",
    )(length, qkv)
    return [qkv, *results, small, column]


def self_bwd(length, places, qkv, out, grad, peak, total, planes):
    width, steps = out.shape
    height = 3 * width // (2 * GROUP * planes)
    sums = shape((width, 2), F32)
    if height % 16 == 0:
        return pl.pallas_call(
            functools.partial(self_bwd_kernel, planes=planes),
            in_specs=[SCALARS] + [WHOLE] * 5,
            out_specs=[WHOLE] * 2,
            out_shape=[shape((GROUP, planes * height, steps), BF), sums],
            scratch_shapes=[pltpu.VMEM(qkv.shape, BF)],
            compiler_params=PARAMS,
            name="self_bwd",
        )(jnp.concatenate([length, places]), qkv, out, grad, peak, total)
    res, total = pl.pallas_call(
        plain_self_bwd_kernel,
        in_specs=[SCALARS] + [WHOLE] * 5,
        out_specs=[WHOLE] * 2,
        out_shape=[shape(qkv.shape, BF), sums],
        compiler_params=PARAMS,
        name="self_bwd",
    )(length, qkv, out, grad, peak, total)
    send = res.reshape(-1, height, steps)[places[: GROUP * planes]]
    return send.reshape(GROUP, planes * height, steps), total


def cross_specs(width, steps, span):
    count = width // HEAD_DIM // HEADS_A_STEP
    height = HEADS_A_STEP * HEAD_DIM
    by_step = pl.BlockSpec((height, steps), lambda i: (i, 0))
    keys = pl.BlockSpec((height, span), lambda i: (i, 0))
    values = pl.BlockSpec((height, span), lambda i: (i + count, 0))
    stats = pl.BlockSpec((1, HEADS_A_STEP, steps), lambda i: (i, 0, 0))
    column = pl.BlockSpec((height, 1), lambda i: (i, 0))
    return count, by_step, keys, values, stats, column


def cross_fwd(length, query, key_value):
    width, steps = query.shape
    count, by_step, keys, values, stats, _ = cross_specs(width, steps, key_value.shape[1])
    stat_shape = shape((count, HEADS_A_STEP, steps), F32)
    return pl.pallas_call(
        cross_fwd_kernel,
        grid=(count,),
        in_specs=[SCALARS, by_step, keys, values],
        out_specs=[by_step, stats, stats],
        out_shape=[shape((width, steps), BF), stat_shape, stat_shape],
        compiler_params=PARAMS,
        name="cross_fwd",
    )(length, query, key_value, key_value)


def cross_bwd(scalars, query, key_value, out, grad, peak, total, chips, height):
    width, steps = query.shape
    span = key_value.shape[1]
    outs = [shape((width, steps), BF), shape((2 * width, span), BF), shape((width, 1), F32)]
    if height:
        outs += [shape((chips, height, steps + span), BF)] * 2
    return pl.pallas_call(
        functools.partial(cross_bwd_kernel, height=height),
        in_specs=[SCALARS] + [WHOLE] * 6,
        out_specs=[WHOLE] * len(outs),
        out_shape=outs,
        compiler_params=PARAMS,
        name="cross_bwd",
    )(scalars, query, key_value, out, grad, peak, total)


def cross_rows(mine, came, normed, memory, other):
    chips, height, _ = mine.shape
    outs = message_shapes(chips // GROUP * height, memory.shape[1])
    return pl.pallas_call(
        cross_rows_kernel,
        in_specs=[WHOLE] * 5,
        out_specs=[WHOLE] * len(outs),
        out_shape=outs,
        compiler_params=PARAMS,
        name="cross_rows",
    )(mine, came, normed, memory, other)


def out_rows(scalars, self_out, cross_out, one, two, height):
    width, steps = self_out.shape
    outs = message_shapes(width // GROUP, width)
    return pl.pallas_call(
        functools.partial(out_rows_kernel, height=height),
        in_specs=[SCALARS] + [WHOLE] * 4,
        out_specs=[WHOLE] * len(outs),
        out_shape=outs,
        scratch_shapes=[pltpu.VMEM((width, 2 * steps), BF)],
        compiler_params=PARAMS,
        name="out_rows",
    )(scalars, self_out, cross_out, one, two)


def member_shapes(rows, width):
    return [shape((rows, width), F32)] + [shape((rows, width), BF)] * (GROUP - 1)


def fc_fwd(tokens, packs):
    rows, width = tokens[0].shape
    hidden = len(packs) * (packs[0].shape[0] - SMALL) // 2
    outs = member_shapes(rows, width)
    outs += [shape((GROUP * rows, hidden), BF), shape((GROUP * rows, hidden), F32)]
    return pl.pallas_call(
        fc_fwd_kernel,
        in_specs=[WHOLE] * (GROUP + len(packs)),
        out_specs=[WHOLE] * len(outs),
        out_shape=outs,
        compiler_params=PARAMS,
        name="fc_fwd",
    )(*tokens, *packs)


def fc_bwd(grads, packs, slope):
    rows, width = grads[0].shape
    hidden = slope.shape[1]
    outs = member_shapes(rows, width)
    outs += [shape((GROUP * rows, hidden), BF), shape((8, hidden), F32)]
    return pl.pallas_call(
        fc_bwd_kernel,
        in_specs=[WHOLE] * (GROUP + 1 + len(packs)),
        out_specs=[WHOLE] * len(outs),
        out_shape=outs,
        compiler_params=PARAMS,
        name="fc_bwd",
    )(*grads, slope, *packs)


def fc_rows(places, tokens, grads, activation, inner, bias, pack_shape):
    return pl.pallas_call(
        fc_rows_kernel,
        in_specs=[SCALARS] + [WHOLE] * (2 * GROUP + 3),
        out_specs=[WHOLE] * 2,
        out_shape=[shape(pack_shape, BF)] * 2,
        compiler_params=PARAMS,
        name="fc_rows",
    )(places, *tokens, *grads, activation, inner, bias)


def place_blocks(places, blocks, heights):
    width = blocks[0].shape[2]
    count = len(blocks) * GROUP
    starts = [sum(heights[:n]) for n in range(len(heights))]

    def kernel(place_ref, *refs):
        ins, outs, sems = refs[: len(blocks)], refs[len(blocks) : -1], refs[-1]
        copies = []
        for block in range(count):
            place = place_ref[block]
            for n, (start, height) in enumerate(zip(starts, heights)):
                copies.append(
                    pltpu.make_async_copy(
                        ins[block // GROUP].at[block % GROUP, pl.ds(start, height)],
                        outs[n].at[place],
                        sems.at[block, n],
                    )
                )
        for copy in copies:
            copy.start()
        for copy in copies:
            copy.wait()

    anywhere = pl.BlockSpec(memory_space=pl.ANY)
    return pl.pallas_call(
        kernel,
        in_specs=[SCALARS] + [WHOLE] * len(blocks),
        out_specs=[anywhere] * len(heights),
        out_shape=[shape((count, height, width), blocks[0].dtype) for height in heights],
        scratch_shapes=[pltpu.SemaphoreType.DMA((count, len(heights)))],
        compiler_params=PARAMS,
        name="place_blocks",
    )(places, *blocks)


def local(mesh, dec_in, memory, cotangent, mem_lengths, dec_lengths, *weights):
    attn_in, cross_in, attn_out, fc_in, fc_out, biases, fc_bias, gains, shifts = weights
    chips, cores = mesh.shape["items"], mesh.shape["mem"]
    devices = chips * cores
    planes = chips // GROUP
    chip, core = lax.axis_index("items"), lax.axis_index("mem")
    plane, member = chip // GROUP, chip % GROUP

    by_plane = [list(range(k, chips, GROUP)) for k in range(GROUP)]

    def ring(a, step, name="plane"):
        pairs = [
            (i, (i // GROUP + step) % planes * GROUP + i % GROUP) for i in range(chips)
        ]
        with jax.named_scope(f"{name}_z{step}"):
            return lax.ppermute(a, "items", pairs)

    def across(a, mask, name="member"):
        with jax.named_scope(f"{name}_xy{mask}"):
            return lax.ppermute(a, "items", [(i, i ^ mask) for i in range(chips)])

    def swap(a, name="core"):
        with jax.named_scope(f"{name}_core"):
            return lax.ppermute(a, "mem", [(0, 1), (1, 0)])

    def by_core(mine, other):
        return jnp.where(core == 0, jnp.concatenate([mine, other]), jnp.concatenate([other, mine]))

    def ring_gather(a, name):
        held = [a]
        for _ in range(planes - 1):
            held.append(ring(held[-1], 1, name))
        return held

    def gather_rows(pack, heights):
        if planes != 4:
            whole = lax.all_gather(pack, ("items", "mem"), axis=0)
            starts = [sum(heights[:n]) for n in range(len(heights))]
            return [whole[:, s : s + h] for s, h in zip(starts, heights)]
        blocks, places = [], []
        for r, block in enumerate(ring_gather(pack, "rest")):
            first, second = (1, 2) if r < 2 else (2, 1)
            one = across(block, first, f"rest{r}")
            two = across(block, second, f"rest{r}")
            three = across(one, second, f"rest{r}far")
            near = jnp.stack([block, one, two, three])
            blocks += [near, swap(near, f"rest{r}")]
            source = (plane - r) % planes * GROUP
            for which in (core, 1 - core):
                places += [(source + (member ^ m)) * cores + which for m in (0, first, second, 3)]
        return place_blocks(jnp.stack(places).astype(jnp.int32), blocks, heights)

    def scatter_first(messages, name):
        _, first, second, _, _ = messages
        return across(first, 1, f"{name}_first"), across(second, 2, f"{name}_first")

    def scatter_second(messages, came, name):
        hold_first, hold_second = messages[3:]
        half = hold_first.shape[0]
        far_first = hold_first.astype(F32) + came[0][half:].astype(F32)
        far_second = hold_second.astype(F32) + came[1][half:].astype(F32)
        far_first = across(far_first.astype(BF), 2, f"{name}_second")
        return far_first, across(far_second.astype(BF), 1, f"{name}_second")

    def scatter_planes(messages, came, far):
        own = messages[0]
        half = own.shape[0] // 2
        height = own.shape[0] // planes
        sums = []
        for r in range(planes):
            which = 0 if 2 * r < planes else 1
            at = r * height % half
            rows = slice(at, at + height)
            near = own[r * height : (r + 1) * height].astype(F32)
            sums.append(near + came[which][rows].astype(F32) + far[which][rows].astype(F32))
        return sums

    def plane_sum(sums, name):
        total = sums[0]
        for r in range(1, planes):
            total = total + ring(sums[r].astype(BF), planes - r, name).astype(F32)
        return total

    def scatter_whole(part):
        return lax.psum_scatter(part, ("items", "mem"), scatter_dimension=0, tiled=True)

    def to_members(mine, name):
        return [mine] + [across(mine, mask, name) for mask in range(1, GROUP)]

    def from_members(parts, name):
        total = parts[0]
        for mask in range(1, GROUP):
            total = total + across(parts[mask], mask, name).astype(F32)
        return total

    def group_gather(mine, name):
        near = jnp.stack([mine] + [across(mine, mask, name) for mask in range(1, GROUP)])
        both = jnp.stack([near, swap(near, name)])
        return both.reshape(cores * GROUP * mine.shape[0], mine.shape[1])

    def group_sum(part, name):
        part = part.reshape(cores, GROUP, -1, part.shape[1])
        near = part[0] + swap(part[1].astype(BF), name).astype(F32)
        total = near[0]
        for mask in range(1, GROUP):
            total = total + across(near[mask].astype(BF), mask, name).astype(F32)
        return total

    width = dec_in.shape[2]
    steps = dec_in.shape[1]
    half = steps // cores
    span = memory.shape[1]
    row_attn, row_out, row_fc = attn_in.shape[0], attn_out.shape[0], fc_in.shape[0]
    small = jnp.concatenate([biases, gains, shifts])
    vectors, slice_width = small.shape

    regular = planes == 4 and row_attn % UNIT == 0 and row_out == HEAD_DIM and row_fc % 128 == 0

    def padded(a):
        return jnp.pad(a, ((0, SMALL - a.shape[0]), (0, width - a.shape[1])))

    def after(a, *others):
        return lax.optimization_barrier((a, *others))[0]

    tokens = dec_in[0]
    mem_rows = memory[0]
    attn_held = ring_gather(jnp.concatenate([attn_in, padded(small)]), "attn")
    group_tokens = jnp.concatenate([tokens] + [across(tokens, k, "tokens") for k in range(1, GROUP)])
    w_attn = jnp.concatenate([a[:row_attn] for a in attn_held])
    projected = contract(w_attn, group_tokens, 1, 1).astype(BF)
    small_held = [a[row_attn:, :steps] for a in attn_held]
    sends = [
        jnp.concatenate([projected[:, k * steps : (k + 1) * steps]] + small_held)
        for k in range(GROUP)
    ]
    mine = jnp.stack([sends[0]] + [across(sends[k], k, "qkv") for k in range(1, GROUP)])
    other = swap(mine, "qkv")
    w_cross = lax.all_gather(cross_in, ("items", "mem"), tiled=True)
    (w_out,) = gather_rows(attn_out, [row_out])
    w_out = w_out.reshape(-1, width)
    fc_held = ring_gather(jnp.concatenate([fc_in, fc_out, padded(fc_bias[None])]), "fc")
    if regular:
        fc_packs = fc_held + [swap(a, "fc") for a in fc_held]
    else:
        fc_held = jnp.stack(fc_held)
        w_fc_in = fc_held[:, :row_fc].reshape(-1, width)
        w_fc_out = fc_held[:, row_fc : 2 * row_fc].reshape(-1, width)
        fc_bias_held = fc_held[:, 2 * row_fc, :row_fc].reshape(-1).astype(F32)

    n = jnp.arange(cores * GROUP * planes)
    from_core, from_member = n // (GROUP * planes), n // planes % GROUP
    from_plane = (plane - n % planes) % planes
    places = (from_plane * GROUP + (member ^ from_member)) * cores + (core ^ from_core)
    places = places.astype(jnp.int32)

    if regular:
        fwd = self_fwd(dec_lengths, mine, other, places, planes)
    else:
        rows_small = lax.all_gather(small, ("items", "mem"), axis=1, tiled=True).astype(F32)
        fwd = plain_self_fwd(dec_lengths, mine, other, places, planes, rows_small)
    qkv, self_out, self_peak, self_total, rows_small, columns = fwd
    bias, gain, shift = (
        [rows_small[n : n + 1] for n in span] for span in (range(7), range(7, 10), range(10, 13))
    )
    hidden_one = tokens.astype(F32) + contract(self_out, w_out[:width], 0, 0) + bias[2]
    normal_one, spread_one = norm_parts(hidden_one)
    normed_one = normal_one * gain[0] + shift[0]
    normed_one_low = normed_one.astype(BF)
    cross_query = (contract(w_cross[:width], normed_one_low, 1, 1) + columns[0]).astype(BF)
    cross_kv = contract(w_cross[width:], mem_rows, 1, 1).astype(BF)
    mem_left = mem_lengths - core * span
    part_out, part_peak, part_total = cross_fwd(mem_left, cross_query, cross_kv)
    other_out = swap(part_out, "cross_out")
    other_stats = swap(jnp.stack([part_peak, part_total]), "stats")
    other_peak, other_total = other_stats[0], other_stats[1]
    cross_peak = jnp.maximum(part_peak, other_peak)
    mine_factor = jnp.exp(part_peak - cross_peak)
    other_factor = jnp.exp(other_peak - cross_peak)
    cross_total = mine_factor * part_total + other_factor * other_total
    heads = width // HEAD_DIM

    def per_head(stat):
        return stat.reshape(heads, 1, steps)

    cross_out = (
        per_head(mine_factor / cross_total) * part_out.reshape(heads, HEAD_DIM, steps).astype(F32)
        + per_head(other_factor / cross_total)
        * other_out.reshape(heads, HEAD_DIM, steps).astype(F32)
    )
    cross_plain = cross_out.reshape(width, steps)
    cross_out = (cross_plain + columns[1]).astype(BF)
    cross_plain = cross_plain.astype(BF)

    def own(rows):
        return lax.dynamic_slice_in_dim(rows, core * half, half)

    hidden_two = own(normed_one + contract(cross_out, w_out[width:], 0, 0)) + bias[5]
    normal_two, spread_two = norm_parts(hidden_two)
    normed_two = normal_two * gain[1] + shift[1]
    if regular:
        member_two = to_members(normed_two.astype(BF), "normed_two")
        *parts, activation, slope = fc_fwd(member_two, fc_packs)
        fc_result = from_members(parts, "three")
    else:
        group_two = group_gather(normed_two.astype(BF), "normed_two")
        inner = contract(group_two, w_fc_in, 1, 1) + fc_bias_held
        activation = jax.nn.gelu(inner, approximate=False).astype(BF)
        fc_result = group_sum(contract(activation, w_fc_out, 1, 0), "three")
    hidden_three = normed_two + fc_result + bias[6]
    normal_three, spread_three = norm_parts(hidden_three)
    out_own = (normal_three * gain[2] + shift[2]).astype(BF)
    output = by_core(out_own, swap(out_own, "output"))[None]
    mem_other = swap(after(mem_rows, out_own), "memory")

    grad_three, grad_gain_three, grad_shift_three = norm_back(
        own(cotangent[0]).astype(F32), normal_three, spread_three, gain[2]
    )
    if regular:
        member_three = to_members(grad_three.astype(BF), "grad_three")
        *parts, grad_inner, grad_fc_bias = fc_bwd(member_three, fc_packs, slope)
        plane_places = ((plane - jnp.arange(planes)) % planes).astype(jnp.int32)
        fc_mine, fc_other = fc_rows(
            plane_places,
            member_two,
            member_three,
            activation,
            grad_inner,
            grad_fc_bias,
            (planes, *fc_held[0].shape),
        )
        grad_normed_two = after(grad_three + from_members(parts, "grad_two"), fc_mine)
        fc_part = (fc_mine.astype(F32) + swap(fc_other, "fc_grad").astype(F32)).astype(BF)
    else:
        group_three = group_gather(grad_three.astype(BF), "grad_three")
        grad_activation = contract(group_three, w_fc_out, 1, 1)
        density = jnp.exp(-0.5 * inner * inner) * 0.3989422804014327
        below = 0.5 * (1.0 + lax.erf(inner * 0.7071067811865476))
        grad_inner = grad_activation * (below + inner * density)
        grad_inner_low = grad_inner.astype(BF)
        grad_normed_two = grad_three + group_sum(
            contract(grad_inner_low, w_fc_in, 1, 0), "grad_two"
        )
        fc_part = jnp.concatenate(
            [
                contract(grad_inner_low, group_two, 0, 0).reshape(planes, row_fc, width),
                contract(activation, group_three, 0, 0).reshape(planes, row_fc, width),
                jnp.pad(
                    jnp.sum(grad_inner, axis=0).reshape(planes, 1, row_fc),
                    ((0, 0), (0, SMALL - 1), (0, width - row_fc)),
                ),
            ],
            axis=1,
        )
        fc_part = jnp.concatenate(
            [
                lax.dynamic_slice_in_dim(fc_part, (plane - at) % planes, 1)
                for at in range(planes)
            ]
        ).astype(BF)
    fc_sum = lax.psum_scatter(
        fc_part, "items", scatter_dimension=0, axis_index_groups=by_plane
    ).astype(F32)
    sum_fc_in, sum_fc_out = fc_sum[:row_fc], fc_sum[row_fc : 2 * row_fc]
    sum_fc_bias = fc_sum[2 * row_fc, :row_fc]
    grad_two, grad_gain_two, grad_shift_two = norm_back(
        grad_normed_two, normal_two, spread_two, gain[1]
    )

    grad_two_low = grad_two.astype(BF)
    grad_two_all = by_core(grad_two_low, swap(grad_two_low, "grad_two"))
    grad_cross = contract(w_out[width:], grad_two_all, 1, 1).astype(BF)
    grad_cross = after(grad_cross, fc_part)
    chip_at = jnp.arange(chips)
    far = ((chip_at % GROUP) ^ member) * planes + (plane - chip_at // GROUP) % planes
    scalars = jnp.concatenate([mem_left, core.reshape(1), far]).astype(jnp.int32)
    grad_query, grad_kv, grad_value_sum, *blocks = cross_bwd(
        scalars,
        cross_query,
        cross_kv,
        cross_plain,
        grad_cross,
        cross_peak.reshape(heads, steps),
        cross_total.reshape(heads, steps),
        chips,
        row_attn if regular else 0,
    )
    if regular:
        came_blocks = swap(blocks[1], "cross_blocks")
        cross_parts = cross_rows(blocks[0], came_blocks, normed_one_low, mem_rows, mem_other)
    grad_query_all = grad_query.astype(F32) + swap(grad_query, "grad_query").astype(F32)
    grad_query_low = grad_query_all.astype(BF)
    grad_one, grad_gain_one, grad_shift_one = norm_back(
        grad_two + own(contract(grad_query_low, w_cross[:width], 0, 0)),
        own(normal_one),
        own(spread_one),
        gain[0],
    )
    grad_one_low = grad_one.astype(BF)
    grad_one_all = by_core(grad_one_low, swap(grad_one_low, "grad_one"))
    if regular:
        grad_one_all = after(grad_one_all, cross_parts[0])
    grad_self = contract(w_out[:width], grad_one_all, 1, 1).astype(BF)
    grad_sends, grad_qv_sum = self_bwd(
        dec_lengths, places, qkv, self_out, grad_self, self_peak, self_total, planes
    )


    def of_core(a, which):
        return lax.dynamic_index_in_dim(a, which, 1, keepdims=False)

    if regular:
        came_cross = scatter_first(cross_parts, "cross_grad")
        far_cross = scatter_second(cross_parts, came_cross, "cross_grad")
        cross_sums = scatter_planes(cross_parts, came_cross, far_cross)
        sum_cross = plane_sum(cross_sums, "cross_grad")
        out_places = places[: GROUP * planes]
        out_parts = out_rows(
            out_places, self_out, cross_out, grad_one_all, grad_two_all, row_out
        )
        came_out = scatter_first(out_parts, "out_grad")
        far_out = scatter_second(out_parts, came_out, "out_grad")
        out_sums = scatter_planes(out_parts, came_out, far_out)
        sum_out = plane_sum(out_sums, "out_grad")
    else:
        sum_cross = scatter_whole(
            jnp.concatenate(
                [contract(grad_query, normed_one_low, 1, 0), contract(grad_kv, mem_rows, 1, 0)]
            )
        )
        part_out = [
            contract(self_out, grad_one_all, 1, 0),
            contract(cross_out, grad_two_all, 1, 0),
        ]
        sum_out = scatter_whole(jnp.concatenate(part_out) / cores)

    grad_held = jnp.concatenate(
        [grad_sends[0]] + [across(grad_sends[k], k, "grad_qkv") for k in range(1, GROUP)], axis=1
    )
    part_attn = contract(grad_held, group_tokens, 1, 0)
    grad_memory = contract(after(grad_kv, part_attn), w_cross[width:], 0, 0).astype(BF)[None]
    sum_attn = part_attn[:row_attn]
    for r in range(1, planes):
        rows = slice(r * row_attn, (r + 1) * row_attn)
        sum_attn = sum_attn + ring(part_attn[rows].astype(BF), planes - r, "attn_grad").astype(F32)
    part_tokens = contract(grad_held, w_attn, 0, 0).reshape(GROUP, cores, half, width)
    part_tokens = jnp.stack([of_core(part_tokens, core), of_core(part_tokens, 1 - core)])
    grad_tokens_low = (grad_one + group_sum(part_tokens.reshape(-1, width), "grad_dec")).astype(BF)
    grad_dec_in = by_core(grad_tokens_low, swap(grad_tokens_low, "grad_dec"))[None]

    part_vectors = jnp.stack(
        [
            grad_qv_sum[:, 0] / cores,
            grad_qv_sum[:, 1] / cores,
            jnp.sum(grad_one, axis=0),
            jnp.sum(grad_query.astype(F32), axis=1),
            grad_value_sum[:, 0],
            jnp.sum(grad_two, axis=0),
            jnp.sum(grad_three, axis=0),
            grad_gain_one,
            grad_gain_two,
            grad_gain_three,
            grad_shift_one,
            grad_shift_two,
            grad_shift_three,
        ]
    )
    part_vectors = jnp.transpose(part_vectors.reshape(vectors, devices, slice_width), (1, 0, 2))
    came = lax.all_to_all(
        after(part_vectors.reshape(devices, vectors * slice_width), part_attn),
        ("items", "mem"),
        split_axis=0,
        concat_axis=0,
        tiled=True,
    )
    sum_vectors = jnp.sum(came, axis=0).reshape(vectors, slice_width)
    return (
        output,
        grad_dec_in,
        grad_memory,
        sum_attn,
        sum_cross,
        sum_out,
        sum_fc_in,
        sum_fc_out,
        sum_vectors[:7],
        sum_fc_bias,
        sum_vectors[7:10],
        sum_vectors[10:vectors],
    )


def solution(mesh):
    rows = P(("items", "mem"), None)
    columns = P(None, ("items", "mem"))
    item = P("items", None, None)
    in_specs = (
        item,
        P("items", "mem", None),
        item,
        P("items"),
        P("items"),
        rows,
        rows,
        rows,
        rows,
        rows,
        columns,
        P(("items", "mem")),
        columns,
        columns,
    )
    out_specs = (
        item,
        item,
        P("items", "mem", None),
        rows,
        rows,
        rows,
        rows,
        rows,
        columns,
        P(("items", "mem")),
        columns,
        columns,
    )

    def program(*args):
        return local(mesh, *args)

    return jax.shard_map(
        program, mesh=mesh, in_specs=in_specs, out_specs=out_specs, check_vma=False
    )
```

```python
import functools

import jax
import jax.numpy as jnp
from jax import lax
from jax.experimental import pallas as pl
from jax.experimental.pallas import tpu as pltpu
from jax.sharding import PartitionSpec as P

HEAD_DIM = 64
SMALL = 16
GROUP = 4
FILL = -1e30
EPSILON = 1e-05
SCALE = 0.125
BF = jnp.bfloat16
F32 = jnp.float32


def contract(a, b, dim_a, dim_b):
    return lax.dot_general(a, b, (((dim_a,), (dim_b,)), ((), ())), preferred_element_type=F32)


def norm_parts(hidden):
    center = hidden - jnp.mean(hidden, axis=-1, keepdims=True)
    spread = lax.rsqrt(jnp.mean(center * center, axis=-1, keepdims=True) + EPSILON)
    return center * spread, spread


def norm_back(grad_out, normal, spread, gain_row):
    grad_normal = grad_out * gain_row
    grad_hidden = spread * (
        grad_normal
        - jnp.mean(grad_normal, axis=-1, keepdims=True)
        - normal * jnp.mean(grad_normal * normal, axis=-1, keepdims=True)
    )
    return grad_hidden, jnp.sum(grad_out * normal, axis=0), jnp.sum(grad_out, axis=0)


def self_fwd_heads(length, qkv_ref, out_ref, peak_ref, total_ref):
    width, steps = out_ref.shape
    key_at = lax.broadcasted_iota(jnp.int32, (steps, steps), 0)
    query_at = lax.broadcasted_iota(jnp.int32, (steps, steps), 1)
    allowed = (key_at <= query_at) & (key_at < length)
    for head in range(width // HEAD_DIM):
        rows = slice(head * HEAD_DIM, (head + 1) * HEAD_DIM)
        query = qkv_ref[rows, :] * SCALE
        key = qkv_ref[width + head * HEAD_DIM : width + (head + 1) * HEAD_DIM, :]
        value = qkv_ref[2 * width + head * HEAD_DIM : 2 * width + (head + 1) * HEAD_DIM, :]
        scores = jnp.where(allowed, contract(key, query, 0, 0), FILL)
        peak = jnp.max(scores, axis=0, keepdims=True)
        weights = jnp.exp(scores - peak)
        total = jnp.sum(weights, axis=0, keepdims=True)
        out_ref[rows, :] = (contract(value, weights.astype(BF), 1, 0) / total).astype(BF)
        peak_ref[head : head + 1, :] = peak
        total_ref[head : head + 1, :] = total


def self_fwd_kernel(
    scalar_ref,
    mine_ref,
    other_ref,
    qkv_ref,
    out_ref,
    peak_ref,
    total_ref,
    small_ref,
    column_ref,
    *,
    planes,
):
    width, steps = out_ref.shape
    devices = 2 * GROUP * planes
    height = 3 * width // devices
    lanes = width // devices
    spread = (
        lax.broadcasted_iota(jnp.int32, (steps, width), 1) % lanes
        == lax.broadcasted_iota(jnp.int32, (steps, width), 0)
    ).astype(BF)
    lane_place = lax.broadcasted_iota(jnp.int32, (SMALL, width), 1) // lanes
    small = jnp.zeros((SMALL, width), F32)
    for n, source in enumerate((mine_ref, other_ref)):
        for k in range(GROUP):
            tiled = contract(source[k, planes * height :, :], spread, 1, 0)
            for r in range(planes):
                place = scalar_ref[1 + (n * GROUP + k) * planes + r]
                at = pl.multiple_of(place * height, height)
                qkv_ref[pl.ds(at, height), :] = source[k, r * height : (r + 1) * height, :]
                mine = tiled[r * SMALL : (r + 1) * SMALL]
                small = jnp.where(lane_place == place, mine, small)
    small_ref[...] = small
    small_low = small.astype(BF)

    def column(row):
        pick = (lax.broadcasted_iota(jnp.int32, (SMALL, steps), 0) == row).astype(BF)
        return contract(small_low, pick, 0, 0)

    for at, row in ((0, 0), (2 * width, 1)):
        rows = slice(at, at + width)
        qkv_ref[rows, :] = (qkv_ref[rows, :].astype(F32) + column(row)).astype(BF)
    column_ref[0] = column(3)
    column_ref[1] = column(4)
    self_fwd_heads(scalar_ref[0], qkv_ref, out_ref, peak_ref, total_ref)


def plain_self_fwd_kernel(scalar_ref, qkv_ref, out_ref, peak_ref, total_ref):
    self_fwd_heads(scalar_ref[0], qkv_ref, out_ref, peak_ref, total_ref)


def self_bwd_heads(length, qkv_ref, out_ref, grad_ref, peak_ref, total_ref, res_ref, sum_ref):
    width, steps = out_ref.shape
    key_at = lax.broadcasted_iota(jnp.int32, (steps, steps), 0)
    query_at = lax.broadcasted_iota(jnp.int32, (steps, steps), 1)
    allowed = (key_at <= query_at) & (key_at < length)
    for head in range(width // HEAD_DIM):
        rows = slice(head * HEAD_DIM, (head + 1) * HEAD_DIM)
        key_rows = slice(width + head * HEAD_DIM, width + (head + 1) * HEAD_DIM)
        value_rows = slice(2 * width + head * HEAD_DIM, 2 * width + (head + 1) * HEAD_DIM)
        query, key, value = qkv_ref[rows, :], qkv_ref[key_rows, :], qkv_ref[value_rows, :]
        scores = jnp.where(allowed, contract(key, query * SCALE, 0, 0), FILL)
        weights = jnp.exp(scores - peak_ref[head : head + 1, :])
        inverse = 1.0 / total_ref[head : head + 1, :]
        grad = grad_ref[rows, :].astype(F32)
        scaled = (grad * inverse).astype(BF)
        delta = jnp.sum(grad * out_ref[rows, :].astype(F32), axis=0, keepdims=True) * inverse
        grad_weights = contract(value, scaled, 0, 0)
        grad_scores = (SCALE * (weights * (grad_weights - delta))).astype(BF)
        grad_query = contract(key, grad_scores, 1, 0)
        grad_value = contract(scaled, weights.astype(BF), 1, 1)
        res_ref[rows, :] = grad_query.astype(BF)
        res_ref[key_rows, :] = contract(query, grad_scores, 1, 1).astype(BF)
        res_ref[value_rows, :] = grad_value.astype(BF)
        sum_ref[rows, 0:1] = jnp.sum(grad_query, axis=1, keepdims=True)
        sum_ref[rows, 1:2] = jnp.sum(grad_value, axis=1, keepdims=True)


def self_bwd_kernel(
    scalar_ref, qkv_ref, out_ref, grad_ref, peak_ref, total_ref, send_ref, sum_ref, res_ref, *, planes
):
    self_bwd_heads(
        scalar_ref[0], qkv_ref, out_ref, grad_ref, peak_ref, total_ref, res_ref, sum_ref
    )
    height = qkv_ref.shape[0] // (2 * GROUP * planes)
    for k in range(GROUP):
        for r in range(planes):
            at = pl.multiple_of(scalar_ref[1 + k * planes + r] * height, height)
            send_ref[k, r * height : (r + 1) * height, :] = res_ref[pl.ds(at, height), :]


def plain_self_bwd_kernel(
    scalar_ref, qkv_ref, out_ref, grad_ref, peak_ref, total_ref, res_ref, sum_ref
):
    self_bwd_heads(
        scalar_ref[0], qkv_ref, out_ref, grad_ref, peak_ref, total_ref, res_ref, sum_ref
    )


def cross_fwd_kernel(len_ref, query_ref, key_ref, value_ref, out_ref, peak_ref, total_ref):
    height, steps = query_ref.shape
    span = key_ref.shape[1]
    valid = lax.broadcasted_iota(jnp.int32, (span, steps), 0) < len_ref[0]
    for head in range(height // HEAD_DIM):
        rows = slice(head * HEAD_DIM, (head + 1) * HEAD_DIM)
        scores = contract(key_ref[rows, :], query_ref[rows, :] * SCALE, 0, 0)
        scores = jnp.where(valid, scores, FILL)
        peak = jnp.max(scores, axis=0, keepdims=True)
        weights = jnp.exp(scores - peak)
        out_ref[rows, :] = contract(value_ref[rows, :], weights.astype(BF), 1, 0).astype(BF)
        peak_ref[0, head : head + 1, :] = peak
        total_ref[0, head : head + 1, :] = jnp.sum(weights, axis=0, keepdims=True)


def cross_bwd_kernel(
    scalar_ref,
    query_ref,
    kv_ref,
    out_ref,
    grad_ref,
    peak_ref,
    total_ref,
    grad_query_ref,
    grad_kv_ref,
    sum_ref,
    *block_refs,
    height,
):
    width, steps = query_ref.shape
    span = kv_ref.shape[1]
    valid = lax.broadcasted_iota(jnp.int32, (span, steps), 0) < scalar_ref[0]

    for head in range(width // HEAD_DIM):
        first = head * HEAD_DIM
        rows = slice(first, first + HEAD_DIM)
        value_rows = slice(width + first, width + first + HEAD_DIM)
        query, key, value = query_ref[rows, :], kv_ref[rows, :], kv_ref[value_rows, :]
        scores = jnp.where(valid, contract(key, query * SCALE, 0, 0), FILL)
        weights = jnp.exp(scores - peak_ref[head : head + 1, :])
        inverse = 1.0 / total_ref[head : head + 1, :]
        grad = grad_ref[rows, :].astype(F32)
        scaled = (grad * inverse).astype(BF)
        delta = jnp.sum(grad * out_ref[rows, :].astype(F32), axis=0, keepdims=True) * inverse
        grad_weights = contract(value, scaled, 0, 0)
        grad_scores = (SCALE * (weights * (grad_weights - delta))).astype(BF)
        grad_query = contract(key, grad_scores, 1, 0).astype(BF)
        grad_key = contract(query, grad_scores, 1, 1).astype(BF)
        grad_value = contract(scaled, weights.astype(BF), 1, 1)
        sum_ref[rows, :] = jnp.sum(grad_value, axis=1, keepdims=True)
        grad_value = grad_value.astype(BF)
        grad_query_ref[rows, :] = grad_query
        grad_kv_ref[rows, :] = grad_key
        grad_kv_ref[value_rows, :] = grad_value
    if not block_refs:
        return
    for ref in block_refs:
        ref[...] = jnp.zeros_like(ref)
    for core in range(2):

        @pl.when(scalar_ref[1] == core)
        def _():
            for first in range(0, 3 * width, UNIT):
                block, offset = divmod(first, height)
                to = block_refs[(block + core) % 2]
                chip = scalar_ref[2 + block // 2]
                rows = slice(offset, offset + UNIT)
                if first < width:
                    to[chip, rows, :steps] = grad_query_ref[first : first + UNIT, :]
                else:
                    from_rows = slice(first - width, first - width + UNIT)
                    to[chip, rows, steps:] = grad_kv_ref[from_rows, :]


def store_messages(parts, own_ref, first_ref, second_ref, hold_first_ref, hold_second_ref):
    half = own_ref.shape[0] // 2
    own_ref[...] = parts[0]
    first_ref[:half] = parts[1][:half]
    first_ref[half:] = parts[3][:half]
    second_ref[:half] = parts[2][half:]
    second_ref[half:] = parts[3][half:]
    hold_first_ref[...] = parts[2][:half]
    hold_second_ref[...] = parts[1][half:]


def message_shapes(rows, width):
    return [shape((n, width), BF) for n in (rows, rows, rows, rows // 2, rows // 2)]


def store_messages(parts, own_ref, first_ref, second_ref, hold_first_ref, hold_second_ref):
    half = own_ref.shape[0] // 2
    own_ref[...] = parts[0]
    first_ref[:half] = parts[1][:half]
    first_ref[half:] = parts[3][:half]
    second_ref[:half] = parts[2][half:]
    second_ref[half:] = parts[3][half:]
    hold_first_ref[...] = parts[2][:half]
    hold_second_ref[...] = parts[1][half:]


def message_shapes(rows, width):
    return [shape((n, width), BF) for n in (rows, rows, rows, rows // 2, rows // 2)]


def cross_rows_kernel(mine_ref, came_ref, normed_ref, memory_ref, other_ref, *out_refs):
    steps = normed_ref.shape[0]
    chips, height, columns = mine_ref.shape
    rows = chips // GROUP
    parts = []
    for n in range(GROUP):
        at = slice(n * rows, (n + 1) * rows)
        mine = mine_ref[at].reshape(rows * height, columns)
        came = came_ref[at].reshape(rows * height, columns)
        query = (mine[:, :steps].astype(F32) + came[:, :steps].astype(F32)).astype(BF)
        total = contract(mine[:, steps:], memory_ref[...], 1, 0)
        total += contract(came[:, steps:], other_ref[...], 1, 0)
        total += contract(query, normed_ref[...], 1, 0)
        parts.append(total.astype(BF))
    store_messages(parts, *out_refs)


def out_rows_kernel(scalar_ref, self_ref, cross_ref, one_ref, two_ref, *rest, height):
    out_refs, left_ref = rest[:-1], rest[-1]
    width, steps = self_ref.shape
    each = width // GROUP
    rows = width // height
    for n in range(rows):
        at = pl.multiple_of(scalar_ref[n] * height, height)
        is_self = at < width
        own = jnp.where(
            is_self,
            self_ref[pl.ds(pl.multiple_of(jnp.where(is_self, at, 0), height), height), :],
            cross_ref[pl.ds(pl.multiple_of(jnp.where(is_self, 0, at - width), height), height), :],
        )
        none = jnp.zeros_like(own)
        to = slice(n * height, (n + 1) * height)
        left_ref[to, :steps] = jnp.where(is_self, own, none)
        left_ref[to, steps:] = jnp.where(is_self, none, own)
    parts = []
    for n in range(GROUP):
        left = left_ref[n * each : (n + 1) * each, :]
        total = contract(left[:, :steps], one_ref[...], 1, 0)
        total += contract(left[:, steps:], two_ref[...], 1, 0)
        parts.append(total.astype(BF))
    store_messages(parts, *out_refs)


def fc_blocks(packs):
    rows = (packs[0].shape[0] - SMALL) // 2
    for n in range(0, len(packs), 2):
        pair = packs[n : n + 2]
        first = jnp.concatenate([pack[:rows, :] for pack in pair])
        second = jnp.concatenate([pack[rows : 2 * rows, :] for pack in pair])
        bias = jnp.concatenate([pack[2 * rows : 2 * rows + 1, :rows] for pack in pair], axis=1)
        yield slice(n * rows, (n + 2) * rows), first, second, bias.astype(F32)


def store_by_member(total, refs):
    rows = refs[0].shape[0]
    for n, ref in enumerate(refs):
        ref[...] = total[n * rows : (n + 1) * rows].astype(ref.dtype)


def fc_fwd_kernel(*refs):
    token_refs, packs = refs[:GROUP], refs[GROUP : -2 - GROUP]
    out_refs, (act_ref, slope_ref) = refs[-2 - GROUP : -2], refs[-2:]
    tokens = jnp.concatenate([ref[...] for ref in token_refs])
    total = jnp.zeros(tokens.shape, F32)
    for at, first, second, bias in fc_blocks(packs):
        inner = contract(tokens, first, 1, 1) + bias
        below = 0.5 * (1.0 + lax.erf(inner * 0.7071067811865476))
        density = jnp.exp(-0.5 * inner * inner) * 0.3989422804014327
        activation = (inner * below).astype(BF)
        act_ref[:, at] = activation
        slope_ref[:, at] = below + inner * density
        total += contract(activation, second, 1, 0)
    store_by_member(total, out_refs)


def fc_bwd_kernel(*refs):
    grad_refs, slope_ref, packs = refs[:GROUP], refs[GROUP], refs[GROUP + 1 : -2 - GROUP]
    out_refs, (inner_ref, bias_ref) = refs[-2 - GROUP : -2], refs[-2:]
    grads = jnp.concatenate([ref[...] for ref in grad_refs])
    total = jnp.zeros(grads.shape, F32)
    for at, first, second, _ in fc_blocks(packs):
        grad_inner = contract(grads, second, 1, 1) * slope_ref[:, at]
        bias_ref[0:1, at] = jnp.sum(grad_inner, axis=0, keepdims=True)
        grad_inner = grad_inner.astype(BF)
        inner_ref[:, at] = grad_inner
        total += contract(grad_inner, first, 1, 0)
    store_by_member(total, out_refs)


def fc_rows_kernel(place_ref, *refs):
    token_refs, grad_refs = refs[:GROUP], refs[GROUP : 2 * GROUP]
    act_ref, inner_ref, bias_ref = refs[2 * GROUP : 2 * GROUP + 3]
    outs = refs[2 * GROUP + 3 :]
    tokens = jnp.concatenate([ref[...] for ref in token_refs])
    grads = jnp.concatenate([ref[...] for ref in grad_refs])
    width = tokens.shape[1]
    rows = (outs[0].shape[1] - SMALL) // 2
    at = 0
    for out in outs:
        for r in range(0, out.shape[0], 2):
            both = slice(at, at + 2 * rows)
            first = contract(inner_ref[:, both], tokens, 0, 0).astype(BF)
            second = contract(act_ref[:, both], grads, 0, 0).astype(BF)
            for n in range(2):
                place = place_ref[r + n]
                part = slice(n * rows, (n + 1) * rows)
                out[place, :rows, :] = first[part]
                out[place, rows : 2 * rows, :] = second[part]
                bias = bias_ref[0:1, at + n * rows : at + (n + 1) * rows].astype(BF)
                bias = jnp.concatenate([bias, jnp.zeros((1, width - rows), BF)], axis=1)
                bias = jnp.concatenate([bias, jnp.zeros((SMALL - 1, width), BF)])
                out[place, 2 * rows :, :] = bias
            at += 2 * rows


SCALARS = pl.BlockSpec(memory_space=pltpu.SMEM)
WHOLE = pl.BlockSpec(memory_space=pltpu.VMEM)
PARAMS = pltpu.CompilerParams(vmem_limit_bytes=48 * 1024 * 1024)
HEADS_A_STEP = 8
UNIT = 32


def shape(dims, dtype):
    return jax.ShapeDtypeStruct(dims, dtype)


def self_fwd(length, mine, other, places, planes):
    steps = mine.shape[2]
    width = (mine.shape[1] - planes * SMALL) * 2 * GROUP // 3
    stats = [shape((width // HEAD_DIM, steps), F32)] * 2
    return pl.pallas_call(
        functools.partial(self_fwd_kernel, planes=planes),
        in_specs=[SCALARS] + [WHOLE] * 2,
        out_specs=[WHOLE] * 6,
        out_shape=[shape((3 * width, steps), BF), shape((width, steps), BF)]
        + stats
        + [shape((SMALL, width), F32), shape((2, width, steps), F32)],
        compiler_params=PARAMS,
        name="self_fwd",
    )(jnp.concatenate([length, places]), mine, other)


def plain_self_fwd(length, mine, other, places, planes, small):
    width, steps = small.shape[1], mine.shape[2]
    stats = [shape((width // HEAD_DIM, steps), F32)] * 2
    height = 3 * width // (2 * GROUP * planes)
    blocks = jnp.stack([mine, other])[:, :, : planes * height].reshape(-1, height, steps)
    qkv = jnp.zeros_like(blocks).at[places].set(blocks).reshape(3 * width, steps)
    bias = jnp.concatenate([small[0], jnp.zeros((width,), F32), small[1]])
    qkv = (qkv.astype(F32) + bias[:, None]).astype(BF)
    column = jnp.broadcast_to(small[3:5, :, None], (2, width, steps))
    results = pl.pallas_call(
        plain_self_fwd_kernel,
        in_specs=[SCALARS, WHOLE],
        out_specs=[WHOLE] * 3,
        out_shape=[shape((width, steps), BF)] + stats,
        compiler_params=PARAMS,
        name="self_fwd",
    )(length, qkv)
    return [qkv, *results, small, column]


def self_bwd(length, places, qkv, out, grad, peak, total, planes):
    width, steps = out.shape
    height = 3 * width // (2 * GROUP * planes)
    sums = shape((width, 2), F32)
    if height % 16 == 0:
        return pl.pallas_call(
            functools.partial(self_bwd_kernel, planes=planes),
            in_specs=[SCALARS] + [WHOLE] * 5,
            out_specs=[WHOLE] * 2,
            out_shape=[shape((GROUP, planes * height, steps), BF), sums],
            scratch_shapes=[pltpu.VMEM(qkv.shape, BF)],
            compiler_params=PARAMS,
            name="self_bwd",
        )(jnp.concatenate([length, places]), qkv, out, grad, peak, total)
    res, total = pl.pallas_call(
        plain_self_bwd_kernel,
        in_specs=[SCALARS] + [WHOLE] * 5,
        out_specs=[WHOLE] * 2,
        out_shape=[shape(qkv.shape, BF), sums],
        compiler_params=PARAMS,
        name="self_bwd",
    )(length, qkv, out, grad, peak, total)
    send = res.reshape(-1, height, steps)[places[: GROUP * planes]]
    return send.reshape(GROUP, planes * height, steps), total


def cross_specs(width, steps, span):
    count = width // HEAD_DIM // HEADS_A_STEP
    height = HEADS_A_STEP * HEAD_DIM
    by_step = pl.BlockSpec((height, steps), lambda i: (i, 0))
    keys = pl.BlockSpec((height, span), lambda i: (i, 0))
    values = pl.BlockSpec((height, span), lambda i: (i + count, 0))
    stats = pl.BlockSpec((1, HEADS_A_STEP, steps), lambda i: (i, 0, 0))
    column = pl.BlockSpec((height, 1), lambda i: (i, 0))
    return count, by_step, keys, values, stats, column


def cross_fwd(length, query, key_value):
    width, steps = query.shape
    count, by_step, keys, values, stats, _ = cross_specs(width, steps, key_value.shape[1])
    stat_shape = shape((count, HEADS_A_STEP, steps), F32)
    return pl.pallas_call(
        cross_fwd_kernel,
        grid=(count,),
        in_specs=[SCALARS, by_step, keys, values],
        out_specs=[by_step, stats, stats],
        out_shape=[shape((width, steps), BF), stat_shape, stat_shape],
        compiler_params=PARAMS,
        name="cross_fwd",
    )(length, query, key_value, key_value)


def cross_bwd(scalars, query, key_value, out, grad, peak, total, chips, height):
    width, steps = query.shape
    span = key_value.shape[1]
    outs = [shape((width, steps), BF), shape((2 * width, span), BF), shape((width, 1), F32)]
    if height:
        outs += [shape((chips, height, steps + span), BF)] * 2
    return pl.pallas_call(
        functools.partial(cross_bwd_kernel, height=height),
        in_specs=[SCALARS] + [WHOLE] * 6,
        out_specs=[WHOLE] * len(outs),
        out_shape=outs,
        compiler_params=PARAMS,
        name="cross_bwd",
    )(scalars, query, key_value, out, grad, peak, total)


def cross_rows(mine, came, normed, memory, other):
    chips, height, _ = mine.shape
    outs = message_shapes(chips // GROUP * height, memory.shape[1])
    return pl.pallas_call(
        cross_rows_kernel,
        in_specs=[WHOLE] * 5,
        out_specs=[WHOLE] * len(outs),
        out_shape=outs,
        compiler_params=PARAMS,
        name="cross_rows",
    )(mine, came, normed, memory, other)


def out_rows(scalars, self_out, cross_out, one, two, height):
    width, steps = self_out.shape
    outs = message_shapes(width // GROUP, width)
    return pl.pallas_call(
        functools.partial(out_rows_kernel, height=height),
        in_specs=[SCALARS] + [WHOLE] * 4,
        out_specs=[WHOLE] * len(outs),
        out_shape=outs,
        scratch_shapes=[pltpu.VMEM((width, 2 * steps), BF)],
        compiler_params=PARAMS,
        name="out_rows",
    )(scalars, self_out, cross_out, one, two)


def member_shapes(rows, width):
    return [shape((rows, width), F32)] + [shape((rows, width), BF)] * (GROUP - 1)


def fc_fwd(tokens, packs):
    rows, width = tokens[0].shape
    hidden = len(packs) * (packs[0].shape[0] - SMALL) // 2
    outs = member_shapes(rows, width)
    outs += [shape((GROUP * rows, hidden), BF), shape((GROUP * rows, hidden), F32)]
    return pl.pallas_call(
        fc_fwd_kernel,
        in_specs=[WHOLE] * (GROUP + len(packs)),
        out_specs=[WHOLE] * len(outs),
        out_shape=outs,
        compiler_params=PARAMS,
        name="fc_fwd",
    )(*tokens, *packs)


def fc_bwd(grads, packs, slope):
    rows, width = grads[0].shape
    hidden = slope.shape[1]
    outs = member_shapes(rows, width)
    outs += [shape((GROUP * rows, hidden), BF), shape((8, hidden), F32)]
    return pl.pallas_call(
        fc_bwd_kernel,
        in_specs=[WHOLE] * (GROUP + 1 + len(packs)),
        out_specs=[WHOLE] * len(outs),
        out_shape=outs,
        compiler_params=PARAMS,
        name="fc_bwd",
    )(*grads, slope, *packs)


def fc_rows(places, tokens, grads, activation, inner, bias, pack_shape):
    return pl.pallas_call(
        fc_rows_kernel,
        in_specs=[SCALARS] + [WHOLE] * (2 * GROUP + 3),
        out_specs=[WHOLE] * 2,
        out_shape=[shape(pack_shape, BF)] * 2,
        compiler_params=PARAMS,
        name="fc_rows",
    )(places, *tokens, *grads, activation, inner, bias)


def place_blocks(places, blocks, heights):
    width = blocks[0].shape[2]
    count = len(blocks) * GROUP
    starts = [sum(heights[:n]) for n in range(len(heights))]

    def kernel(place_ref, *refs):
        ins, outs = refs[: len(blocks)], refs[len(blocks) :]
        for block in range(count):
            place = place_ref[block]
            for n, (start, height) in enumerate(zip(starts, heights)):
                rows = ins[block // GROUP][block % GROUP, start : start + height, :]
                outs[n][place] = rows

    return pl.pallas_call(
        kernel,
        in_specs=[SCALARS] + [WHOLE] * len(blocks),
        out_specs=[WHOLE] * len(heights),
        out_shape=[shape((count, height, width), blocks[0].dtype) for height in heights],
        compiler_params=PARAMS,
        name="place_blocks",
    )(places, *blocks)


def local(mesh, dec_in, memory, cotangent, mem_lengths, dec_lengths, *weights):
    attn_in, cross_in, attn_out, fc_in, fc_out, biases, fc_bias, gains, shifts = weights
    chips, cores = mesh.shape["items"], mesh.shape["mem"]
    devices = chips * cores
    planes = chips // GROUP
    chip, core = lax.axis_index("items"), lax.axis_index("mem")
    plane, member = chip // GROUP, chip % GROUP

    by_plane = [list(range(k, chips, GROUP)) for k in range(GROUP)]

    def ring(a, step, name="plane"):
        pairs = [
            (i, (i // GROUP + step) % planes * GROUP + i % GROUP) for i in range(chips)
        ]
        with jax.named_scope(f"{name}_z{step}"):
            return lax.ppermute(a, "items", pairs)

    def across(a, mask, name="member"):
        with jax.named_scope(f"{name}_xy{mask}"):
            return lax.ppermute(a, "items", [(i, i ^ mask) for i in range(chips)])

    def swap(a, name="core"):
        with jax.named_scope(f"{name}_core"):
            return lax.ppermute(a, "mem", [(0, 1), (1, 0)])

    def by_core(mine, other):
        return jnp.where(core == 0, jnp.concatenate([mine, other]), jnp.concatenate([other, mine]))

    def ring_gather(a, name):
        held = [a]
        for _ in range(planes - 1):
            held.append(ring(held[-1], 1, name))
        return held

    def gather_rows(pack, heights):
        if planes != 4:
            whole = lax.all_gather(pack, ("items", "mem"), axis=0)
            starts = [sum(heights[:n]) for n in range(len(heights))]
            return [whole[:, s : s + h] for s, h in zip(starts, heights)]
        blocks, places = [], []
        for r, block in enumerate(ring_gather(pack, "rest")):
            first, second = (1, 2) if r < 2 else (2, 1)
            one = across(block, first, f"rest{r}")
            two = across(block, second, f"rest{r}")
            three = across(one, second, f"rest{r}far")
            near = jnp.stack([block, one, two, three])
            blocks += [near, swap(near, f"rest{r}")]
            source = (plane - r) % planes * GROUP
            for which in (core, 1 - core):
                places += [(source + (member ^ m)) * cores + which for m in (0, first, second, 3)]
        return place_blocks(jnp.stack(places).astype(jnp.int32), blocks, heights)

    def scatter_first(messages, name):
        _, first, second, _, _ = messages
        return across(first, 1, f"{name}_first"), across(second, 2, f"{name}_first")

    def scatter_second(messages, came, name):
        hold_first, hold_second = messages[3:]
        half = hold_first.shape[0]
        far_first = hold_first.astype(F32) + came[0][half:].astype(F32)
        far_second = hold_second.astype(F32) + came[1][half:].astype(F32)
        far_first = across(far_first.astype(BF), 2, f"{name}_second")
        return far_first, across(far_second.astype(BF), 1, f"{name}_second")

    def scatter_planes(messages, came, far):
        own = messages[0]
        half = own.shape[0] // 2
        height = own.shape[0] // planes
        sums = []
        for r in range(planes):
            which = 0 if 2 * r < planes else 1
            at = r * height % half
            rows = slice(at, at + height)
            near = own[r * height : (r + 1) * height].astype(F32)
            sums.append(near + came[which][rows].astype(F32) + far[which][rows].astype(F32))
        return sums

    def plane_sum(sums, name):
        total = sums[0]
        for r in range(1, planes):
            total = total + ring(sums[r].astype(BF), planes - r, name).astype(F32)
        return total

    def scatter_whole(part):
        return lax.psum_scatter(part, ("items", "mem"), scatter_dimension=0, tiled=True)

    def to_members(mine, name):
        return [mine] + [across(mine, mask, name) for mask in range(1, GROUP)]

    def from_members(parts, name):
        total = parts[0]
        for mask in range(1, GROUP):
            total = total + across(parts[mask], mask, name).astype(F32)
        return total

    def group_gather(mine, name):
        near = jnp.stack([mine] + [across(mine, mask, name) for mask in range(1, GROUP)])
        both = jnp.stack([near, swap(near, name)])
        return both.reshape(cores * GROUP * mine.shape[0], mine.shape[1])

    def group_sum(part, name):
        part = part.reshape(cores, GROUP, -1, part.shape[1])
        near = part[0] + swap(part[1].astype(BF), name).astype(F32)
        total = near[0]
        for mask in range(1, GROUP):
            total = total + across(near[mask].astype(BF), mask, name).astype(F32)
        return total

    width = dec_in.shape[2]
    steps = dec_in.shape[1]
    half = steps // cores
    span = memory.shape[1]
    row_attn, row_out, row_fc = attn_in.shape[0], attn_out.shape[0], fc_in.shape[0]
    small = jnp.concatenate([biases, gains, shifts])
    vectors, slice_width = small.shape

    regular = planes == 4 and row_attn % UNIT == 0 and row_out == HEAD_DIM and row_fc % 128 == 0

    def padded(a):
        return jnp.pad(a, ((0, SMALL - a.shape[0]), (0, width - a.shape[1])))

    def after(a, *others):
        return lax.optimization_barrier((a, *others))[0]

    tokens = dec_in[0]
    mem_rows = memory[0]
    came = [across(tokens, k, "tokens") for k in range(1, GROUP)]
    attn_held = [jnp.concatenate([attn_in, padded(small)])]
    for r in range(1, planes):
        held = attn_held[-1]
        if r == planes - 1:
            held = after(held, *came)
        attn_held.append(ring(held, 1, "attn"))
    group_tokens = jnp.concatenate([tokens] + came)
    w_attn = jnp.concatenate([a[:row_attn] for a in attn_held])
    projected = contract(w_attn, group_tokens, 1, 1).astype(BF)
    small_held = [a[row_attn:, :steps] for a in attn_held]
    sends = [
        jnp.concatenate([projected[:, k * steps : (k + 1) * steps]] + small_held)
        for k in range(GROUP)
    ]
    mine = jnp.stack([sends[0]] + [across(sends[k], k, "qkv") for k in range(1, GROUP)])
    other = swap(mine, "qkv")
    w_out = lax.all_gather(attn_out, ("items", "mem"), tiled=True)
    (w_cross,) = gather_rows(cross_in, [row_attn])
    w_cross = w_cross.reshape(-1, width)
    fc_held = ring_gather(jnp.concatenate([fc_in, fc_out, padded(fc_bias[None])]), "fc")
    if regular:
        fc_packs = fc_held + [swap(a, "fc") for a in fc_held]
    else:
        fc_held = jnp.stack(fc_held)
        w_fc_in = fc_held[:, :row_fc].reshape(-1, width)
        w_fc_out = fc_held[:, row_fc : 2 * row_fc].reshape(-1, width)
        fc_bias_held = fc_held[:, 2 * row_fc, :row_fc].reshape(-1).astype(F32)

    n = jnp.arange(cores * GROUP * planes)
    from_core, from_member = n // (GROUP * planes), n // planes % GROUP
    from_plane = (plane - n % planes) % planes
    places = (from_plane * GROUP + (member ^ from_member)) * cores + (core ^ from_core)
    places = places.astype(jnp.int32)

    if regular:
        fwd = self_fwd(dec_lengths, mine, other, places, planes)
    else:
        rows_small = lax.all_gather(small, ("items", "mem"), axis=1, tiled=True).astype(F32)
        fwd = plain_self_fwd(dec_lengths, mine, other, places, planes, rows_small)
    qkv, self_out, self_peak, self_total, rows_small, columns = fwd
    bias, gain, shift = (
        [rows_small[n : n + 1] for n in span] for span in (range(7), range(7, 10), range(10, 13))
    )
    hidden_one = tokens.astype(F32) + contract(self_out, w_out[:width], 0, 0) + bias[2]
    normal_one, spread_one = norm_parts(hidden_one)
    normed_one = normal_one * gain[0] + shift[0]
    normed_one_low = normed_one.astype(BF)
    cross_query = (contract(w_cross[:width], normed_one_low, 1, 1) + columns[0]).astype(BF)
    cross_kv = contract(w_cross[width:], mem_rows, 1, 1).astype(BF)
    mem_left = mem_lengths - core * span
    part_out, part_peak, part_total = cross_fwd(mem_left, cross_query, cross_kv)
    other_out = swap(part_out, "cross_out")
    other_stats = swap(jnp.stack([part_peak, part_total]), "stats")
    other_peak, other_total = other_stats[0], other_stats[1]
    cross_peak = jnp.maximum(part_peak, other_peak)
    mine_factor = jnp.exp(part_peak - cross_peak)
    other_factor = jnp.exp(other_peak - cross_peak)
    cross_total = mine_factor * part_total + other_factor * other_total
    heads = width // HEAD_DIM

    def per_head(stat):
        return stat.reshape(heads, 1, steps)

    cross_out = (
        per_head(mine_factor / cross_total) * part_out.reshape(heads, HEAD_DIM, steps).astype(F32)
        + per_head(other_factor / cross_total)
        * other_out.reshape(heads, HEAD_DIM, steps).astype(F32)
    )
    cross_plain = cross_out.reshape(width, steps)
    cross_out = (cross_plain + columns[1]).astype(BF)
    cross_plain = cross_plain.astype(BF)

    def own(rows):
        return lax.dynamic_slice_in_dim(rows, core * half, half)

    hidden_two = own(normed_one + contract(cross_out, w_out[width:], 0, 0)) + bias[5]
    normal_two, spread_two = norm_parts(hidden_two)
    normed_two = normal_two * gain[1] + shift[1]
    if regular:
        member_two = to_members(normed_two.astype(BF), "normed_two")
        *parts, activation, slope = fc_fwd(member_two, fc_packs)
        fc_result = from_members(parts, "three")
    else:
        group_two = group_gather(normed_two.astype(BF), "normed_two")
        inner = contract(group_two, w_fc_in, 1, 1) + fc_bias_held
        activation = jax.nn.gelu(inner, approximate=False).astype(BF)
        fc_result = group_sum(contract(activation, w_fc_out, 1, 0), "three")
    hidden_three = normed_two + fc_result + bias[6]
    normal_three, spread_three = norm_parts(hidden_three)
    out_own = (normal_three * gain[2] + shift[2]).astype(BF)
    output = by_core(out_own, swap(out_own, "output"))[None]
    mem_other = swap(after(mem_rows, out_own), "memory")

    grad_three, grad_gain_three, grad_shift_three = norm_back(
        own(cotangent[0]).astype(F32), normal_three, spread_three, gain[2]
    )
    if regular:
        member_three = to_members(grad_three.astype(BF), "grad_three")
        *parts, grad_inner, grad_fc_bias = fc_bwd(member_three, fc_packs, slope)
        grad_normed_two = grad_three + from_members(parts, "grad_two")
    else:
        group_three = group_gather(grad_three.astype(BF), "grad_three")
        grad_activation = contract(group_three, w_fc_out, 1, 1)
        density = jnp.exp(-0.5 * inner * inner) * 0.3989422804014327
        below = 0.5 * (1.0 + lax.erf(inner * 0.7071067811865476))
        grad_inner = grad_activation * (below + inner * density)
        grad_inner_low = grad_inner.astype(BF)
        grad_normed_two = grad_three + group_sum(
            contract(grad_inner_low, w_fc_in, 1, 0), "grad_two"
        )
        fc_part = jnp.concatenate(
            [
                contract(grad_inner_low, group_two, 0, 0).reshape(planes, row_fc, width),
                contract(activation, group_three, 0, 0).reshape(planes, row_fc, width),
                jnp.pad(
                    jnp.sum(grad_inner, axis=0).reshape(planes, 1, row_fc),
                    ((0, 0), (0, SMALL - 1), (0, width - row_fc)),
                ),
            ],
            axis=1,
        )
        fc_part = jnp.concatenate(
            [
                lax.dynamic_slice_in_dim(fc_part, (plane - at) % planes, 1)
                for at in range(planes)
            ]
        ).astype(BF)
    grad_two, grad_gain_two, grad_shift_two = norm_back(
        grad_normed_two, normal_two, spread_two, gain[1]
    )

    grad_two_low = grad_two.astype(BF)
    if regular:
        plane_places = ((plane - jnp.arange(planes)) % planes).astype(jnp.int32)
        fc_mine, fc_other = fc_rows(
            plane_places,
            member_two,
            member_three,
            activation,
            after(grad_inner, grad_two_low),
            grad_fc_bias,
            (planes, *fc_held[0].shape),
        )
        fc_part = (fc_mine.astype(F32) + swap(fc_other, "fc_grad").astype(F32)).astype(BF)
    fc_sum = lax.psum_scatter(
        fc_part, "items", scatter_dimension=0, axis_index_groups=by_plane
    ).astype(F32)
    sum_fc_in, sum_fc_out = fc_sum[:row_fc], fc_sum[row_fc : 2 * row_fc]
    sum_fc_bias = fc_sum[2 * row_fc, :row_fc]
    grad_two_all = by_core(grad_two_low, swap(grad_two_low, "grad_two"))
    grad_cross = contract(w_out[width:], grad_two_all, 1, 1).astype(BF)
    chip_at = jnp.arange(chips)
    far = ((chip_at % GROUP) ^ member) * planes + (plane - chip_at // GROUP) % planes
    scalars = jnp.concatenate([mem_left, core.reshape(1), far]).astype(jnp.int32)
    grad_query, grad_kv, grad_value_sum, *blocks = cross_bwd(
        scalars,
        cross_query,
        cross_kv,
        cross_plain,
        grad_cross,
        cross_peak.reshape(heads, steps),
        cross_total.reshape(heads, steps),
        chips,
        row_attn if regular else 0,
    )
    if regular:
        came_blocks = swap(blocks[1], "cross_blocks")
        cross_parts = cross_rows(blocks[0], came_blocks, normed_one_low, mem_rows, mem_other)
    grad_query_all = grad_query.astype(F32) + swap(grad_query, "grad_query").astype(F32)
    grad_query_low = after(grad_query_all.astype(BF), fc_part)
    grad_one, grad_gain_one, grad_shift_one = norm_back(
        grad_two + own(contract(grad_query_low, w_cross[:width], 0, 0)),
        own(normal_one),
        own(spread_one),
        gain[0],
    )
    grad_one_low = grad_one.astype(BF)
    grad_one_all = by_core(grad_one_low, swap(grad_one_low, "grad_one"))
    if regular:
        grad_one_all = after(grad_one_all, cross_parts[0])
    grad_self = contract(w_out[:width], grad_one_all, 1, 1).astype(BF)
    grad_sends, grad_qv_sum = self_bwd(
        dec_lengths, places, qkv, self_out, grad_self, self_peak, self_total, planes
    )


    def of_core(a, which):
        return lax.dynamic_index_in_dim(a, which, 1, keepdims=False)

    if regular:
        came_cross = scatter_first(cross_parts, "cross_grad")
        far_cross = scatter_second(cross_parts, came_cross, "cross_grad")
        cross_sums = scatter_planes(cross_parts, came_cross, far_cross)
        cross_sums = lax.optimization_barrier((*cross_sums, fc_sum))[:planes]
        sum_cross = plane_sum(cross_sums, "cross_grad")
        out_places = places[: GROUP * planes]
        out_parts = out_rows(
            out_places, self_out, cross_out, grad_one_all, grad_two_all, row_out
        )
        out_parts = lax.optimization_barrier((*out_parts, *came_cross))[: len(out_parts)]
        came_out = scatter_first(out_parts, "out_grad")
        far_out = scatter_second(out_parts, came_out, "out_grad")
        out_sums = scatter_planes(out_parts, came_out, far_out)
        sum_out = plane_sum(out_sums, "out_grad")
    else:
        sum_cross = scatter_whole(
            jnp.concatenate(
                [contract(grad_query, normed_one_low, 1, 0), contract(grad_kv, mem_rows, 1, 0)]
            )
        )
        part_out = [
            contract(self_out, grad_one_all, 1, 0),
            contract(cross_out, grad_two_all, 1, 0),
        ]
        sum_out = scatter_whole(jnp.concatenate(part_out) / cores)

    grad_held = jnp.concatenate(
        [grad_sends[0]] + [across(grad_sends[k], k, "grad_qkv") for k in range(1, GROUP)], axis=1
    )
    part_attn = contract(grad_held, group_tokens, 1, 0)
    grad_memory = contract(after(grad_kv, part_attn), w_cross[width:], 0, 0).astype(BF)[None]
    if regular:
        part_attn = after(part_attn, *far_cross)
    sum_attn = part_attn[:row_attn]
    for r in range(1, planes):
        rows = slice(r * row_attn, (r + 1) * row_attn)
        sum_attn = sum_attn + ring(part_attn[rows].astype(BF), planes - r, "attn_grad").astype(F32)
    part_tokens = contract(grad_held, w_attn, 0, 0).reshape(GROUP, cores, half, width)
    part_tokens = jnp.stack([of_core(part_tokens, core), of_core(part_tokens, 1 - core)])
    part_tokens = part_tokens[0] + swap(part_tokens[1].astype(BF), "grad_dec").astype(F32)
    came = across(jnp.concatenate([part_tokens[1], part_tokens[3]]).astype(BF), 1, "grad_dec")
    far = across((part_tokens[2] + came[half:].astype(F32)).astype(BF), 2, "grad_dec")
    grad_tokens = grad_one + part_tokens[0] + came[:half].astype(F32) + far.astype(F32)
    grad_tokens_low = grad_tokens.astype(BF)
    grad_dec_in = by_core(grad_tokens_low, swap(grad_tokens_low, "grad_dec"))[None]

    part_vectors = jnp.stack(
        [
            grad_qv_sum[:, 0] / cores,
            grad_qv_sum[:, 1] / cores,
            jnp.sum(grad_one, axis=0),
            jnp.sum(grad_query.astype(F32), axis=1),
            grad_value_sum[:, 0],
            jnp.sum(grad_two, axis=0),
            jnp.sum(grad_three, axis=0),
            grad_gain_one,
            grad_gain_two,
            grad_gain_three,
            grad_shift_one,
            grad_shift_two,
            grad_shift_three,
        ]
    )
    part_vectors = jnp.transpose(part_vectors.reshape(vectors, devices, slice_width), (1, 0, 2))
    came = lax.all_to_all(
        after(part_vectors.reshape(devices, vectors * slice_width), part_attn),
        ("items", "mem"),
        split_axis=0,
        concat_axis=0,
        tiled=True,
    )
    sum_vectors = jnp.sum(came, axis=0).reshape(vectors, slice_width)
    return (
        output,
        grad_dec_in,
        grad_memory,
        sum_attn,
        sum_cross,
        sum_out,
        sum_fc_in,
        sum_fc_out,
        sum_vectors[:7],
        sum_fc_bias,
        sum_vectors[7:10],
        sum_vectors[10:vectors],
    )


def solution(mesh):
    rows = P(("items", "mem"), None)
    columns = P(None, ("items", "mem"))
    item = P("items", None, None)
    in_specs = (
        item,
        P("items", "mem", None),
        item,
        P("items"),
        P("items"),
        rows,
        rows,
        rows,
        rows,
        rows,
        columns,
        P(("items", "mem")),
        columns,
        columns,
    )
    out_specs = (
        item,
        item,
        P("items", "mem", None),
        rows,
        rows,
        rows,
        rows,
        rows,
        columns,
        P(("items", "mem")),
        columns,
        columns,
    )

    def program(*args):
        return local(mesh, *args)

    return jax.shard_map(
        program, mesh=mesh, in_specs=in_specs, out_specs=out_specs, check_vma=False
    )
```

```python
import functools

import jax
import jax.numpy as jnp
from jax import lax
from jax.experimental import pallas as pl
from jax.experimental.pallas import tpu as pltpu
from jax.sharding import PartitionSpec as P

HEAD_DIM = 64
SMALL = 16
GROUP = 4
FILL = -1e30
EPSILON = 1e-05
SCALE = 0.125
BF = jnp.bfloat16
F32 = jnp.float32


def contract(a, b, dim_a, dim_b):
    return lax.dot_general(a, b, (((dim_a,), (dim_b,)), ((), ())), preferred_element_type=F32)


def norm_parts(hidden):
    center = hidden - jnp.mean(hidden, axis=-1, keepdims=True)
    spread = lax.rsqrt(jnp.mean(center * center, axis=-1, keepdims=True) + EPSILON)
    return center * spread, spread


def norm_back(grad_out, normal, spread, gain_row):
    grad_normal = grad_out * gain_row
    grad_hidden = spread * (
        grad_normal
        - jnp.mean(grad_normal, axis=-1, keepdims=True)
        - normal * jnp.mean(grad_normal * normal, axis=-1, keepdims=True)
    )
    return grad_hidden, jnp.sum(grad_out * normal, axis=0), jnp.sum(grad_out, axis=0)


def self_fwd_heads(length, qkv_ref, out_ref, peak_ref, total_ref):
    width, steps = out_ref.shape
    key_at = lax.broadcasted_iota(jnp.int32, (steps, steps), 0)
    query_at = lax.broadcasted_iota(jnp.int32, (steps, steps), 1)
    allowed = (key_at <= query_at) & (key_at < length)
    for head in range(width // HEAD_DIM):
        rows = slice(head * HEAD_DIM, (head + 1) * HEAD_DIM)
        query = qkv_ref[rows, :] * SCALE
        key = qkv_ref[width + head * HEAD_DIM : width + (head + 1) * HEAD_DIM, :]
        value = qkv_ref[2 * width + head * HEAD_DIM : 2 * width + (head + 1) * HEAD_DIM, :]
        scores = jnp.where(allowed, contract(key, query, 0, 0), FILL)
        peak = jnp.max(scores, axis=0, keepdims=True)
        weights = jnp.exp(scores - peak)
        total = jnp.sum(weights, axis=0, keepdims=True)
        out_ref[rows, :] = (contract(value, weights.astype(BF), 1, 0) / total).astype(BF)
        peak_ref[head : head + 1, :] = peak
        total_ref[head : head + 1, :] = total


def self_fwd_kernel(
    scalar_ref,
    mine_ref,
    other_ref,
    qkv_ref,
    out_ref,
    peak_ref,
    total_ref,
    small_ref,
    column_ref,
    *,
    planes,
):
    width, steps = out_ref.shape
    devices = 2 * GROUP * planes
    height = 3 * width // devices
    lanes = width // devices
    spread = (
        lax.broadcasted_iota(jnp.int32, (steps, width), 1) % lanes
        == lax.broadcasted_iota(jnp.int32, (steps, width), 0)
    ).astype(BF)
    lane_place = lax.broadcasted_iota(jnp.int32, (SMALL, width), 1) // lanes
    small = jnp.zeros((SMALL, width), F32)
    for n, source in enumerate((mine_ref, other_ref)):
        for k in range(GROUP):
            tiled = contract(source[k, planes * height :, :], spread, 1, 0)
            for r in range(planes):
                place = scalar_ref[1 + (n * GROUP + k) * planes + r]
                at = pl.multiple_of(place * height, height)
                qkv_ref[pl.ds(at, height), :] = source[k, r * height : (r + 1) * height, :]
                mine = tiled[r * SMALL : (r + 1) * SMALL]
                small = jnp.where(lane_place == place, mine, small)
    small_ref[...] = small
    small_low = small.astype(BF)

    def column(row):
        pick = (lax.broadcasted_iota(jnp.int32, (SMALL, steps), 0) == row).astype(BF)
        return contract(small_low, pick, 0, 0)

    for at, row in ((0, 0), (2 * width, 1)):
        rows = slice(at, at + width)
        qkv_ref[rows, :] = (qkv_ref[rows, :].astype(F32) + column(row)).astype(BF)
    column_ref[0] = column(3)
    column_ref[1] = column(4)
    self_fwd_heads(scalar_ref[0], qkv_ref, out_ref, peak_ref, total_ref)


def plain_self_fwd_kernel(scalar_ref, qkv_ref, out_ref, peak_ref, total_ref):
    self_fwd_heads(scalar_ref[0], qkv_ref, out_ref, peak_ref, total_ref)


def self_bwd_heads(length, qkv_ref, out_ref, grad_ref, peak_ref, total_ref, res_ref, sum_ref):
    width, steps = out_ref.shape
    key_at = lax.broadcasted_iota(jnp.int32, (steps, steps), 0)
    query_at = lax.broadcasted_iota(jnp.int32, (steps, steps), 1)
    allowed = (key_at <= query_at) & (key_at < length)
    for head in range(width // HEAD_DIM):
        rows = slice(head * HEAD_DIM, (head + 1) * HEAD_DIM)
        key_rows = slice(width + head * HEAD_DIM, width + (head + 1) * HEAD_DIM)
        value_rows = slice(2 * width + head * HEAD_DIM, 2 * width + (head + 1) * HEAD_DIM)
        query, key, value = qkv_ref[rows, :], qkv_ref[key_rows, :], qkv_ref[value_rows, :]
        scores = jnp.where(allowed, contract(key, query * SCALE, 0, 0), FILL)
        weights = jnp.exp(scores - peak_ref[head : head + 1, :])
        inverse = 1.0 / total_ref[head : head + 1, :]
        grad = grad_ref[rows, :].astype(F32)
        scaled = (grad * inverse).astype(BF)
        delta = jnp.sum(grad * out_ref[rows, :].astype(F32), axis=0, keepdims=True) * inverse
        grad_weights = contract(value, scaled, 0, 0)
        grad_scores = (SCALE * (weights * (grad_weights - delta))).astype(BF)
        grad_query = contract(key, grad_scores, 1, 0)
        grad_value = contract(scaled, weights.astype(BF), 1, 1)
        res_ref[rows, :] = grad_query.astype(BF)
        res_ref[key_rows, :] = contract(query, grad_scores, 1, 1).astype(BF)
        res_ref[value_rows, :] = grad_value.astype(BF)
        sum_ref[rows, 0:1] = jnp.sum(grad_query, axis=1, keepdims=True)
        sum_ref[rows, 1:2] = jnp.sum(grad_value, axis=1, keepdims=True)


def self_bwd_kernel(
    scalar_ref, qkv_ref, out_ref, grad_ref, peak_ref, total_ref, send_ref, sum_ref, res_ref, *, planes
):
    self_bwd_heads(
        scalar_ref[0], qkv_ref, out_ref, grad_ref, peak_ref, total_ref, res_ref, sum_ref
    )
    height = qkv_ref.shape[0] // (2 * GROUP * planes)
    for k in range(GROUP):
        for r in range(planes):
            at = pl.multiple_of(scalar_ref[1 + k * planes + r] * height, height)
            send_ref[k, r * height : (r + 1) * height, :] = res_ref[pl.ds(at, height), :]


def plain_self_bwd_kernel(
    scalar_ref, qkv_ref, out_ref, grad_ref, peak_ref, total_ref, res_ref, sum_ref
):
    self_bwd_heads(
        scalar_ref[0], qkv_ref, out_ref, grad_ref, peak_ref, total_ref, res_ref, sum_ref
    )


def cross_fwd_kernel(len_ref, query_ref, key_ref, value_ref, out_ref, peak_ref, total_ref):
    height, steps = query_ref.shape
    span = key_ref.shape[1]
    valid = lax.broadcasted_iota(jnp.int32, (span, steps), 0) < len_ref[0]
    for head in range(height // HEAD_DIM):
        rows = slice(head * HEAD_DIM, (head + 1) * HEAD_DIM)
        scores = contract(key_ref[rows, :], query_ref[rows, :] * SCALE, 0, 0)
        scores = jnp.where(valid, scores, FILL)
        peak = jnp.max(scores, axis=0, keepdims=True)
        weights = jnp.exp(scores - peak)
        out_ref[rows, :] = contract(value_ref[rows, :], weights.astype(BF), 1, 0).astype(BF)
        peak_ref[0, head : head + 1, :] = peak
        total_ref[0, head : head + 1, :] = jnp.sum(weights, axis=0, keepdims=True)


def cross_bwd_kernel(
    scalar_ref,
    query_ref,
    kv_ref,
    out_ref,
    grad_ref,
    peak_ref,
    total_ref,
    grad_query_ref,
    grad_kv_ref,
    sum_ref,
    *block_refs,
    height,
):
    width, steps = query_ref.shape
    span = kv_ref.shape[1]
    valid = lax.broadcasted_iota(jnp.int32, (span, steps), 0) < scalar_ref[0]

    for head in range(width // HEAD_DIM):
        first = head * HEAD_DIM
        rows = slice(first, first + HEAD_DIM)
        value_rows = slice(width + first, width + first + HEAD_DIM)
        query, key, value = query_ref[rows, :], kv_ref[rows, :], kv_ref[value_rows, :]
        scores = jnp.where(valid, contract(key, query * SCALE, 0, 0), FILL)
        weights = jnp.exp(scores - peak_ref[head : head + 1, :])
        inverse = 1.0 / total_ref[head : head + 1, :]
        grad = grad_ref[rows, :].astype(F32)
        scaled = (grad * inverse).astype(BF)
        delta = jnp.sum(grad * out_ref[rows, :].astype(F32), axis=0, keepdims=True) * inverse
        grad_weights = contract(value, scaled, 0, 0)
        grad_scores = (SCALE * (weights * (grad_weights - delta))).astype(BF)
        grad_query = contract(key, grad_scores, 1, 0).astype(BF)
        grad_key = contract(query, grad_scores, 1, 1).astype(BF)
        grad_value = contract(scaled, weights.astype(BF), 1, 1)
        sum_ref[rows, :] = jnp.sum(grad_value, axis=1, keepdims=True)
        grad_value = grad_value.astype(BF)
        grad_query_ref[rows, :] = grad_query
        grad_kv_ref[rows, :] = grad_key
        grad_kv_ref[value_rows, :] = grad_value
    if not block_refs:
        return
    for core in range(2):

        @pl.when(scalar_ref[1] == core)
        def _():
            for first in range(0, 3 * width, UNIT):
                block, offset = divmod(first, height)
                to = block_refs[(block + core) % 2]
                chip = scalar_ref[2 + block // 2]
                rows = slice(offset, offset + UNIT)
                if first < width:
                    to[chip, rows, :steps] = grad_query_ref[first : first + UNIT, :]
                    to[chip, rows, steps:] = jnp.zeros((UNIT, span), BF)
                else:
                    from_rows = slice(first - width, first - width + UNIT)
                    to[chip, rows, :steps] = jnp.zeros((UNIT, steps), BF)
                    to[chip, rows, steps:] = grad_kv_ref[from_rows, :]


def store_messages(parts, own_ref, first_ref, second_ref, hold_first_ref, hold_second_ref):
    half = own_ref.shape[0] // 2
    own_ref[...] = parts[0]
    first_ref[:half] = parts[1][:half]
    first_ref[half:] = parts[3][:half]
    second_ref[:half] = parts[2][half:]
    second_ref[half:] = parts[3][half:]
    hold_first_ref[...] = parts[2][:half]
    hold_second_ref[...] = parts[1][half:]


def message_shapes(rows, width):
    return [shape((n, width), BF) for n in (rows, rows, rows, rows // 2, rows // 2)]


def store_messages(parts, own_ref, first_ref, second_ref, hold_first_ref, hold_second_ref):
    half = own_ref.shape[0] // 2
    own_ref[...] = parts[0]
    first_ref[:half] = parts[1][:half]
    first_ref[half:] = parts[3][:half]
    second_ref[:half] = parts[2][half:]
    second_ref[half:] = parts[3][half:]
    hold_first_ref[...] = parts[2][:half]
    hold_second_ref[...] = parts[1][half:]


def message_shapes(rows, width):
    return [shape((n, width), BF) for n in (rows, rows, rows, rows // 2, rows // 2)]


def cross_rows_kernel(mine_ref, came_ref, normed_ref, memory_ref, other_ref, *out_refs):
    steps = normed_ref.shape[0]
    chips, height, columns = mine_ref.shape
    rows = chips // GROUP
    parts = []
    for n in range(GROUP):
        at = slice(n * rows, (n + 1) * rows)
        mine = mine_ref[at].reshape(rows * height, columns)
        came = came_ref[at].reshape(rows * height, columns)
        query = (mine[:, :steps].astype(F32) + came[:, :steps].astype(F32)).astype(BF)
        total = contract(mine[:, steps:], memory_ref[...], 1, 0)
        total += contract(came[:, steps:], other_ref[...], 1, 0)
        total += contract(query, normed_ref[...], 1, 0)
        parts.append(total.astype(BF))
    store_messages(parts, *out_refs)


def out_rows_kernel(scalar_ref, self_ref, cross_ref, one_ref, two_ref, *rest, height):
    out_refs, left_ref = rest[:-1], rest[-1]
    width, steps = self_ref.shape
    each = width // GROUP
    rows = width // height
    for n in range(rows):
        at = pl.multiple_of(scalar_ref[n] * height, height)
        is_self = at < width
        own = jnp.where(
            is_self,
            self_ref[pl.ds(pl.multiple_of(jnp.where(is_self, at, 0), height), height), :],
            cross_ref[pl.ds(pl.multiple_of(jnp.where(is_self, 0, at - width), height), height), :],
        )
        none = jnp.zeros_like(own)
        to = slice(n * height, (n + 1) * height)
        left_ref[to, :steps] = jnp.where(is_self, own, none)
        left_ref[to, steps:] = jnp.where(is_self, none, own)
    parts = []
    for n in range(GROUP):
        left = left_ref[n * each : (n + 1) * each, :]
        total = contract(left[:, :steps], one_ref[...], 1, 0)
        total += contract(left[:, steps:], two_ref[...], 1, 0)
        parts.append(total.astype(BF))
    store_messages(parts, *out_refs)


def fc_blocks(packs):
    rows = (packs[0].shape[0] - SMALL) // 2
    for n in range(0, len(packs), 2):
        pair = packs[n : n + 2]
        first = jnp.concatenate([pack[:rows, :] for pack in pair])
        second = jnp.concatenate([pack[rows : 2 * rows, :] for pack in pair])
        bias = jnp.concatenate([pack[2 * rows : 2 * rows + 1, :rows] for pack in pair], axis=1)
        yield slice(n * rows, (n + 2) * rows), first, second, bias.astype(F32)


def store_by_member(total, refs):
    rows = refs[0].shape[0]
    for n, ref in enumerate(refs):
        ref[...] = total[n * rows : (n + 1) * rows].astype(ref.dtype)


def fc_fwd_kernel(*refs):
    token_refs, packs = refs[:GROUP], refs[GROUP : -2 - GROUP]
    out_refs, (act_ref, slope_ref) = refs[-2 - GROUP : -2], refs[-2:]
    tokens = jnp.concatenate([ref[...] for ref in token_refs])
    total = jnp.zeros(tokens.shape, F32)
    for at, first, second, bias in fc_blocks(packs):
        inner = contract(tokens, first, 1, 1) + bias
        below = 0.5 * (1.0 + lax.erf(inner * 0.7071067811865476))
        density = jnp.exp(-0.5 * inner * inner) * 0.3989422804014327
        activation = (inner * below).astype(BF)
        act_ref[:, at] = activation
        slope_ref[:, at] = below + inner * density
        total += contract(activation, second, 1, 0)
    store_by_member(total, out_refs)


def fc_bwd_kernel(*refs):
    grad_refs, slope_ref, packs = refs[:GROUP], refs[GROUP], refs[GROUP + 1 : -2 - GROUP]
    out_refs, (inner_ref, bias_ref) = refs[-2 - GROUP : -2], refs[-2:]
    grads = jnp.concatenate([ref[...] for ref in grad_refs])
    total = jnp.zeros(grads.shape, F32)
    for at, first, second, _ in fc_blocks(packs):
        grad_inner = contract(grads, second, 1, 1) * slope_ref[:, at]
        bias_ref[0:1, at] = jnp.sum(grad_inner, axis=0, keepdims=True)
        grad_inner = grad_inner.astype(BF)
        inner_ref[:, at] = grad_inner
        total += contract(grad_inner, first, 1, 0)
    store_by_member(total, out_refs)


def fc_rows_kernel(place_ref, *refs):
    token_refs, grad_refs = refs[:GROUP], refs[GROUP : 2 * GROUP]
    act_ref, inner_ref, bias_ref = refs[2 * GROUP : 2 * GROUP + 3]
    outs = refs[2 * GROUP + 3 :]
    tokens = jnp.concatenate([ref[...] for ref in token_refs])
    grads = jnp.concatenate([ref[...] for ref in grad_refs])
    width = tokens.shape[1]
    rows = (outs[0].shape[1] - SMALL) // 2
    at = 0
    for out in outs:
        for r in range(0, out.shape[0], 2):
            both = slice(at, at + 2 * rows)
            first = contract(inner_ref[:, both], tokens, 0, 0).astype(BF)
            second = contract(act_ref[:, both], grads, 0, 0).astype(BF)
            for n in range(2):
                place = place_ref[r + n]
                part = slice(n * rows, (n + 1) * rows)
                out[place, :rows, :] = first[part]
                out[place, rows : 2 * rows, :] = second[part]
                bias = bias_ref[0:1, at + n * rows : at + (n + 1) * rows].astype(BF)
                bias = jnp.concatenate([bias, jnp.zeros((1, width - rows), BF)], axis=1)
                bias = jnp.concatenate([bias, jnp.zeros((SMALL - 1, width), BF)])
                out[place, 2 * rows :, :] = bias
            at += 2 * rows


SCALARS = pl.BlockSpec(memory_space=pltpu.SMEM)
WHOLE = pl.BlockSpec(memory_space=pltpu.VMEM)
PARAMS = pltpu.CompilerParams(vmem_limit_bytes=48 * 1024 * 1024)
HEADS_A_STEP = 8
UNIT = 32


def shape(dims, dtype):
    return jax.ShapeDtypeStruct(dims, dtype)


def self_fwd(length, mine, other, places, planes):
    steps = mine.shape[2]
    width = (mine.shape[1] - planes * SMALL) * 2 * GROUP // 3
    stats = [shape((width // HEAD_DIM, steps), F32)] * 2
    return pl.pallas_call(
        functools.partial(self_fwd_kernel, planes=planes),
        in_specs=[SCALARS] + [WHOLE] * 2,
        out_specs=[WHOLE] * 6,
        out_shape=[shape((3 * width, steps), BF), shape((width, steps), BF)]
        + stats
        + [shape((SMALL, width), F32), shape((2, width, steps), F32)],
        compiler_params=PARAMS,
        name="self_fwd",
    )(jnp.concatenate([length, places]), mine, other)


def plain_self_fwd(length, mine, other, places, planes, small):
    width, steps = small.shape[1], mine.shape[2]
    stats = [shape((width // HEAD_DIM, steps), F32)] * 2
    height = 3 * width // (2 * GROUP * planes)
    blocks = jnp.stack([mine, other])[:, :, : planes * height].reshape(-1, height, steps)
    qkv = jnp.zeros_like(blocks).at[places].set(blocks).reshape(3 * width, steps)
    bias = jnp.concatenate([small[0], jnp.zeros((width,), F32), small[1]])
    qkv = (qkv.astype(F32) + bias[:, None]).astype(BF)
    column = jnp.broadcast_to(small[3:5, :, None], (2, width, steps))
    results = pl.pallas_call(
        plain_self_fwd_kernel,
        in_specs=[SCALARS, WHOLE],
        out_specs=[WHOLE] * 3,
        out_shape=[shape((width, steps), BF)] + stats,
        compiler_params=PARAMS,
        name="self_fwd",
    )(length, qkv)
    return [qkv, *results, small, column]


def self_bwd(length, places, qkv, out, grad, peak, total, planes):
    width, steps = out.shape
    height = 3 * width // (2 * GROUP * planes)
    sums = shape((width, 2), F32)
    if height % 16 == 0:
        return pl.pallas_call(
            functools.partial(self_bwd_kernel, planes=planes),
            in_specs=[SCALARS] + [WHOLE] * 5,
            out_specs=[WHOLE] * 2,
            out_shape=[shape((GROUP, planes * height, steps), BF), sums],
            scratch_shapes=[pltpu.VMEM(qkv.shape, BF)],
            compiler_params=PARAMS,
            name="self_bwd",
        )(jnp.concatenate([length, places]), qkv, out, grad, peak, total)
    res, total = pl.pallas_call(
        plain_self_bwd_kernel,
        in_specs=[SCALARS] + [WHOLE] * 5,
        out_specs=[WHOLE] * 2,
        out_shape=[shape(qkv.shape, BF), sums],
        compiler_params=PARAMS,
        name="self_bwd",
    )(length, qkv, out, grad, peak, total)
    send = res.reshape(-1, height, steps)[places[: GROUP * planes]]
    return send.reshape(GROUP, planes * height, steps), total


def cross_specs(width, steps, span):
    count = width // HEAD_DIM // HEADS_A_STEP
    height = HEADS_A_STEP * HEAD_DIM
    by_step = pl.BlockSpec((height, steps), lambda i: (i, 0))
    keys = pl.BlockSpec((height, span), lambda i: (i, 0))
    values = pl.BlockSpec((height, span), lambda i: (i + count, 0))
    stats = pl.BlockSpec((1, HEADS_A_STEP, steps), lambda i: (i, 0, 0))
    column = pl.BlockSpec((height, 1), lambda i: (i, 0))
    return count, by_step, keys, values, stats, column


def cross_fwd(length, query, key_value):
    width, steps = query.shape
    count, by_step, keys, values, stats, _ = cross_specs(width, steps, key_value.shape[1])
    stat_shape = shape((count, HEADS_A_STEP, steps), F32)
    return pl.pallas_call(
        cross_fwd_kernel,
        grid=(count,),
        in_specs=[SCALARS, by_step, keys, values],
        out_specs=[by_step, stats, stats],
        out_shape=[shape((width, steps), BF), stat_shape, stat_shape],
        compiler_params=PARAMS,
        name="cross_fwd",
    )(length, query, key_value, key_value)


def cross_bwd(scalars, query, key_value, out, grad, peak, total, chips, height):
    width, steps = query.shape
    span = key_value.shape[1]
    outs = [shape((width, steps), BF), shape((2 * width, span), BF), shape((width, 1), F32)]
    if height:
        outs += [shape((chips, height, steps + span), BF)] * 2
    return pl.pallas_call(
        functools.partial(cross_bwd_kernel, height=height),
        in_specs=[SCALARS] + [WHOLE] * 6,
        out_specs=[WHOLE] * len(outs),
        out_shape=outs,
        compiler_params=PARAMS,
        name="cross_bwd",
    )(scalars, query, key_value, out, grad, peak, total)


def cross_rows(mine, came, normed, memory, other):
    chips, height, _ = mine.shape
    outs = message_shapes(chips // GROUP * height, memory.shape[1])
    return pl.pallas_call(
        cross_rows_kernel,
        in_specs=[WHOLE] * 5,
        out_specs=[WHOLE] * len(outs),
        out_shape=outs,
        compiler_params=PARAMS,
        name="cross_rows",
    )(mine, came, normed, memory, other)


def out_rows(scalars, self_out, cross_out, one, two, height):
    width, steps = self_out.shape
    outs = message_shapes(width // GROUP, width)
    return pl.pallas_call(
        functools.partial(out_rows_kernel, height=height),
        in_specs=[SCALARS] + [WHOLE] * 4,
        out_specs=[WHOLE] * len(outs),
        out_shape=outs,
        scratch_shapes=[pltpu.VMEM((width, 2 * steps), BF)],
        compiler_params=PARAMS,
        name="out_rows",
    )(scalars, self_out, cross_out, one, two)


def member_shapes(rows, width):
    return [shape((rows, width), F32)] + [shape((rows, width), BF)] * (GROUP - 1)


def fc_fwd(tokens, packs):
    rows, width = tokens[0].shape
    hidden = len(packs) * (packs[0].shape[0] - SMALL) // 2
    outs = member_shapes(rows, width)
    outs += [shape((GROUP * rows, hidden), BF), shape((GROUP * rows, hidden), F32)]
    return pl.pallas_call(
        fc_fwd_kernel,
        in_specs=[WHOLE] * (GROUP + len(packs)),
        out_specs=[WHOLE] * len(outs),
        out_shape=outs,
        compiler_params=PARAMS,
        name="fc_fwd",
    )(*tokens, *packs)


def fc_bwd(grads, packs, slope):
    rows, width = grads[0].shape
    hidden = slope.shape[1]
    outs = member_shapes(rows, width)
    outs += [shape((GROUP * rows, hidden), BF), shape((8, hidden), F32)]
    return pl.pallas_call(
        fc_bwd_kernel,
        in_specs=[WHOLE] * (GROUP + 1 + len(packs)),
        out_specs=[WHOLE] * len(outs),
        out_shape=outs,
        compiler_params=PARAMS,
        name="fc_bwd",
    )(*grads, slope, *packs)


def fc_rows(places, tokens, grads, activation, inner, bias, pack_shape):
    return pl.pallas_call(
        fc_rows_kernel,
        in_specs=[SCALARS] + [WHOLE] * (2 * GROUP + 3),
        out_specs=[WHOLE] * 2,
        out_shape=[shape(pack_shape, BF)] * 2,
        compiler_params=PARAMS,
        name="fc_rows",
    )(places, *tokens, *grads, activation, inner, bias)


def place_blocks(places, blocks, heights):
    width = blocks[0].shape[2]
    count = len(blocks) * GROUP
    starts = [sum(heights[:n]) for n in range(len(heights))]

    def kernel(place_ref, *refs):
        ins, outs = refs[: len(blocks)], refs[len(blocks) :]
        for block in range(count):
            place = place_ref[block]
            for n, (start, height) in enumerate(zip(starts, heights)):
                rows = ins[block // GROUP][block % GROUP, start : start + height, :]
                outs[n][place] = rows

    return pl.pallas_call(
        kernel,
        in_specs=[SCALARS] + [WHOLE] * len(blocks),
        out_specs=[WHOLE] * len(heights),
        out_shape=[shape((count, height, width), blocks[0].dtype) for height in heights],
        compiler_params=PARAMS,
        name="place_blocks",
    )(places, *blocks)


def local(mesh, dec_in, memory, cotangent, mem_lengths, dec_lengths, *weights):
    attn_in, cross_in, attn_out, fc_in, fc_out, biases, fc_bias, gains, shifts = weights
    chips, cores = mesh.shape["items"], mesh.shape["mem"]
    devices = chips * cores
    planes = chips // GROUP
    chip, core = lax.axis_index("items"), lax.axis_index("mem")
    plane, member = chip // GROUP, chip % GROUP

    by_plane = [list(range(k, chips, GROUP)) for k in range(GROUP)]

    def ring(a, step, name="plane"):
        pairs = [
            (i, (i // GROUP + step) % planes * GROUP + i % GROUP) for i in range(chips)
        ]
        with jax.named_scope(f"{name}_z{step}"):
            return lax.ppermute(a, "items", pairs)

    def across(a, mask, name="member"):
        with jax.named_scope(f"{name}_xy{mask}"):
            return lax.ppermute(a, "items", [(i, i ^ mask) for i in range(chips)])

    def swap(a, name="core"):
        with jax.named_scope(f"{name}_core"):
            return lax.ppermute(a, "mem", [(0, 1), (1, 0)])

    def by_core(mine, other):
        return jnp.where(core == 0, jnp.concatenate([mine, other]), jnp.concatenate([other, mine]))

    def ring_gather(a, name):
        held = [a]
        for _ in range(planes - 1):
            held.append(ring(held[-1], 1, name))
        return held

    def gather_rows(pack, heights):
        if planes != 4:
            whole = lax.all_gather(pack, ("items", "mem"), axis=0)
            starts = [sum(heights[:n]) for n in range(len(heights))]
            return [whole[:, s : s + h] for s, h in zip(starts, heights)]
        blocks, places = [], []
        for r, block in enumerate(ring_gather(pack, "rest")):
            first, second = (1, 2) if r < 2 else (2, 1)
            one = across(block, first, f"rest{r}")
            two = across(block, second, f"rest{r}")
            three = across(one, second, f"rest{r}far")
            near = jnp.stack([block, one, two, three])
            blocks += [near, swap(near, f"rest{r}")]
            source = (plane - r) % planes * GROUP
            for which in (core, 1 - core):
                places += [(source + (member ^ m)) * cores + which for m in (0, first, second, 3)]
        return place_blocks(jnp.stack(places).astype(jnp.int32), blocks, heights)

    def scatter_first(messages, name):
        _, first, second, _, _ = messages
        return across(first, 1, f"{name}_first"), across(second, 2, f"{name}_first")

    def scatter_second(messages, came, name):
        hold_first, hold_second = messages[3:]
        half = hold_first.shape[0]
        far_first = hold_first.astype(F32) + came[0][half:].astype(F32)
        far_second = hold_second.astype(F32) + came[1][half:].astype(F32)
        far_first = across(far_first.astype(BF), 2, f"{name}_second")
        return far_first, across(far_second.astype(BF), 1, f"{name}_second")

    def scatter_planes(messages, came, far):
        own = messages[0]
        half = own.shape[0] // 2
        height = own.shape[0] // planes
        sums = []
        for r in range(planes):
            which = 0 if 2 * r < planes else 1
            at = r * height % half
            rows = slice(at, at + height)
            near = own[r * height : (r + 1) * height].astype(F32)
            sums.append(near + came[which][rows].astype(F32) + far[which][rows].astype(F32))
        return sums

    def plane_sum(sums, name):
        total = sums[0]
        for r in range(1, planes):
            total = total + ring(sums[r].astype(BF), planes - r, name).astype(F32)
        return total

    def scatter_whole(part):
        return lax.psum_scatter(part, ("items", "mem"), scatter_dimension=0, tiled=True)

    def to_members(mine, name):
        return [mine] + [across(mine, mask, name) for mask in range(1, GROUP)]

    def from_members(parts, name):
        total = parts[0]
        for mask in range(1, GROUP):
            total = total + across(parts[mask], mask, name).astype(F32)
        return total

    def group_gather(mine, name):
        near = jnp.stack([mine] + [across(mine, mask, name) for mask in range(1, GROUP)])
        both = jnp.stack([near, swap(near, name)])
        return both.reshape(cores * GROUP * mine.shape[0], mine.shape[1])

    def group_sum(part, name):
        part = part.reshape(cores, GROUP, -1, part.shape[1])
        near = part[0] + swap(part[1].astype(BF), name).astype(F32)
        total = near[0]
        for mask in range(1, GROUP):
            total = total + across(near[mask].astype(BF), mask, name).astype(F32)
        return total

    width = dec_in.shape[2]
    steps = dec_in.shape[1]
    half = steps // cores
    span = memory.shape[1]
    row_attn, row_out, row_fc = attn_in.shape[0], attn_out.shape[0], fc_in.shape[0]
    small = jnp.concatenate([biases, gains, shifts])
    vectors, slice_width = small.shape

    regular = planes == 4 and row_attn % UNIT == 0 and row_out == HEAD_DIM and row_fc % 128 == 0

    def padded(a):
        return jnp.pad(a, ((0, SMALL - a.shape[0]), (0, width - a.shape[1])))

    def after(a, *others):
        return lax.optimization_barrier((a, *others))[0]

    tokens = dec_in[0]
    mem_rows = memory[0]
    came = [across(tokens, k, "tokens") for k in range(1, GROUP)]
    attn_held = [jnp.concatenate([attn_in, padded(small)])]
    for r in range(1, planes):
        held = attn_held[-1]
        if r == planes - 1:
            held = after(held, *came)
        attn_held.append(ring(held, 1, "attn"))
    group_tokens = jnp.concatenate([tokens] + came)
    w_attn = jnp.concatenate([a[:row_attn] for a in attn_held])
    projected = contract(w_attn, group_tokens, 1, 1).astype(BF)
    small_held = [a[row_attn:, :steps] for a in attn_held]
    sends = [
        jnp.concatenate([projected[:, k * steps : (k + 1) * steps]] + small_held)
        for k in range(GROUP)
    ]
    mine = jnp.stack([sends[0]] + [across(sends[k], k, "qkv") for k in range(1, GROUP)])
    other = swap(mine, "qkv")
    w_out = lax.all_gather(attn_out, ("items", "mem"), tiled=True)
    (w_cross,) = gather_rows(cross_in, [row_attn])
    w_cross = w_cross.reshape(-1, width)
    fc_held = ring_gather(jnp.concatenate([fc_in, fc_out, padded(fc_bias[None])]), "fc")
    if regular:
        fc_packs = fc_held + [swap(a, "fc") for a in fc_held]
    else:
        fc_held = jnp.stack(fc_held)
        w_fc_in = fc_held[:, :row_fc].reshape(-1, width)
        w_fc_out = fc_held[:, row_fc : 2 * row_fc].reshape(-1, width)
        fc_bias_held = fc_held[:, 2 * row_fc, :row_fc].reshape(-1).astype(F32)

    n = jnp.arange(cores * GROUP * planes)
    from_core, from_member = n // (GROUP * planes), n // planes % GROUP
    from_plane = (plane - n % planes) % planes
    places = (from_plane * GROUP + (member ^ from_member)) * cores + (core ^ from_core)
    places = places.astype(jnp.int32)

    if regular:
        fwd = self_fwd(dec_lengths, mine, other, places, planes)
    else:
        rows_small = lax.all_gather(small, ("items", "mem"), axis=1, tiled=True).astype(F32)
        fwd = plain_self_fwd(dec_lengths, mine, other, places, planes, rows_small)
    qkv, self_out, self_peak, self_total, rows_small, columns = fwd
    bias, gain, shift = (
        [rows_small[n : n + 1] for n in span] for span in (range(7), range(7, 10), range(10, 13))
    )
    hidden_one = tokens.astype(F32) + contract(self_out, w_out[:width], 0, 0) + bias[2]
    normal_one, spread_one = norm_parts(hidden_one)
    normed_one = normal_one * gain[0] + shift[0]
    normed_one_low = normed_one.astype(BF)
    cross_query = (contract(w_cross[:width], normed_one_low, 1, 1) + columns[0]).astype(BF)
    cross_kv = contract(w_cross[width:], mem_rows, 1, 1).astype(BF)
    mem_left = mem_lengths - core * span
    part_out, part_peak, part_total = cross_fwd(mem_left, cross_query, cross_kv)
    other_out = swap(part_out, "cross_out")
    other_stats = swap(jnp.stack([part_peak, part_total]), "stats")
    other_peak, other_total = other_stats[0], other_stats[1]
    cross_peak = jnp.maximum(part_peak, other_peak)
    mine_factor = jnp.exp(part_peak - cross_peak)
    other_factor = jnp.exp(other_peak - cross_peak)
    cross_total = mine_factor * part_total + other_factor * other_total
    heads = width // HEAD_DIM

    def per_head(stat):
        return stat.reshape(heads, 1, steps)

    cross_out = (
        per_head(mine_factor / cross_total) * part_out.reshape(heads, HEAD_DIM, steps).astype(F32)
        + per_head(other_factor / cross_total)
        * other_out.reshape(heads, HEAD_DIM, steps).astype(F32)
    )
    cross_plain = cross_out.reshape(width, steps)
    cross_out = (cross_plain + columns[1]).astype(BF)
    cross_plain = cross_plain.astype(BF)

    def own(rows):
        return lax.dynamic_slice_in_dim(rows, core * half, half)

    hidden_two = own(normed_one + contract(cross_out, w_out[width:], 0, 0)) + bias[5]
    normal_two, spread_two = norm_parts(hidden_two)
    normed_two = normal_two * gain[1] + shift[1]
    if regular:
        member_two = to_members(normed_two.astype(BF), "normed_two")
        *parts, activation, slope = fc_fwd(member_two, fc_packs)
        fc_result = from_members(parts, "three")
    else:
        group_two = group_gather(normed_two.astype(BF), "normed_two")
        inner = contract(group_two, w_fc_in, 1, 1) + fc_bias_held
        activation = jax.nn.gelu(inner, approximate=False).astype(BF)
        fc_result = group_sum(contract(activation, w_fc_out, 1, 0), "three")
    hidden_three = normed_two + fc_result + bias[6]
    normal_three, spread_three = norm_parts(hidden_three)
    out_own = (normal_three * gain[2] + shift[2]).astype(BF)
    output = by_core(out_own, swap(out_own, "output"))[None]
    mem_other = swap(after(mem_rows, out_own), "memory")

    grad_three, grad_gain_three, grad_shift_three = norm_back(
        own(cotangent[0]).astype(F32), normal_three, spread_three, gain[2]
    )
    if regular:
        member_three = to_members(grad_three.astype(BF), "grad_three")
        *parts, grad_inner, grad_fc_bias = fc_bwd(member_three, fc_packs, slope)
        grad_normed_two = grad_three + from_members(parts, "grad_two")
    else:
        group_three = group_gather(grad_three.astype(BF), "grad_three")
        grad_activation = contract(group_three, w_fc_out, 1, 1)
        density = jnp.exp(-0.5 * inner * inner) * 0.3989422804014327
        below = 0.5 * (1.0 + lax.erf(inner * 0.7071067811865476))
        grad_inner = grad_activation * (below + inner * density)
        grad_inner_low = grad_inner.astype(BF)
        grad_normed_two = grad_three + group_sum(
            contract(grad_inner_low, w_fc_in, 1, 0), "grad_two"
        )
        fc_part = jnp.concatenate(
            [
                contract(grad_inner_low, group_two, 0, 0).reshape(planes, row_fc, width),
                contract(activation, group_three, 0, 0).reshape(planes, row_fc, width),
                jnp.pad(
                    jnp.sum(grad_inner, axis=0).reshape(planes, 1, row_fc),
                    ((0, 0), (0, SMALL - 1), (0, width - row_fc)),
                ),
            ],
            axis=1,
        )
        fc_part = jnp.concatenate(
            [
                lax.dynamic_slice_in_dim(fc_part, (plane - at) % planes, 1)
                for at in range(planes)
            ]
        ).astype(BF)
    grad_two, grad_gain_two, grad_shift_two = norm_back(
        grad_normed_two, normal_two, spread_two, gain[1]
    )

    grad_two_low = grad_two.astype(BF)
    if regular:
        plane_places = ((plane - jnp.arange(planes)) % planes).astype(jnp.int32)
        fc_mine, fc_other = fc_rows(
            plane_places,
            member_two,
            member_three,
            activation,
            after(grad_inner, grad_two_low),
            grad_fc_bias,
            (planes, *fc_held[0].shape),
        )
        fc_part = (fc_mine.astype(F32) + swap(fc_other, "fc_grad").astype(F32)).astype(BF)
    fc_sum = lax.psum_scatter(
        fc_part, "items", scatter_dimension=0, axis_index_groups=by_plane
    ).astype(F32)
    sum_fc_in, sum_fc_out = fc_sum[:row_fc], fc_sum[row_fc : 2 * row_fc]
    sum_fc_bias = fc_sum[2 * row_fc, :row_fc]
    grad_two_all = by_core(grad_two_low, swap(grad_two_low, "grad_two"))
    grad_cross = contract(w_out[width:], grad_two_all, 1, 1).astype(BF)
    chip_at = jnp.arange(chips)
    far = ((chip_at % GROUP) ^ member) * planes + (plane - chip_at // GROUP) % planes
    scalars = jnp.concatenate([mem_left, core.reshape(1), far]).astype(jnp.int32)
    grad_query, grad_kv, grad_value_sum, *blocks = cross_bwd(
        scalars,
        cross_query,
        cross_kv,
        cross_plain,
        grad_cross,
        cross_peak.reshape(heads, steps),
        cross_total.reshape(heads, steps),
        chips,
        row_attn if regular else 0,
    )
    if regular:
        came_blocks = swap(blocks[1], "cross_blocks")
        cross_parts = cross_rows(blocks[0], came_blocks, normed_one_low, mem_rows, mem_other)
    grad_query_all = grad_query.astype(F32) + swap(grad_query, "grad_query").astype(F32)
    grad_query_low = after(grad_query_all.astype(BF), fc_part)
    grad_one, grad_gain_one, grad_shift_one = norm_back(
        grad_two + own(contract(grad_query_low, w_cross[:width], 0, 0)),
        own(normal_one),
        own(spread_one),
        gain[0],
    )
    grad_one_low = grad_one.astype(BF)
    grad_one_all = by_core(grad_one_low, swap(grad_one_low, "grad_one"))
    if regular:
        grad_one_all = after(grad_one_all, cross_parts[0])
    grad_self = contract(w_out[:width], grad_one_all, 1, 1).astype(BF)
    grad_sends, grad_qv_sum = self_bwd(
        dec_lengths, places, qkv, self_out, grad_self, self_peak, self_total, planes
    )


    def of_core(a, which):
        return lax.dynamic_index_in_dim(a, which, 1, keepdims=False)

    if regular:
        came_cross = scatter_first(cross_parts, "cross_grad")
        far_cross = scatter_second(cross_parts, came_cross, "cross_grad")
        cross_sums = scatter_planes(cross_parts, came_cross, far_cross)
        out_places = places[: GROUP * planes]
        out_parts = out_rows(
            out_places, self_out, cross_out, grad_one_all, grad_two_all, row_out
        )
        out_parts = lax.optimization_barrier((*out_parts, *came_cross))[: len(out_parts)]
        came_out = scatter_first(out_parts, "out_grad")
        far_out = scatter_second(out_parts, came_out, "out_grad")
        out_sums = scatter_planes(out_parts, came_out, far_out)
        sum_out = plane_sum(out_sums, "out_grad")
    else:
        sum_cross = scatter_whole(
            jnp.concatenate(
                [contract(grad_query, normed_one_low, 1, 0), contract(grad_kv, mem_rows, 1, 0)]
            )
        )
        part_out = [
            contract(self_out, grad_one_all, 1, 0),
            contract(cross_out, grad_two_all, 1, 0),
        ]
        sum_out = scatter_whole(jnp.concatenate(part_out) / cores)

    grad_held = jnp.concatenate(
        [grad_sends[0]] + [across(grad_sends[k], k, "grad_qkv") for k in range(1, GROUP)], axis=1
    )
    part_attn = contract(grad_held, group_tokens, 1, 0)
    grad_memory = contract(after(grad_kv, part_attn), w_cross[width:], 0, 0).astype(BF)[None]
    if regular:
        part_attn = after(part_attn, *far_cross)
    sum_attn = part_attn[:row_attn]
    for r in range(1, planes):
        rows = slice(r * row_attn, (r + 1) * row_attn)
        sum_attn = sum_attn + ring(part_attn[rows].astype(BF), planes - r, "attn_grad").astype(F32)
    if regular:
        cross_sums = lax.optimization_barrier((*cross_sums, sum_attn))[:planes]
        sum_cross = plane_sum(cross_sums, "cross_grad")
    part_tokens = contract(grad_held, w_attn, 0, 0).reshape(GROUP, cores, half, width)
    part_tokens = jnp.stack([of_core(part_tokens, core), of_core(part_tokens, 1 - core)])
    part_tokens = part_tokens[0] + swap(part_tokens[1].astype(BF), "grad_dec").astype(F32)
    came = across(jnp.concatenate([part_tokens[1], part_tokens[3]]).astype(BF), 1, "grad_dec")
    far = across((part_tokens[2] + came[half:].astype(F32)).astype(BF), 2, "grad_dec")
    grad_tokens = grad_one + part_tokens[0] + came[:half].astype(F32) + far.astype(F32)
    grad_tokens_low = grad_tokens.astype(BF)
    grad_dec_in = by_core(grad_tokens_low, swap(grad_tokens_low, "grad_dec"))[None]

    part_vectors = jnp.stack(
        [
            grad_qv_sum[:, 0] / cores,
            grad_qv_sum[:, 1] / cores,
            jnp.sum(grad_one, axis=0),
            jnp.sum(grad_query.astype(F32), axis=1),
            grad_value_sum[:, 0],
            jnp.sum(grad_two, axis=0),
            jnp.sum(grad_three, axis=0),
            grad_gain_one,
            grad_gain_two,
            grad_gain_three,
            grad_shift_one,
            grad_shift_two,
            grad_shift_three,
        ]
    )
    part_vectors = jnp.transpose(part_vectors.reshape(vectors, devices, slice_width), (1, 0, 2))
    late = far_out if regular else (part_attn,)
    came = lax.all_to_all(
        after(part_vectors.reshape(devices, vectors * slice_width), *late),
        ("items", "mem"),
        split_axis=0,
        concat_axis=0,
        tiled=True,
    )
    sum_vectors = jnp.sum(came, axis=0).reshape(vectors, slice_width)
    return (
        output,
        grad_dec_in,
        grad_memory,
        sum_attn,
        sum_cross,
        sum_out,
        sum_fc_in,
        sum_fc_out,
        sum_vectors[:7],
        sum_fc_bias,
        sum_vectors[7:10],
        sum_vectors[10:vectors],
    )


def solution(mesh):
    rows = P(("items", "mem"), None)
    columns = P(None, ("items", "mem"))
    item = P("items", None, None)
    in_specs = (
        item,
        P("items", "mem", None),
        item,
        P("items"),
        P("items"),
        rows,
        rows,
        rows,
        rows,
        rows,
        columns,
        P(("items", "mem")),
        columns,
        columns,
    )
    out_specs = (
        item,
        item,
        P("items", "mem", None),
        rows,
        rows,
        rows,
        rows,
        rows,
        columns,
        P(("items", "mem")),
        columns,
        columns,
    )

    def program(*args):
        return local(mesh, *args)

    return jax.shard_map(
        program, mesh=mesh, in_specs=in_specs, out_specs=out_specs, check_vma=False
    )
```

```python
import functools

import jax
import jax.numpy as jnp
from jax import lax
from jax.experimental import pallas as pl
from jax.experimental.pallas import tpu as pltpu
from jax.sharding import PartitionSpec as P

HEAD_DIM = 64
SMALL = 16
GROUP = 4
FILL = -1e30
EPSILON = 1e-05
SCALE = 0.125
BF = jnp.bfloat16
F32 = jnp.float32


def contract(a, b, dim_a, dim_b):
    return lax.dot_general(a, b, (((dim_a,), (dim_b,)), ((), ())), preferred_element_type=F32)


def norm_parts(hidden):
    center = hidden - jnp.mean(hidden, axis=-1, keepdims=True)
    spread = lax.rsqrt(jnp.mean(center * center, axis=-1, keepdims=True) + EPSILON)
    return center * spread, spread


def norm_back(grad_out, normal, spread, gain_row):
    grad_normal = grad_out * gain_row
    grad_hidden = spread * (
        grad_normal
        - jnp.mean(grad_normal, axis=-1, keepdims=True)
        - normal * jnp.mean(grad_normal * normal, axis=-1, keepdims=True)
    )
    return grad_hidden, jnp.sum(grad_out * normal, axis=0), jnp.sum(grad_out, axis=0)


def self_fwd_heads(length, qkv_ref, out_ref, peak_ref, total_ref):
    width, steps = out_ref.shape
    key_at = lax.broadcasted_iota(jnp.int32, (steps, steps), 0)
    query_at = lax.broadcasted_iota(jnp.int32, (steps, steps), 1)
    allowed = (key_at <= query_at) & (key_at < length)
    for head in range(width // HEAD_DIM):
        rows = slice(head * HEAD_DIM, (head + 1) * HEAD_DIM)
        query = qkv_ref[rows, :] * SCALE
        key = qkv_ref[width + head * HEAD_DIM : width + (head + 1) * HEAD_DIM, :]
        value = qkv_ref[2 * width + head * HEAD_DIM : 2 * width + (head + 1) * HEAD_DIM, :]
        scores = jnp.where(allowed, contract(key, query, 0, 0), FILL)
        peak = jnp.max(scores, axis=0, keepdims=True)
        weights = jnp.exp(scores - peak)
        total = jnp.sum(weights, axis=0, keepdims=True)
        out_ref[rows, :] = (contract(value, weights.astype(BF), 1, 0) / total).astype(BF)
        peak_ref[head : head + 1, :] = peak
        total_ref[head : head + 1, :] = total


def self_fwd_kernel(
    scalar_ref,
    mine_ref,
    other_ref,
    qkv_ref,
    out_ref,
    peak_ref,
    total_ref,
    small_ref,
    column_ref,
    *,
    planes,
):
    width, steps = out_ref.shape
    devices = 2 * GROUP * planes
    height = 3 * width // devices
    lanes = width // devices
    spread = (
        lax.broadcasted_iota(jnp.int32, (steps, width), 1) % lanes
        == lax.broadcasted_iota(jnp.int32, (steps, width), 0)
    ).astype(BF)
    lane_place = lax.broadcasted_iota(jnp.int32, (SMALL, width), 1) // lanes
    small = jnp.zeros((SMALL, width), F32)
    for n, source in enumerate((mine_ref, other_ref)):
        for k in range(GROUP):
            tiled = contract(source[k, planes * height :, :], spread, 1, 0)
            for r in range(planes):
                place = scalar_ref[1 + (n * GROUP + k) * planes + r]
                at = pl.multiple_of(place * height, height)
                qkv_ref[pl.ds(at, height), :] = source[k, r * height : (r + 1) * height, :]
                mine = tiled[r * SMALL : (r + 1) * SMALL]
                small = jnp.where(lane_place == place, mine, small)
    small_ref[...] = small
    small_low = small.astype(BF)

    def column(row):
        pick = (lax.broadcasted_iota(jnp.int32, (SMALL, steps), 0) == row).astype(BF)
        return contract(small_low, pick, 0, 0)

    for at, row in ((0, 0), (2 * width, 1)):
        rows = slice(at, at + width)
        qkv_ref[rows, :] = (qkv_ref[rows, :].astype(F32) + column(row)).astype(BF)
    column_ref[0] = column(3)
    column_ref[1] = column(4)
    self_fwd_heads(scalar_ref[0], qkv_ref, out_ref, peak_ref, total_ref)


def plain_self_fwd_kernel(scalar_ref, qkv_ref, out_ref, peak_ref, total_ref):
    self_fwd_heads(scalar_ref[0], qkv_ref, out_ref, peak_ref, total_ref)


def self_bwd_heads(length, qkv_ref, out_ref, grad_ref, peak_ref, total_ref, res_ref, sum_ref):
    width, steps = out_ref.shape
    key_at = lax.broadcasted_iota(jnp.int32, (steps, steps), 0)
    query_at = lax.broadcasted_iota(jnp.int32, (steps, steps), 1)
    allowed = (key_at <= query_at) & (key_at < length)
    for head in range(width // HEAD_DIM):
        rows = slice(head * HEAD_DIM, (head + 1) * HEAD_DIM)
        key_rows = slice(width + head * HEAD_DIM, width + (head + 1) * HEAD_DIM)
        value_rows = slice(2 * width + head * HEAD_DIM, 2 * width + (head + 1) * HEAD_DIM)
        query, key, value = qkv_ref[rows, :], qkv_ref[key_rows, :], qkv_ref[value_rows, :]
        scores = jnp.where(allowed, contract(key, query * SCALE, 0, 0), FILL)
        weights = jnp.exp(scores - peak_ref[head : head + 1, :])
        inverse = 1.0 / total_ref[head : head + 1, :]
        grad = grad_ref[rows, :].astype(F32)
        scaled = (grad * inverse).astype(BF)
        delta = jnp.sum(grad * out_ref[rows, :].astype(F32), axis=0, keepdims=True) * inverse
        grad_weights = contract(value, scaled, 0, 0)
        grad_scores = (SCALE * (weights * (grad_weights - delta))).astype(BF)
        grad_query = contract(key, grad_scores, 1, 0)
        grad_value = contract(scaled, weights.astype(BF), 1, 1)
        res_ref[rows, :] = grad_query.astype(BF)
        res_ref[key_rows, :] = contract(query, grad_scores, 1, 1).astype(BF)
        res_ref[value_rows, :] = grad_value.astype(BF)
        sum_ref[rows, 0:1] = jnp.sum(grad_query, axis=1, keepdims=True)
        sum_ref[rows, 1:2] = jnp.sum(grad_value, axis=1, keepdims=True)


def self_bwd_kernel(
    scalar_ref, qkv_ref, out_ref, grad_ref, peak_ref, total_ref, send_ref, sum_ref, res_ref, *, planes
):
    self_bwd_heads(
        scalar_ref[0], qkv_ref, out_ref, grad_ref, peak_ref, total_ref, res_ref, sum_ref
    )
    height = qkv_ref.shape[0] // (2 * GROUP * planes)
    for k in range(GROUP):
        for r in range(planes):
            at = pl.multiple_of(scalar_ref[1 + k * planes + r] * height, height)
            send_ref[k, r * height : (r + 1) * height, :] = res_ref[pl.ds(at, height), :]


def plain_self_bwd_kernel(
    scalar_ref, qkv_ref, out_ref, grad_ref, peak_ref, total_ref, res_ref, sum_ref
):
    self_bwd_heads(
        scalar_ref[0], qkv_ref, out_ref, grad_ref, peak_ref, total_ref, res_ref, sum_ref
    )


def cross_fwd_kernel(len_ref, query_ref, key_ref, value_ref, out_ref, peak_ref, total_ref):
    height, steps = query_ref.shape
    span = key_ref.shape[1]
    valid = lax.broadcasted_iota(jnp.int32, (span, steps), 0) < len_ref[0]
    for head in range(height // HEAD_DIM):
        rows = slice(head * HEAD_DIM, (head + 1) * HEAD_DIM)
        scores = contract(key_ref[rows, :], query_ref[rows, :] * SCALE, 0, 0)
        scores = jnp.where(valid, scores, FILL)
        peak = jnp.max(scores, axis=0, keepdims=True)
        weights = jnp.exp(scores - peak)
        out_ref[rows, :] = contract(value_ref[rows, :], weights.astype(BF), 1, 0).astype(BF)
        peak_ref[0, head : head + 1, :] = peak
        total_ref[0, head : head + 1, :] = jnp.sum(weights, axis=0, keepdims=True)


def cross_bwd_kernel(
    scalar_ref,
    query_ref,
    kv_ref,
    out_ref,
    grad_ref,
    peak_ref,
    total_ref,
    grad_query_ref,
    grad_kv_ref,
    sum_ref,
    *block_refs,
    height,
):
    width, steps = query_ref.shape
    span = kv_ref.shape[1]
    valid = lax.broadcasted_iota(jnp.int32, (span, steps), 0) < scalar_ref[0]

    for head in range(width // HEAD_DIM):
        first = head * HEAD_DIM
        rows = slice(first, first + HEAD_DIM)
        value_rows = slice(width + first, width + first + HEAD_DIM)
        query, key, value = query_ref[rows, :], kv_ref[rows, :], kv_ref[value_rows, :]
        scores = jnp.where(valid, contract(key, query * SCALE, 0, 0), FILL)
        weights = jnp.exp(scores - peak_ref[head : head + 1, :])
        inverse = 1.0 / total_ref[head : head + 1, :]
        grad = grad_ref[rows, :].astype(F32)
        scaled = (grad * inverse).astype(BF)
        delta = jnp.sum(grad * out_ref[rows, :].astype(F32), axis=0, keepdims=True) * inverse
        grad_weights = contract(value, scaled, 0, 0)
        grad_scores = (SCALE * (weights * (grad_weights - delta))).astype(BF)
        grad_query = contract(key, grad_scores, 1, 0).astype(BF)
        grad_key = contract(query, grad_scores, 1, 1).astype(BF)
        grad_value = contract(scaled, weights.astype(BF), 1, 1)
        sum_ref[rows, :] = jnp.sum(grad_value, axis=1, keepdims=True)
        grad_value = grad_value.astype(BF)
        grad_query_ref[rows, :] = grad_query
        grad_kv_ref[rows, :] = grad_key
        grad_kv_ref[value_rows, :] = grad_value
    if not block_refs:
        return
    for core in range(2):

        @pl.when(scalar_ref[1] == core)
        def _():
            for first in range(0, 3 * width, UNIT):
                block, offset = divmod(first, height)
                to = block_refs[(block + core) % 2]
                chip = scalar_ref[2 + block // 2]
                rows = slice(offset, offset + UNIT)
                if first < width:
                    to[chip, rows, :steps] = grad_query_ref[first : first + UNIT, :]
                    to[chip, rows, steps:] = jnp.zeros((UNIT, span), BF)
                else:
                    from_rows = slice(first - width, first - width + UNIT)
                    to[chip, rows, :steps] = jnp.zeros((UNIT, steps), BF)
                    to[chip, rows, steps:] = grad_kv_ref[from_rows, :]


def store_messages(parts, own_ref, first_ref, second_ref, hold_first_ref, hold_second_ref):
    half = own_ref.shape[0] // 2
    own_ref[...] = parts[0]
    first_ref[:half] = parts[1][:half]
    first_ref[half:] = parts[3][:half]
    second_ref[:half] = parts[2][half:]
    second_ref[half:] = parts[3][half:]
    hold_first_ref[...] = parts[2][:half]
    hold_second_ref[...] = parts[1][half:]


def message_shapes(rows, width):
    return [shape((n, width), BF) for n in (rows, rows, rows, rows // 2, rows // 2)]


def store_messages(parts, own_ref, first_ref, second_ref, hold_first_ref, hold_second_ref):
    half = own_ref.shape[0] // 2
    own_ref[...] = parts[0]
    first_ref[:half] = parts[1][:half]
    first_ref[half:] = parts[3][:half]
    second_ref[:half] = parts[2][half:]
    second_ref[half:] = parts[3][half:]
    hold_first_ref[...] = parts[2][:half]
    hold_second_ref[...] = parts[1][half:]


def message_shapes(rows, width):
    return [shape((n, width), BF) for n in (rows, rows, rows, rows // 2, rows // 2)]


def cross_rows_kernel(mine_ref, came_ref, normed_ref, memory_ref, other_ref, *out_refs):
    steps = normed_ref.shape[0]
    chips, height, columns = mine_ref.shape
    rows = chips // GROUP
    parts = []
    for n in range(GROUP):
        at = slice(n * rows, (n + 1) * rows)
        mine = mine_ref[at].reshape(rows * height, columns)
        came = came_ref[at].reshape(rows * height, columns)
        query = (mine[:, :steps].astype(F32) + came[:, :steps].astype(F32)).astype(BF)
        total = contract(mine[:, steps:], memory_ref[...], 1, 0)
        total += contract(came[:, steps:], other_ref[...], 1, 0)
        total += contract(query, normed_ref[...], 1, 0)
        parts.append(total.astype(BF))
    store_messages(parts, *out_refs)


def out_rows_kernel(scalar_ref, self_ref, cross_ref, one_ref, two_ref, *rest, height):
    out_refs, left_ref = rest[:-1], rest[-1]
    width, steps = self_ref.shape
    each = width // GROUP
    rows = width // height
    for n in range(rows):
        at = pl.multiple_of(scalar_ref[n] * height, height)
        is_self = at < width
        own = jnp.where(
            is_self,
            self_ref[pl.ds(pl.multiple_of(jnp.where(is_self, at, 0), height), height), :],
            cross_ref[pl.ds(pl.multiple_of(jnp.where(is_self, 0, at - width), height), height), :],
        )
        none = jnp.zeros_like(own)
        to = slice(n * height, (n + 1) * height)
        left_ref[to, :steps] = jnp.where(is_self, own, none)
        left_ref[to, steps:] = jnp.where(is_self, none, own)
    parts = []
    for n in range(GROUP):
        left = left_ref[n * each : (n + 1) * each, :]
        total = contract(left[:, :steps], one_ref[...], 1, 0)
        total += contract(left[:, steps:], two_ref[...], 1, 0)
        parts.append(total.astype(BF))
    store_messages(parts, *out_refs)


def fc_blocks(packs):
    rows = (packs[0].shape[0] - SMALL) // 2
    for n in range(0, len(packs), 2):
        pair = packs[n : n + 2]
        first = jnp.concatenate([pack[:rows, :] for pack in pair])
        second = jnp.concatenate([pack[rows : 2 * rows, :] for pack in pair])
        bias = jnp.concatenate([pack[2 * rows : 2 * rows + 1, :rows] for pack in pair], axis=1)
        yield slice(n * rows, (n + 2) * rows), first, second, bias.astype(F32)


def store_by_member(total, refs):
    rows = refs[0].shape[0]
    for n, ref in enumerate(refs):
        ref[...] = total[n * rows : (n + 1) * rows].astype(ref.dtype)


def fc_fwd_kernel(*refs):
    token_refs, packs = refs[:GROUP], refs[GROUP : -2 - GROUP]
    out_refs, (act_ref, slope_ref) = refs[-2 - GROUP : -2], refs[-2:]
    tokens = jnp.concatenate([ref[...] for ref in token_refs])
    total = jnp.zeros(tokens.shape, F32)
    for at, first, second, bias in fc_blocks(packs):
        inner = contract(tokens, first, 1, 1) + bias
        below = 0.5 * (1.0 + lax.erf(inner * 0.7071067811865476))
        density = jnp.exp(-0.5 * inner * inner) * 0.3989422804014327
        activation = (inner * below).astype(BF)
        act_ref[:, at] = activation
        slope_ref[:, at] = below + inner * density
        total += contract(activation, second, 1, 0)
    store_by_member(total, out_refs)


def fc_bwd_kernel(*refs):
    grad_refs, slope_ref, packs = refs[:GROUP], refs[GROUP], refs[GROUP + 1 : -2 - GROUP]
    out_refs, (inner_ref, bias_ref) = refs[-2 - GROUP : -2], refs[-2:]
    grads = jnp.concatenate([ref[...] for ref in grad_refs])
    total = jnp.zeros(grads.shape, F32)
    for at, first, second, _ in fc_blocks(packs):
        grad_inner = contract(grads, second, 1, 1) * slope_ref[:, at]
        bias_ref[0:1, at] = jnp.sum(grad_inner, axis=0, keepdims=True)
        grad_inner = grad_inner.astype(BF)
        inner_ref[:, at] = grad_inner
        total += contract(grad_inner, first, 1, 0)
    store_by_member(total, out_refs)


def fc_rows_kernel(place_ref, *refs):
    token_refs, grad_refs = refs[:GROUP], refs[GROUP : 2 * GROUP]
    act_ref, inner_ref, bias_ref = refs[2 * GROUP : 2 * GROUP + 3]
    outs = refs[2 * GROUP + 3 :]
    tokens = jnp.concatenate([ref[...] for ref in token_refs])
    grads = jnp.concatenate([ref[...] for ref in grad_refs])
    width = tokens.shape[1]
    rows = (outs[0].shape[1] - SMALL) // 2
    at = 0
    for out in outs:
        for r in range(0, out.shape[0], 2):
            both = slice(at, at + 2 * rows)
            first = contract(inner_ref[:, both], tokens, 0, 0).astype(BF)
            second = contract(act_ref[:, both], grads, 0, 0).astype(BF)
            for n in range(2):
                place = place_ref[r + n]
                part = slice(n * rows, (n + 1) * rows)
                out[place, :rows, :] = first[part]
                out[place, rows : 2 * rows, :] = second[part]
                bias = bias_ref[0:1, at + n * rows : at + (n + 1) * rows].astype(BF)
                bias = jnp.concatenate([bias, jnp.zeros((1, width - rows), BF)], axis=1)
                bias = jnp.concatenate([bias, jnp.zeros((SMALL - 1, width), BF)])
                out[place, 2 * rows :, :] = bias
            at += 2 * rows


SCALARS = pl.BlockSpec(memory_space=pltpu.SMEM)
WHOLE = pl.BlockSpec(memory_space=pltpu.VMEM)
PARAMS = pltpu.CompilerParams(vmem_limit_bytes=48 * 1024 * 1024)
HEADS_A_STEP = 8
UNIT = 32


def shape(dims, dtype):
    return jax.ShapeDtypeStruct(dims, dtype)


def self_fwd(length, mine, other, places, planes):
    steps = mine.shape[2]
    width = (mine.shape[1] - planes * SMALL) * 2 * GROUP // 3
    stats = [shape((width // HEAD_DIM, steps), F32)] * 2
    return pl.pallas_call(
        functools.partial(self_fwd_kernel, planes=planes),
        in_specs=[SCALARS] + [WHOLE] * 2,
        out_specs=[WHOLE] * 6,
        out_shape=[shape((3 * width, steps), BF), shape((width, steps), BF)]
        + stats
        + [shape((SMALL, width), F32), shape((2, width, steps), F32)],
        compiler_params=PARAMS,
        name="self_fwd",
    )(jnp.concatenate([length, places]), mine, other)


def plain_self_fwd(length, mine, other, places, planes, small):
    width, steps = small.shape[1], mine.shape[2]
    stats = [shape((width // HEAD_DIM, steps), F32)] * 2
    height = 3 * width // (2 * GROUP * planes)
    blocks = jnp.stack([mine, other])[:, :, : planes * height].reshape(-1, height, steps)
    qkv = jnp.zeros_like(blocks).at[places].set(blocks).reshape(3 * width, steps)
    bias = jnp.concatenate([small[0], jnp.zeros((width,), F32), small[1]])
    qkv = (qkv.astype(F32) + bias[:, None]).astype(BF)
    column = jnp.broadcast_to(small[3:5, :, None], (2, width, steps))
    results = pl.pallas_call(
        plain_self_fwd_kernel,
        in_specs=[SCALARS, WHOLE],
        out_specs=[WHOLE] * 3,
        out_shape=[shape((width, steps), BF)] + stats,
        compiler_params=PARAMS,
        name="self_fwd",
    )(length, qkv)
    return [qkv, *results, small, column]


def self_bwd(length, places, qkv, out, grad, peak, total, planes):
    width, steps = out.shape
    height = 3 * width // (2 * GROUP * planes)
    sums = shape((width, 2), F32)
    if height % 16 == 0:
        return pl.pallas_call(
            functools.partial(self_bwd_kernel, planes=planes),
            in_specs=[SCALARS] + [WHOLE] * 5,
            out_specs=[WHOLE] * 2,
            out_shape=[shape((GROUP, planes * height, steps), BF), sums],
            scratch_shapes=[pltpu.VMEM(qkv.shape, BF)],
            compiler_params=PARAMS,
            name="self_bwd",
        )(jnp.concatenate([length, places]), qkv, out, grad, peak, total)
    res, total = pl.pallas_call(
        plain_self_bwd_kernel,
        in_specs=[SCALARS] + [WHOLE] * 5,
        out_specs=[WHOLE] * 2,
        out_shape=[shape(qkv.shape, BF), sums],
        compiler_params=PARAMS,
        name="self_bwd",
    )(length, qkv, out, grad, peak, total)
    send = res.reshape(-1, height, steps)[places[: GROUP * planes]]
    return send.reshape(GROUP, planes * height, steps), total


def cross_specs(width, steps, span):
    count = width // HEAD_DIM // HEADS_A_STEP
    height = HEADS_A_STEP * HEAD_DIM
    by_step = pl.BlockSpec((height, steps), lambda i: (i, 0))
    keys = pl.BlockSpec((height, span), lambda i: (i, 0))
    values = pl.BlockSpec((height, span), lambda i: (i + count, 0))
    stats = pl.BlockSpec((1, HEADS_A_STEP, steps), lambda i: (i, 0, 0))
    column = pl.BlockSpec((height, 1), lambda i: (i, 0))
    return count, by_step, keys, values, stats, column


def cross_fwd(length, query, key_value):
    width, steps = query.shape
    count, by_step, keys, values, stats, _ = cross_specs(width, steps, key_value.shape[1])
    stat_shape = shape((count, HEADS_A_STEP, steps), F32)
    return pl.pallas_call(
        cross_fwd_kernel,
        grid=(count,),
        in_specs=[SCALARS, by_step, keys, values],
        out_specs=[by_step, stats, stats],
        out_shape=[shape((width, steps), BF), stat_shape, stat_shape],
        compiler_params=PARAMS,
        name="cross_fwd",
    )(length, query, key_value, key_value)


def cross_bwd(scalars, query, key_value, out, grad, peak, total, chips, height):
    width, steps = query.shape
    span = key_value.shape[1]
    outs = [shape((width, steps), BF), shape((2 * width, span), BF), shape((width, 1), F32)]
    if height:
        outs += [shape((chips, height, steps + span), BF)] * 2
    return pl.pallas_call(
        functools.partial(cross_bwd_kernel, height=height),
        in_specs=[SCALARS] + [WHOLE] * 6,
        out_specs=[WHOLE] * len(outs),
        out_shape=outs,
        compiler_params=PARAMS,
        name="cross_bwd",
    )(scalars, query, key_value, out, grad, peak, total)


def cross_rows(mine, came, normed, memory, other):
    chips, height, _ = mine.shape
    outs = message_shapes(chips // GROUP * height, memory.shape[1])
    return pl.pallas_call(
        cross_rows_kernel,
        in_specs=[WHOLE] * 5,
        out_specs=[WHOLE] * len(outs),
        out_shape=outs,
        compiler_params=PARAMS,
        name="cross_rows",
    )(mine, came, normed, memory, other)


def out_rows(scalars, self_out, cross_out, one, two, height):
    width, steps = self_out.shape
    outs = message_shapes(width // GROUP, width)
    return pl.pallas_call(
        functools.partial(out_rows_kernel, height=height),
        in_specs=[SCALARS] + [WHOLE] * 4,
        out_specs=[WHOLE] * len(outs),
        out_shape=outs,
        scratch_shapes=[pltpu.VMEM((width, 2 * steps), BF)],
        compiler_params=PARAMS,
        name="out_rows",
    )(scalars, self_out, cross_out, one, two)


def member_shapes(rows, width):
    return [shape((rows, width), F32)] + [shape((rows, width), BF)] * (GROUP - 1)


def fc_fwd(tokens, packs):
    rows, width = tokens[0].shape
    hidden = len(packs) * (packs[0].shape[0] - SMALL) // 2
    outs = member_shapes(rows, width)
    outs += [shape((GROUP * rows, hidden), BF), shape((GROUP * rows, hidden), F32)]
    return pl.pallas_call(
        fc_fwd_kernel,
        in_specs=[WHOLE] * (GROUP + len(packs)),
        out_specs=[WHOLE] * len(outs),
        out_shape=outs,
        compiler_params=PARAMS,
        name="fc_fwd",
    )(*tokens, *packs)


def fc_bwd(grads, packs, slope):
    rows, width = grads[0].shape
    hidden = slope.shape[1]
    outs = member_shapes(rows, width)
    outs += [shape((GROUP * rows, hidden), BF), shape((8, hidden), F32)]
    return pl.pallas_call(
        fc_bwd_kernel,
        in_specs=[WHOLE] * (GROUP + 1 + len(packs)),
        out_specs=[WHOLE] * len(outs),
        out_shape=outs,
        compiler_params=PARAMS,
        name="fc_bwd",
    )(*grads, slope, *packs)


def fc_rows(places, tokens, grads, activation, inner, bias, pack_shape):
    return pl.pallas_call(
        fc_rows_kernel,
        in_specs=[SCALARS] + [WHOLE] * (2 * GROUP + 3),
        out_specs=[WHOLE] * 2,
        out_shape=[shape(pack_shape, BF)] * 2,
        compiler_params=PARAMS,
        name="fc_rows",
    )(places, *tokens, *grads, activation, inner, bias)


def place_blocks(places, blocks, heights):
    width = blocks[0].shape[2]
    count = len(blocks) * GROUP
    starts = [sum(heights[:n]) for n in range(len(heights))]

    def kernel(place_ref, *refs):
        ins, outs = refs[: len(blocks)], refs[len(blocks) :]
        for block in range(count):
            place = place_ref[block]
            for n, (start, height) in enumerate(zip(starts, heights)):
                rows = ins[block // GROUP][block % GROUP, start : start + height, :]
                outs[n][place] = rows

    return pl.pallas_call(
        kernel,
        in_specs=[SCALARS] + [WHOLE] * len(blocks),
        out_specs=[WHOLE] * len(heights),
        out_shape=[shape((count, height, width), blocks[0].dtype) for height in heights],
        compiler_params=PARAMS,
        name="place_blocks",
    )(places, *blocks)


def local(mesh, dec_in, memory, cotangent, mem_lengths, dec_lengths, *weights):
    attn_in, cross_in, attn_out, fc_in, fc_out, biases, fc_bias, gains, shifts = weights
    chips, cores = mesh.shape["items"], mesh.shape["mem"]
    devices = chips * cores
    planes = chips // GROUP
    chip, core = lax.axis_index("items"), lax.axis_index("mem")
    plane, member = chip // GROUP, chip % GROUP

    by_plane = [list(range(k, chips, GROUP)) for k in range(GROUP)]

    def ring(a, step, name="plane"):
        pairs = [
            (i, (i // GROUP + step) % planes * GROUP + i % GROUP) for i in range(chips)
        ]
        with jax.named_scope(f"{name}_z{step}"):
            return lax.ppermute(a, "items", pairs)

    def across(a, mask, name="member"):
        with jax.named_scope(f"{name}_xy{mask}"):
            return lax.ppermute(a, "items", [(i, i ^ mask) for i in range(chips)])

    def swap(a, name="core"):
        with jax.named_scope(f"{name}_core"):
            return lax.ppermute(a, "mem", [(0, 1), (1, 0)])

    def by_core(mine, other):
        return jnp.where(core == 0, jnp.concatenate([mine, other]), jnp.concatenate([other, mine]))

    def ring_gather(a, name):
        held = [a]
        for _ in range(planes - 1):
            held.append(ring(held[-1], 1, name))
        return held

    def gather_rows(pack, heights):
        if planes != 4:
            whole = lax.all_gather(pack, ("items", "mem"), axis=0)
            starts = [sum(heights[:n]) for n in range(len(heights))]
            return [whole[:, s : s + h] for s, h in zip(starts, heights)]
        blocks, places = [], []
        for r, block in enumerate(ring_gather(pack, "rest")):
            first, second = (1, 2) if r < 2 else (2, 1)
            one = across(block, first, f"rest{r}")
            two = across(block, second, f"rest{r}")
            three = across(one, second, f"rest{r}far")
            near = jnp.stack([block, one, two, three])
            blocks += [near, swap(near, f"rest{r}")]
            source = (plane - r) % planes * GROUP
            for which in (core, 1 - core):
                places += [(source + (member ^ m)) * cores + which for m in (0, first, second, 3)]
        return place_blocks(jnp.stack(places).astype(jnp.int32), blocks, heights)

    def scatter_first(messages, name):
        _, first, second, _, _ = messages
        return across(first, 1, f"{name}_first"), across(second, 2, f"{name}_first")

    def scatter_second(messages, came, name):
        hold_first, hold_second = messages[3:]
        half = hold_first.shape[0]
        far_first = hold_first.astype(F32) + came[0][half:].astype(F32)
        far_second = hold_second.astype(F32) + came[1][half:].astype(F32)
        far_first = across(far_first.astype(BF), 2, f"{name}_second")
        return far_first, across(far_second.astype(BF), 1, f"{name}_second")

    def scatter_planes(messages, came, far):
        own = messages[0]
        half = own.shape[0] // 2
        height = own.shape[0] // planes
        sums = []
        for r in range(planes):
            which = 0 if 2 * r < planes else 1
            at = r * height % half
            rows = slice(at, at + height)
            near = own[r * height : (r + 1) * height].astype(F32)
            sums.append(near + came[which][rows].astype(F32) + far[which][rows].astype(F32))
        return sums

    def plane_sum(sums, name):
        total = sums[0]
        for r in range(1, planes):
            total = total + ring(sums[r].astype(BF), planes - r, name).astype(F32)
        return total

    def scatter_whole(part):
        return lax.psum_scatter(part, ("items", "mem"), scatter_dimension=0, tiled=True)

    def to_members(mine, name):
        return [mine] + [across(mine, mask, name) for mask in range(1, GROUP)]

    def from_members(parts, name):
        total = parts[0]
        for mask in range(1, GROUP):
            total = total + across(parts[mask], mask, name).astype(F32)
        return total

    def group_gather(mine, name):
        near = jnp.stack([mine] + [across(mine, mask, name) for mask in range(1, GROUP)])
        both = jnp.stack([near, swap(near, name)])
        return both.reshape(cores * GROUP * mine.shape[0], mine.shape[1])

    def group_sum(part, name):
        part = part.reshape(cores, GROUP, -1, part.shape[1])
        near = part[0] + swap(part[1].astype(BF), name).astype(F32)
        total = near[0]
        for mask in range(1, GROUP):
            total = total + across(near[mask].astype(BF), mask, name).astype(F32)
        return total

    width = dec_in.shape[2]
    steps = dec_in.shape[1]
    half = steps // cores
    span = memory.shape[1]
    row_attn, row_out, row_fc = attn_in.shape[0], attn_out.shape[0], fc_in.shape[0]
    small = jnp.concatenate([biases, gains, shifts])
    vectors, slice_width = small.shape

    regular = planes == 4 and row_attn % UNIT == 0 and row_out == HEAD_DIM and row_fc % 128 == 0

    def padded(a):
        return jnp.pad(a, ((0, SMALL - a.shape[0]), (0, width - a.shape[1])))

    def after(a, *others):
        return lax.optimization_barrier((a, *others))[0]

    tokens = dec_in[0]
    mem_rows = memory[0]
    came = [across(tokens, k, "tokens") for k in range(1, GROUP)]
    attn_held = [jnp.concatenate([attn_in, padded(small)])]
    for r in range(1, planes):
        held = attn_held[-1]
        if r == planes - 1:
            held = after(held, *came)
        attn_held.append(ring(held, 1, "attn"))
    group_tokens = jnp.concatenate([tokens] + came)
    w_attn = jnp.concatenate([a[:row_attn] for a in attn_held])
    projected = contract(w_attn, group_tokens, 1, 1).astype(BF)
    small_held = [a[row_attn:, :steps] for a in attn_held]
    sends = [
        jnp.concatenate([projected[:, k * steps : (k + 1) * steps]] + small_held)
        for k in range(GROUP)
    ]
    mine = jnp.stack([sends[0]] + [across(sends[k], k, "qkv") for k in range(1, GROUP)])
    other = swap(mine, "qkv")
    w_out = lax.all_gather(attn_out, ("items", "mem"), tiled=True)
    (w_cross,) = gather_rows(cross_in, [row_attn])
    w_cross = w_cross.reshape(-1, width)
    fc_held = ring_gather(jnp.concatenate([fc_in, fc_out, padded(fc_bias[None])]), "fc")
    if regular:
        fc_packs = fc_held + [swap(a, "fc") for a in fc_held]
    else:
        fc_held = jnp.stack(fc_held)
        w_fc_in = fc_held[:, :row_fc].reshape(-1, width)
        w_fc_out = fc_held[:, row_fc : 2 * row_fc].reshape(-1, width)
        fc_bias_held = fc_held[:, 2 * row_fc, :row_fc].reshape(-1).astype(F32)

    n = jnp.arange(cores * GROUP * planes)
    from_core, from_member = n // (GROUP * planes), n // planes % GROUP
    from_plane = (plane - n % planes) % planes
    places = (from_plane * GROUP + (member ^ from_member)) * cores + (core ^ from_core)
    places = places.astype(jnp.int32)

    if regular:
        fwd = self_fwd(dec_lengths, mine, other, places, planes)
    else:
        rows_small = lax.all_gather(small, ("items", "mem"), axis=1, tiled=True).astype(F32)
        fwd = plain_self_fwd(dec_lengths, mine, other, places, planes, rows_small)
    qkv, self_out, self_peak, self_total, rows_small, columns = fwd
    bias, gain, shift = (
        [rows_small[n : n + 1] for n in span] for span in (range(7), range(7, 10), range(10, 13))
    )
    hidden_one = tokens.astype(F32) + contract(self_out, w_out[:width], 0, 0) + bias[2]
    normal_one, spread_one = norm_parts(hidden_one)
    normed_one = normal_one * gain[0] + shift[0]
    normed_one_low = normed_one.astype(BF)
    cross_query = (contract(w_cross[:width], normed_one_low, 1, 1) + columns[0]).astype(BF)
    cross_kv = contract(w_cross[width:], mem_rows, 1, 1).astype(BF)
    mem_left = mem_lengths - core * span
    part_out, part_peak, part_total = cross_fwd(mem_left, cross_query, cross_kv)
    other_out = swap(part_out, "cross_out")
    other_stats = swap(jnp.stack([part_peak, part_total]), "stats")
    other_peak, other_total = other_stats[0], other_stats[1]
    cross_peak = jnp.maximum(part_peak, other_peak)
    mine_factor = jnp.exp(part_peak - cross_peak)
    other_factor = jnp.exp(other_peak - cross_peak)
    cross_total = mine_factor * part_total + other_factor * other_total
    heads = width // HEAD_DIM

    def per_head(stat):
        return stat.reshape(heads, 1, steps)

    cross_out = (
        per_head(mine_factor / cross_total) * part_out.reshape(heads, HEAD_DIM, steps).astype(F32)
        + per_head(other_factor / cross_total)
        * other_out.reshape(heads, HEAD_DIM, steps).astype(F32)
    )
    cross_plain = cross_out.reshape(width, steps)
    cross_out = (cross_plain + columns[1]).astype(BF)
    cross_plain = cross_plain.astype(BF)

    def own(rows):
        return lax.dynamic_slice_in_dim(rows, core * half, half)

    hidden_two = own(normed_one + contract(cross_out, w_out[width:], 0, 0)) + bias[5]
    normal_two, spread_two = norm_parts(hidden_two)
    normed_two = normal_two * gain[1] + shift[1]
    if regular:
        member_two = to_members(normed_two.astype(BF), "normed_two")
        *parts, activation, slope = fc_fwd(member_two, fc_packs)
        fc_result = from_members(parts, "three")
    else:
        group_two = group_gather(normed_two.astype(BF), "normed_two")
        inner = contract(group_two, w_fc_in, 1, 1) + fc_bias_held
        activation = jax.nn.gelu(inner, approximate=False).astype(BF)
        fc_result = group_sum(contract(activation, w_fc_out, 1, 0), "three")
    hidden_three = normed_two + fc_result + bias[6]
    normal_three, spread_three = norm_parts(hidden_three)
    out_own = (normal_three * gain[2] + shift[2]).astype(BF)
    output = by_core(out_own, swap(out_own, "output"))[None]
    mem_other = swap(after(mem_rows, out_own), "memory")

    grad_three, grad_gain_three, grad_shift_three = norm_back(
        own(cotangent[0]).astype(F32), normal_three, spread_three, gain[2]
    )
    if regular:
        member_three = to_members(grad_three.astype(BF), "grad_three")
        *parts, grad_inner, grad_fc_bias = fc_bwd(member_three, fc_packs, slope)
        grad_normed_two = grad_three + from_members(parts, "grad_two")
    else:
        group_three = group_gather(grad_three.astype(BF), "grad_three")
        grad_activation = contract(group_three, w_fc_out, 1, 1)
        density = jnp.exp(-0.5 * inner * inner) * 0.3989422804014327
        below = 0.5 * (1.0 + lax.erf(inner * 0.7071067811865476))
        grad_inner = grad_activation * (below + inner * density)
        grad_inner_low = grad_inner.astype(BF)
        grad_normed_two = grad_three + group_sum(
            contract(grad_inner_low, w_fc_in, 1, 0), "grad_two"
        )
        fc_part = jnp.concatenate(
            [
                contract(grad_inner_low, group_two, 0, 0).reshape(planes, row_fc, width),
                contract(activation, group_three, 0, 0).reshape(planes, row_fc, width),
                jnp.pad(
                    jnp.sum(grad_inner, axis=0).reshape(planes, 1, row_fc),
                    ((0, 0), (0, SMALL - 1), (0, width - row_fc)),
                ),
            ],
            axis=1,
        )
        fc_part = jnp.concatenate(
            [
                lax.dynamic_slice_in_dim(fc_part, (plane - at) % planes, 1)
                for at in range(planes)
            ]
        ).astype(BF)
    grad_two, grad_gain_two, grad_shift_two = norm_back(
        grad_normed_two, normal_two, spread_two, gain[1]
    )

    grad_two_low = grad_two.astype(BF)
    grad_two_all = by_core(grad_two_low, swap(grad_two_low, "grad_two"))
    grad_cross = contract(w_out[width:], grad_two_all, 1, 1).astype(BF)
    if regular:
        plane_places = ((plane - jnp.arange(planes)) % planes).astype(jnp.int32)
        fc_mine, fc_other = fc_rows(
            plane_places,
            member_two,
            member_three,
            activation,
            after(grad_inner, grad_cross),
            grad_fc_bias,
            (planes, *fc_held[0].shape),
        )
        fc_part = (fc_mine.astype(F32) + swap(fc_other, "fc_grad").astype(F32)).astype(BF)
    fc_sum = lax.psum_scatter(
        fc_part, "items", scatter_dimension=0, axis_index_groups=by_plane
    ).astype(F32)
    sum_fc_in, sum_fc_out = fc_sum[:row_fc], fc_sum[row_fc : 2 * row_fc]
    sum_fc_bias = fc_sum[2 * row_fc, :row_fc]
    chip_at = jnp.arange(chips)
    far = ((chip_at % GROUP) ^ member) * planes + (plane - chip_at // GROUP) % planes
    scalars = jnp.concatenate([mem_left, core.reshape(1), far]).astype(jnp.int32)
    grad_query, grad_kv, grad_value_sum, *blocks = cross_bwd(
        scalars,
        cross_query,
        cross_kv,
        cross_plain,
        grad_cross,
        cross_peak.reshape(heads, steps),
        cross_total.reshape(heads, steps),
        chips,
        row_attn if regular else 0,
    )
    if regular:
        came_blocks = swap(blocks[1], "cross_blocks")
        cross_parts = cross_rows(blocks[0], came_blocks, normed_one_low, mem_rows, mem_other)
    grad_query_all = grad_query.astype(F32) + swap(grad_query, "grad_query").astype(F32)
    grad_query_low = after(grad_query_all.astype(BF), fc_part)
    grad_one, grad_gain_one, grad_shift_one = norm_back(
        grad_two + own(contract(grad_query_low, w_cross[:width], 0, 0)),
        own(normal_one),
        own(spread_one),
        gain[0],
    )
    grad_one_low = grad_one.astype(BF)
    grad_one_all = by_core(grad_one_low, swap(grad_one_low, "grad_one"))
    if regular:
        grad_one_all = after(grad_one_all, cross_parts[0])
    grad_self = contract(w_out[:width], grad_one_all, 1, 1).astype(BF)
    grad_sends, grad_qv_sum = self_bwd(
        dec_lengths, places, qkv, self_out, grad_self, self_peak, self_total, planes
    )


    def of_core(a, which):
        return lax.dynamic_index_in_dim(a, which, 1, keepdims=False)

    if regular:
        came_cross = scatter_first(cross_parts, "cross_grad")
        far_cross = scatter_second(cross_parts, came_cross, "cross_grad")
        cross_sums = scatter_planes(cross_parts, came_cross, far_cross)
        out_places = places[: GROUP * planes]
        out_parts = out_rows(
            out_places, self_out, cross_out, grad_one_all, grad_two_all, row_out
        )
        out_parts = lax.optimization_barrier((*out_parts, *came_cross))[: len(out_parts)]
        came_out = scatter_first(out_parts, "out_grad")
        far_out = scatter_second(out_parts, came_out, "out_grad")
        out_sums = scatter_planes(out_parts, came_out, far_out)
        sum_out = plane_sum(out_sums, "out_grad")
    else:
        sum_cross = scatter_whole(
            jnp.concatenate(
                [contract(grad_query, normed_one_low, 1, 0), contract(grad_kv, mem_rows, 1, 0)]
            )
        )
        part_out = [
            contract(self_out, grad_one_all, 1, 0),
            contract(cross_out, grad_two_all, 1, 0),
        ]
        sum_out = scatter_whole(jnp.concatenate(part_out) / cores)

    grad_held = jnp.concatenate(
        [grad_sends[0]] + [across(grad_sends[k], k, "grad_qkv") for k in range(1, GROUP)], axis=1
    )
    part_attn = contract(grad_held, group_tokens, 1, 0)
    grad_memory = contract(after(grad_kv, part_attn), w_cross[width:], 0, 0).astype(BF)[None]
    if regular:
        part_attn = after(part_attn, *far_cross)
    sum_attn = part_attn[:row_attn]
    for r in range(1, planes):
        rows = slice(r * row_attn, (r + 1) * row_attn)
        sum_attn = sum_attn + ring(part_attn[rows].astype(BF), planes - r, "attn_grad").astype(F32)
    if regular:
        cross_sums = lax.optimization_barrier((*cross_sums, sum_attn))[:planes]
        sum_cross = plane_sum(cross_sums, "cross_grad")
    part_tokens = contract(grad_held, w_attn, 0, 0).reshape(GROUP, cores, half, width)
    part_tokens = jnp.stack([of_core(part_tokens, core), of_core(part_tokens, 1 - core)])
    part_tokens = part_tokens[0] + swap(part_tokens[1].astype(BF), "grad_dec").astype(F32)
    came = across(jnp.concatenate([part_tokens[1], part_tokens[3]]).astype(BF), 1, "grad_dec")
    far = across((part_tokens[2] + came[half:].astype(F32)).astype(BF), 2, "grad_dec")
    grad_tokens = grad_one + part_tokens[0] + came[:half].astype(F32) + far.astype(F32)
    grad_tokens_low = grad_tokens.astype(BF)
    grad_dec_in = by_core(grad_tokens_low, swap(grad_tokens_low, "grad_dec"))[None]

    part_vectors = jnp.stack(
        [
            grad_qv_sum[:, 0] / cores,
            grad_qv_sum[:, 1] / cores,
            jnp.sum(grad_one, axis=0),
            jnp.sum(grad_query.astype(F32), axis=1),
            grad_value_sum[:, 0],
            jnp.sum(grad_two, axis=0),
            jnp.sum(grad_three, axis=0),
            grad_gain_one,
            grad_gain_two,
            grad_gain_three,
            grad_shift_one,
            grad_shift_two,
            grad_shift_three,
        ]
    )
    part_vectors = jnp.transpose(part_vectors.reshape(vectors, devices, slice_width), (1, 0, 2))
    late = far_out if regular else (part_attn,)
    came = lax.all_to_all(
        after(part_vectors.reshape(devices, vectors * slice_width), *late),
        ("items", "mem"),
        split_axis=0,
        concat_axis=0,
        tiled=True,
    )
    sum_vectors = jnp.sum(came, axis=0).reshape(vectors, slice_width)
    return (
        output,
        grad_dec_in,
        grad_memory,
        sum_attn,
        sum_cross,
        sum_out,
        sum_fc_in,
        sum_fc_out,
        sum_vectors[:7],
        sum_fc_bias,
        sum_vectors[7:10],
        sum_vectors[10:vectors],
    )


def solution(mesh):
    rows = P(("items", "mem"), None)
    columns = P(None, ("items", "mem"))
    item = P("items", None, None)
    in_specs = (
        item,
        P("items", "mem", None),
        item,
        P("items"),
        P("items"),
        rows,
        rows,
        rows,
        rows,
        rows,
        columns,
        P(("items", "mem")),
        columns,
        columns,
    )
    out_specs = (
        item,
        item,
        P("items", "mem", None),
        rows,
        rows,
        rows,
        rows,
        rows,
        columns,
        P(("items", "mem")),
        columns,
        columns,
    )

    def program(*args):
        return local(mesh, *args)

    return jax.shard_map(
        program, mesh=mesh, in_specs=in_specs, out_specs=out_specs, check_vma=False
    )
```
